128 devices in a mesh: ctx: 8 (over y_lo, z), head: 16 (over x, y_hi, core).
Axes of the slice: x: 4, y: 4 (y_hi: 2, y_lo: 2; y = y_hi * 2 + y_lo), z: 4, core: 2. Of those that a mesh axis runs over, the one named last changes fastest.
Arguments:
- residual: bfloat16 [8192, 8192], P(('ctx', 'head')), may hold values from -6 to 6
- q_win: bfloat16 [8192, 16, 256], P('ctx', 'head'), may hold values from -10 to 10
- kv_win: bfloat16 [8192, 16, 2, 256], P('ctx', 'head'), may hold values from -28 to 28
- lam_win: float32 [4, 128], replicated, may hold values from -1.2 to 1.2
- gn_gain: float32 [256], replicated, may hold values from 0.1 to 1.9
- w_out_a: bfloat16 [4096, 8192], P('head'), may hold values from -0.09375 to 0.09375
- norm_gain: float32 [8192], replicated, may hold values from 0.1 to 1.9
- w_qkv: bfloat16 [8192, 16, 3, 256], P(None, 'head'), may hold values from -4 to 4, as said below
Outputs:
- hidden: bfloat16 [8192, 8192], P(('ctx', 'head'))
- part_out: float32 [2, 8192, 16, 256], P(None, 'ctx', 'head')
- log_sums: float32 [2, 16, 8192], P(None, 'head', 'ctx')
The draws below stay inside these ranges and needn't reach their ends.
Inputs may be any that keep to these rules, and one draw needn't show every extreme that they name: `w_qkv`: projection weights of the next layer.
All inputs are finite; a program needn't handle non-finite values.
Results may differ from the reference program's by a relative error of at most 0.04.
Values may be sent and summed in bfloat16 or wider, within the bound.
A program may use at most 192 MiB of HBM per device.

```python
import math
from functools import reduce
import jax
import jax.numpy as jnp
from jax import lax

D = 8192
HEADS = 16
HDIM = 128
WINDOW = 4096
TOK_DEV = 1024
TOKENS = 8192
N_HEAD = 16


def window_pair(key):
    key_query = jax.random.fold_in(key, 101)
    key_keys = jax.random.fold_in(key, 102)
    key_values = jax.random.fold_in(key, 103)
    shape_sub = (TOKENS, HEADS, 2, HDIM)
    queries = jnp.clip(1.7 * jax.random.normal(key_query, shape_sub, jnp.float32), -10.0, 10.0)
    keys_drawn = jnp.clip(1.7 * jax.random.normal(key_keys, shape_sub, jnp.float32), -10.0, 10.0)
    values_drawn = jnp.clip(jax.random.normal(key_values, (TOKENS, HEADS, 2 * HDIM), jnp.float32), -6.0, 6.0)
    stacked = jnp.stack([keys_drawn.reshape(TOKENS, HEADS, 2 * HDIM), values_drawn], axis=2)
    return (queries.reshape(TOKENS, HEADS, 2 * HDIM), stacked)


def draw_q_win(key, part):
    return window_pair(key)[0].astype(jnp.bfloat16)


def draw_kv_win(key, part):
    return window_pair(key)[1].astype(jnp.bfloat16)


def draw_w_qkv(key, part):
    key_query = jax.random.fold_in(key, 201)
    key_keys = jax.random.fold_in(key, 202)
    key_values = jax.random.fold_in(key, 203)
    shape_sub = (D, HEADS, 2, HDIM)
    spread = D ** (-0.5)
    query_part = jnp.clip(1.7 * jax.random.normal(key_query, shape_sub, jnp.float32), -10.0, 10.0) * spread
    key_part = jnp.clip(1.7 * jax.random.normal(key_keys, shape_sub, jnp.float32), -10.0, 10.0) * spread
    value_part = jnp.clip(jax.random.normal(key_values, (D, HEADS, 2 * HDIM), jnp.float32), -6.0, 6.0) * spread
    stacked = jnp.stack([query_part.reshape(D, HEADS, 2 * HDIM), key_part.reshape(D, HEADS, 2 * HDIM), value_part], axis=2)
    return stacked.astype(jnp.bfloat16)


def block_levels(rng, extent, shards, least, largest):
    gain = 1.0
    for axis_at, parts in shards:
        steps = jax.random.uniform(jax.random.fold_in(jax.random.fold_in(rng, 6), axis_at), (parts,), jnp.float32, least / len(shards), largest / len(shards))
        gain = gain * jnp.repeat(jnp.exp(steps), extent[axis_at] // parts).reshape((-1,) + (1,) * (len(extent) - 1 - axis_at))
    return gain


def centred(rng, shape, deviation, limit, split=(), kind=jnp.bfloat16):
    values = jax.random.normal(rng, shape, jnp.float32) * deviation
    if len(split) > 0:
        values = block_levels(rng, shape, split, -0.22, 0.18) * values
    return jnp.clip(values, min=-limit, max=limit).astype(kind)


def setup_inputs(seed: int = 0) -> dict:
    arg_keys = jax.random.split(jax.random.key(seed), 9)
    return {
        "residual": centred(arg_keys[0], (TOKENS, D), 1.0, 6.0, ((0, 128),)),
        "q_win": draw_q_win(jax.random.fold_in(arg_keys[8], 71), 0),
        "kv_win": draw_kv_win(jax.random.fold_in(arg_keys[8], 71), 0),
        "lam_win": centred(arg_keys[3], (4, HDIM), 0.2, 1.2, (), jnp.float32),
        "gn_gain": jnp.clip(1.0 + 0.18 * jax.random.normal(arg_keys[4], (2 * HDIM,), jnp.float32), 0.1, 1.9),
        "w_out_a": centred(arg_keys[5], (HEADS * 2 * HDIM, D), (HEADS * 2 * HDIM) ** -0.5, 0.09375, ((0, 16),)),
        "norm_gain": jnp.clip(1.0 + 0.18 * jax.random.normal(arg_keys[6], (D,), jnp.float32), 0.1, 1.9),
        "w_qkv": draw_w_qkv(jax.random.fold_in(arg_keys[8], 71), 0),
    }


EPSILON = 1e-05
LAMBDA_INIT = 0.8 - 0.6 * math.exp(-3.3)

def window_block(queries, key_rows, value_rows, row_first, key_first, lambda_full, group_gain):
    key_pos = key_first + jnp.arange(key_rows.shape[0], dtype=jnp.int32)
    row_pos = row_first + jnp.arange(queries.shape[0], dtype=jnp.int32)
    scores = jnp.einsum('qhjd,khjd->hjqk', queries.astype(jnp.float32), key_rows.astype(jnp.float32)) / math.sqrt(HDIM)
    allowed = (key_pos[None, :] <= row_pos[:, None]) & (key_pos[None, :] > row_pos[:, None] - WINDOW) & (key_pos[None, :] >= 0)
    scores = jnp.where(allowed, scores, -jnp.inf)
    highest = lax.optimization_barrier(jnp.max(scores, axis=-1, keepdims=True))
    shifted = jnp.exp(scores - highest)
    probs = shifted / lax.optimization_barrier(jnp.sum(shifted, axis=-1, keepdims=True))
    combined = (probs[:, 0] - lambda_full * probs[:, 1]).astype(jnp.bfloat16)
    attended = jnp.einsum('hqk,khe->qhe', combined.astype(jnp.float32), value_rows.astype(jnp.float32))
    factor = lax.rsqrt(lax.optimization_barrier(jnp.mean(attended * attended, axis=-1, keepdims=True)) + EPSILON)
    normed = attended * factor * group_gain * (1.0 - LAMBDA_INIT)
    return normed.astype(jnp.bfloat16).reshape(queries.shape[0], -1)

def window_layer(q_win, kv_win, lam_win, gn_gain):
    lambda_full = jnp.exp(jnp.sum(lam_win[0] * lam_win[1])) - jnp.exp(jnp.sum(lam_win[2] * lam_win[3])) + LAMBDA_INIT
    queries = q_win.reshape(TOKENS, HEADS, 2, HDIM)
    key_rows = kv_win[:, :, 0].reshape(TOKENS, HEADS, 2, HDIM)
    value_rows = kv_win[:, :, 1]
    key_pad = jnp.concatenate([jnp.zeros((WINDOW, HEADS, 2, HDIM), key_rows.dtype), key_rows], axis=0)
    value_pad = jnp.concatenate([jnp.zeros((WINDOW, HEADS, 2 * HDIM), value_rows.dtype), value_rows], axis=0)
    rows_block = min(512, TOK_DEV)

    def one_block(number):
        row_start = number * rows_block
        picked = lax.dynamic_slice_in_dim(queries, row_start, rows_block, 0)
        key_slab = lax.dynamic_slice_in_dim(key_pad, row_start, WINDOW + rows_block, 0)
        value_slab = lax.dynamic_slice_in_dim(value_pad, row_start, WINDOW + rows_block, 0)
        return window_block(picked, key_slab, value_slab, row_start, row_start - WINDOW, lambda_full, gn_gain)
    pieces = lax.map(one_block, jnp.arange(TOKENS // rows_block, dtype=jnp.int32))
    return pieces.reshape(TOKENS, HEADS * 2 * HDIM)

def project_out(normed, w_out_a):
    group_cols = HEADS * 2 * HDIM // N_HEAD

    def add_group(number, totals):
        offset = jnp.asarray(number, jnp.int32) * group_cols
        columns = lax.dynamic_slice_in_dim(normed, offset, group_cols, 1)
        weights = lax.dynamic_slice_in_dim(w_out_a, offset, group_cols, 0)
        partial_value = jnp.dot(columns, weights, preferred_element_type=jnp.float32).astype(jnp.bfloat16)
        partial_value = lax.optimization_barrier(partial_value)
        return totals + partial_value.astype(jnp.float32)
    return lax.fori_loop(0, N_HEAD, add_group, jnp.zeros((TOKENS, D), jnp.float32))

def rms_rows(values_in, gain_row):
    widened = values_in.astype(jnp.float32)
    factor = lax.rsqrt(lax.optimization_barrier(jnp.mean(widened * widened, axis=-1, keepdims=True)) + EPSILON)
    return (widened * factor * gain_row).astype(jnp.bfloat16)

def cycle_stats(queries, key_rows, value_rows, row_pos, key_pos, present):
    scores = jnp.einsum('qhjd,khjd->hjqk', queries.astype(jnp.float32), key_rows.astype(jnp.float32)) / math.sqrt(HDIM)
    allowed = jnp.broadcast_to(present & (key_pos[None, :] <= row_pos[:, None]), scores.shape)
    any_seen = jnp.any(allowed, axis=-1)
    highest = jnp.where(any_seen, lax.optimization_barrier(jnp.max(jnp.where(allowed, scores, -jnp.inf), axis=-1)), 0.0)
    weights = jnp.where(allowed, jnp.exp(scores - highest[..., None]), 0.0)
    totals = lax.optimization_barrier(jnp.sum(weights, axis=-1))
    rounded = lax.optimization_barrier(weights.astype(jnp.bfloat16))
    summed = jnp.einsum('hjqk,khe->hjqe', rounded.astype(jnp.float32), value_rows.astype(jnp.float32))
    return (highest, any_seen, totals, summed)

def cycle_finish(collected):
    marked = [jnp.where(member[1], member[0], -jnp.inf) for member in collected]
    overall = reduce(jnp.maximum, marked)
    weight_sum = reduce(jnp.add, [jnp.where(member[1], member[2] * jnp.exp(member[0] - overall), 0.0) for member in collected])
    log_total = overall + jnp.log(weight_sum)
    result = reduce(jnp.add, [jnp.where(member[1][..., None], jnp.exp(member[0] - log_total)[..., None] * member[3], 0.0) for member in collected])
    return (result, log_total)

def cycle_layer(qkv):
    rows_block = min(512, TOK_DEV)

    def one_block(number):
        row_start = number * rows_block
        queries = lax.dynamic_slice_in_dim(qkv, row_start, rows_block, 0)[:, :, 0].reshape(rows_block, HEADS, 2, HDIM)
        row_pos = row_start + jnp.arange(rows_block, dtype=jnp.int32)
        own_block = row_start // TOK_DEV
        collected = []
        for behind in range(3):
            block_id = own_block - behind
            key_start = jnp.maximum(block_id, 0) * TOK_DEV
            kv_rows = lax.dynamic_slice_in_dim(qkv, key_start, TOK_DEV, 0)
            key_pos = block_id * TOK_DEV + jnp.arange(TOK_DEV, dtype=jnp.int32)
            collected.append(cycle_stats(queries, kv_rows[:, :, 1].reshape(TOK_DEV, HEADS, 2, HDIM), kv_rows[:, :, 2], row_pos, key_pos, block_id >= 0))
        return cycle_finish(collected)
    outputs, log_parts = lax.map(one_block, jnp.arange(TOKENS // rows_block, dtype=jnp.int32))
    part_out = outputs.transpose(2, 0, 3, 1, 4).reshape(2, TOKENS, HEADS, 2 * HDIM)
    log_out = log_parts.transpose(2, 1, 0, 3).reshape(2, HEADS, TOKENS)
    return (part_out, log_out)

def reference(residual, q_win, kv_win, lam_win, gn_gain, w_out_a, norm_gain, w_qkv):
    normed = window_layer(q_win, kv_win, lam_win, gn_gain)
    totals = project_out(normed, w_out_a)
    hidden = (residual.astype(jnp.float32) + totals).astype(jnp.bfloat16)
    normal_rows = rms_rows(hidden, norm_gain)
    qkv = jnp.dot(normal_rows, w_qkv.reshape(D, -1), preferred_element_type=jnp.float32).astype(jnp.bfloat16)
    qkv = qkv.reshape(TOKENS, HEADS, 3, 2 * HDIM)
    part_out, log_out = cycle_layer(qkv)
    return (hidden, part_out, log_out)
```

```python
import functools
import math

import jax
import jax.numpy as jnp
from jax import lax
from jax.experimental import pallas as pl
from jax.experimental.pallas import tpu as pltpu
from jax.sharding import PartitionSpec as P

HDIM = 128
WINDOW = 4096
EPSILON = 1e-05
LAMBDA_INIT = 0.8 - 0.6 * math.exp(-3.3)
SCALE = math.log2(math.e) / math.sqrt(HDIM)
LN2 = math.log(2.0)
NEG = -1e30
ONES = 16
ROWS = 256


def passed_along(block, axis, distance):
    devices = range(lax.axis_size(axis))
    route = [(i - distance, i) for i in devices if i - distance in devices]
    return lax.ppermute(block, axis, route)


def with_ones(values):
    flipped = values.astype(jnp.float32).T.astype(jnp.bfloat16)
    return jnp.concatenate([flipped, jnp.ones((ONES, values.shape[0]), jnp.bfloat16)], axis=0)


def scaled_queries(picked):
    return (picked.astype(jnp.float32) * SCALE).astype(jnp.bfloat16)


def online_step(queries, keys, values_up, m_ref, acc_ref, mask):
    for j in range(2):
        scores = lax.dot_general(
            keys[:, j * HDIM : (j + 1) * HDIM],
            queries[:, j * HDIM : (j + 1) * HDIM],
            (((1,), (1,)), ((), ())),
            preferred_element_type=jnp.float32,
        )
        if mask is not None:
            scores = jnp.where(mask, scores, NEG)
        before = m_ref[j]
        after = jnp.maximum(before, jnp.max(scores, axis=0, keepdims=True))
        weights = jnp.exp2(scores - after).astype(jnp.bfloat16)
        acc_ref[j] = acc_ref[j] * jnp.exp2(before - after) + jnp.dot(
            values_up, weights, preferred_element_type=jnp.float32
        )
        m_ref[j] = after


def window_kernel(lam_ref, q_ref, gain_ref, *refs):
    kv_refs, (out_ref, vt_ref, m_ref, acc_ref) = refs[:5], refs[5:]
    number = pl.program_id(0)
    ctx = lax.axis_index("ctx")

    @pl.when(number == 0)
    def _():
        for n in range(5):
            vt_ref[n] = with_ones(kv_refs[n][:, 256:])

    queries = scaled_queries(q_ref[...])
    m_ref[...] = jnp.full_like(m_ref, NEG)
    acc_ref[...] = jnp.zeros_like(acc_ref)
    tokens = kv_refs[0].shape[0]
    key_pos = lax.broadcasted_iota(jnp.int32, (tokens, ROWS), 0)
    row_pos = lax.broadcasted_iota(jnp.int32, (tokens, ROWS), 1) + number * ROWS
    online_step(queries, kv_refs[0], vt_ref[0], m_ref, acc_ref, key_pos <= row_pos)
    for n in range(1, 5):

        @pl.when(ctx >= n)
        def _():
            online_step(
                queries, kv_refs[n], vt_ref[n], m_ref, acc_ref, key_pos > row_pos if n == 4 else None
            )

    one = acc_ref[0, :256] / acc_ref[0, 256:257]
    two = acc_ref[1, :256] / acc_ref[1, 256:257]
    attended = one - lam_ref[0] * two
    factor = lax.rsqrt(jnp.mean(attended * attended, axis=0, keepdims=True) + EPSILON)
    normed = (attended * factor).T * (gain_ref[...] * (1.0 - LAMBDA_INIT))
    out_ref[...] = normed.astype(jnp.bfloat16)


def window_attention(queries, blocks, lam, gain):
    tokens = queries.shape[0]
    whole = pl.BlockSpec((tokens, 512), lambda i: (0, 0))
    return pl.pallas_call(
        window_kernel,
        name="window",
        grid=(tokens // ROWS,),
        out_shape=jax.ShapeDtypeStruct((tokens, 256), jnp.bfloat16),
        in_specs=[
            pl.BlockSpec(memory_space=pltpu.SMEM),
            pl.BlockSpec((ROWS, 256), lambda i: (i, 0)),
            pl.BlockSpec((1, 256), lambda i: (0, 0)),
        ]
        + [whole] * 5,
        out_specs=pl.BlockSpec((ROWS, 256), lambda i: (i, 0)),
        scratch_shapes=[
            pltpu.VMEM((5, 256 + ONES, tokens), jnp.bfloat16),
            pltpu.VMEM((2, 1, ROWS), jnp.float32),
            pltpu.VMEM((2, 256 + ONES, ROWS), jnp.float32),
        ],
        compiler_params=pltpu.CompilerParams(vmem_limit_bytes=48 * 2**20),
    )(lam.reshape(1), queries, gain.reshape(1, 256), *blocks)


def cycle_kernel(q_ref, kv0_ref, kv1_ref, kv2_ref, out_ref, log_ref, vt_ref, m_ref, acc_ref):
    number = pl.program_id(0)
    ctx = lax.axis_index("ctx")
    kv_refs = (kv0_ref, kv1_ref, kv2_ref)

    @pl.when(number == 0)
    def _():
        for n in range(3):
            vt_ref[n] = with_ones(kv_refs[n][:, 256:])

    queries = scaled_queries(q_ref[...])
    m_ref[...] = jnp.full_like(m_ref, NEG)
    acc_ref[...] = jnp.zeros_like(acc_ref)
    tokens = kv0_ref.shape[0]
    key_pos = lax.broadcasted_iota(jnp.int32, (tokens, ROWS), 0)
    row_pos = lax.broadcasted_iota(jnp.int32, (tokens, ROWS), 1) + number * ROWS
    online_step(queries, kv0_ref, vt_ref[0], m_ref, acc_ref, key_pos <= row_pos)
    for n in (1, 2):

        @pl.when(ctx >= n)
        def _():
            online_step(queries, kv_refs[n], vt_ref[n], m_ref, acc_ref, None)

    for j in range(2):
        total = acc_ref[j, 256:257]
        out_ref[j] = (acc_ref[j, :256] / total).T
        log_ref[j : j + 1, :] = (m_ref[j] + jnp.log2(total)) * LN2


def cycle_attention(queries, blocks):
    tokens = queries.shape[0]
    whole = pl.BlockSpec((tokens, 512), lambda i: (0, 0))
    return pl.pallas_call(
        cycle_kernel,
        name="cycle",
        grid=(tokens // ROWS,),
        out_shape=(
            jax.ShapeDtypeStruct((2, tokens, 256), jnp.float32),
            jax.ShapeDtypeStruct((2, tokens), jnp.float32),
        ),
        in_specs=[pl.BlockSpec((ROWS, 256), lambda i: (i, 0))] + [whole] * 3,
        out_specs=(
            pl.BlockSpec((2, ROWS, 256), lambda i: (0, i, 0)),
            pl.BlockSpec((2, ROWS), lambda i: (0, i)),
        ),
        scratch_shapes=[
            pltpu.VMEM((3, 256 + ONES, tokens), jnp.bfloat16),
            pltpu.VMEM((2, 1, ROWS), jnp.float32),
            pltpu.VMEM((2, 256 + ONES, ROWS), jnp.float32),
        ],
        compiler_params=pltpu.CompilerParams(vmem_limit_bytes=48 * 2**20),
    )(queries, *blocks)


def rms_rows(values_in, gain_row):
    widened = values_in.astype(jnp.float32)
    factor = lax.rsqrt(jnp.mean(widened * widened, axis=-1, keepdims=True) + EPSILON)
    return (widened * factor * gain_row).astype(jnp.bfloat16)


def on_device(residual, q_win, kv_win, lam_win, gn_gain, w_out_a, norm_gain, w_qkv):
    tokens_here = q_win.shape[0]
    lambda_full = (
        jnp.exp(jnp.sum(lam_win[0] * lam_win[1]))
        - jnp.exp(jnp.sum(lam_win[2] * lam_win[3]))
        + LAMBDA_INIT
    )
    kv_here = kv_win.reshape(tokens_here, 512)
    blocks = [kv_here] + [passed_along(kv_here, "ctx", behind) for behind in (1, 2, 3, 4)]
    normed = window_attention(q_win.reshape(tokens_here, 256), blocks, lambda_full, gn_gain)
    w_flat = w_qkv.reshape(w_qkv.shape[0], -1)
    summed_out = lax.psum_scatter(
        jnp.dot(normed, w_out_a, preferred_element_type=jnp.float32).astype(jnp.bfloat16),
        "head",
        scatter_dimension=0,
        tiled=True,
    ).astype(jnp.float32)
    h_rows = (residual.astype(jnp.float32) + summed_out).astype(jnp.bfloat16)
    normal_rows = rms_rows(h_rows, norm_gain)
    qkv = jnp.dot(
        lax.all_gather(normal_rows, "head", axis=0, tiled=True),
        w_flat,
        preferred_element_type=jnp.float32,
    ).astype(jnp.bfloat16)
    kv_next = qkv[:, 256:]
    next_blocks = [kv_next] + [passed_along(kv_next, "ctx", behind) for behind in (1, 2)]
    part_out, log_out = cycle_attention(qkv[:, :256], next_blocks)
    return (
        h_rows,
        part_out.reshape(2, tokens_here, 1, 256),
        log_out.reshape(2, 1, tokens_here),
    )


def solution(mesh):
    in_specs = (
        P(("ctx", "head"), None),
        P("ctx", "head", None),
        P("ctx", "head", None, None),
        P(),
        P(),
        P("head", None),
        P(),
        P(None, "head", None, None),
    )
    out_specs = (P(("ctx", "head"), None), P(None, "ctx", "head", None), P(None, "head", "ctx"))
    return jax.shard_map(
        on_device, mesh=mesh, in_specs=in_specs, out_specs=out_specs, check_vma=False
    )
```

```python
import functools
import math

import jax
import jax.numpy as jnp
from jax import lax
from jax.experimental import pallas as pl
from jax.experimental.pallas import tpu as pltpu
from jax.sharding import PartitionSpec as P

HDIM = 128
WINDOW = 4096
EPSILON = 1e-05
LAMBDA_INIT = 0.8 - 0.6 * math.exp(-3.3)
SCALE = math.log2(math.e) / math.sqrt(HDIM)
LN2 = math.log(2.0)
NEG = -1e30
ONES = 16
ROWS = 256


def passed_along(block, axis, distance):
    devices = range(lax.axis_size(axis))
    route = [(i - distance, i) for i in devices if i - distance in devices]
    return lax.ppermute(block, axis, route)


def with_ones(values):
    flipped = values.astype(jnp.float32).T.astype(jnp.bfloat16)
    return jnp.concatenate([flipped, jnp.ones((ONES, values.shape[0]), jnp.bfloat16)], axis=0)


def scaled_queries(picked):
    return (picked.astype(jnp.float32) * SCALE).astype(jnp.bfloat16)


def online_step(queries, keys, values_up, m_ref, acc_ref, mask):
    for j in range(2):
        scores = lax.dot_general(
            keys[:, j * HDIM : (j + 1) * HDIM],
            queries[:, j * HDIM : (j + 1) * HDIM],
            (((1,), (1,)), ((), ())),
            preferred_element_type=jnp.float32,
        )
        if mask is not None:
            scores = jnp.where(mask, scores, NEG)
        before = m_ref[j]
        after = jnp.maximum(before, jnp.max(scores, axis=0, keepdims=True))
        weights = jnp.exp2(scores - after).astype(jnp.bfloat16)
        acc_ref[j] = acc_ref[j] * jnp.exp2(before - after) + jnp.dot(
            values_up, weights, preferred_element_type=jnp.float32
        )
        m_ref[j] = after


def window_kernel(lam_ref, q_ref, gain_ref, *refs):
    kv_refs, (out_ref, vt_ref, m_ref, acc_ref) = refs[:5], refs[5:]
    number = pl.program_id(0)
    ctx = lax.axis_index("ctx")

    @pl.when(number == 0)
    def _():
        for n in range(5):
            vt_ref[n] = with_ones(kv_refs[n][:, 256:])

    queries = scaled_queries(q_ref[...])
    m_ref[...] = jnp.full_like(m_ref, NEG)
    acc_ref[...] = jnp.zeros_like(acc_ref)
    tokens = kv_refs[0].shape[0]
    key_pos = lax.broadcasted_iota(jnp.int32, (tokens, ROWS), 0)
    row_pos = lax.broadcasted_iota(jnp.int32, (tokens, ROWS), 1) + number * ROWS
    online_step(queries, kv_refs[0], vt_ref[0], m_ref, acc_ref, key_pos <= row_pos)
    for n in range(1, 5):

        @pl.when(ctx >= n)
        def _():
            online_step(
                queries, kv_refs[n], vt_ref[n], m_ref, acc_ref, key_pos > row_pos if n == 4 else None
            )

    one = acc_ref[0, :256] / acc_ref[0, 256:257]
    two = acc_ref[1, :256] / acc_ref[1, 256:257]
    attended = one - lam_ref[0] * two
    factor = lax.rsqrt(jnp.mean(attended * attended, axis=0, keepdims=True) + EPSILON)
    normed = (attended * factor).T * (gain_ref[...] * (1.0 - LAMBDA_INIT))
    out_ref[...] = normed.astype(jnp.bfloat16)


def window_attention(queries, blocks, lam, gain):
    tokens = queries.shape[0]
    whole = pl.BlockSpec((tokens, 512), lambda i: (0, 0))
    return pl.pallas_call(
        window_kernel,
        name="window",
        grid=(tokens // ROWS,),
        out_shape=jax.ShapeDtypeStruct((tokens, 256), jnp.bfloat16),
        in_specs=[
            pl.BlockSpec(memory_space=pltpu.SMEM),
            pl.BlockSpec((ROWS, 256), lambda i: (i, 0)),
            pl.BlockSpec((1, 256), lambda i: (0, 0)),
        ]
        + [whole] * 5,
        out_specs=pl.BlockSpec((ROWS, 256), lambda i: (i, 0)),
        scratch_shapes=[
            pltpu.VMEM((5, 256 + ONES, tokens), jnp.bfloat16),
            pltpu.VMEM((2, 1, ROWS), jnp.float32),
            pltpu.VMEM((2, 256 + ONES, ROWS), jnp.float32),
        ],
        compiler_params=pltpu.CompilerParams(vmem_limit_bytes=48 * 2**20),
    )(lam.reshape(1), queries, gain.reshape(1, 256), *blocks)


def cycle_kernel(q_ref, kv0_ref, kv1_ref, kv2_ref, out_ref, log_ref, vt_ref, m_ref, acc_ref):
    number = pl.program_id(0)
    ctx = lax.axis_index("ctx")
    kv_refs = (kv0_ref, kv1_ref, kv2_ref)

    @pl.when(number == 0)
    def _():
        for n in range(3):
            vt_ref[n] = with_ones(kv_refs[n][:, 256:])

    queries = scaled_queries(q_ref[...])
    m_ref[...] = jnp.full_like(m_ref, NEG)
    acc_ref[...] = jnp.zeros_like(acc_ref)
    tokens = kv0_ref.shape[0]
    key_pos = lax.broadcasted_iota(jnp.int32, (tokens, ROWS), 0)
    row_pos = lax.broadcasted_iota(jnp.int32, (tokens, ROWS), 1) + number * ROWS
    online_step(queries, kv0_ref, vt_ref[0], m_ref, acc_ref, key_pos <= row_pos)
    for n in (1, 2):

        @pl.when(ctx >= n)
        def _():
            online_step(queries, kv_refs[n], vt_ref[n], m_ref, acc_ref, None)

    for j in range(2):
        total = acc_ref[j, 256:257]
        out_ref[j] = (acc_ref[j, :256] / total).T
        log_ref[j : j + 1, :] = (m_ref[j] + jnp.log2(total)) * LN2


def cycle_attention(queries, blocks):
    tokens = queries.shape[0]
    whole = pl.BlockSpec((tokens, 512), lambda i: (0, 0))
    return pl.pallas_call(
        cycle_kernel,
        name="cycle",
        grid=(tokens // ROWS,),
        out_shape=(
            jax.ShapeDtypeStruct((2, tokens, 256), jnp.float32),
            jax.ShapeDtypeStruct((2, tokens), jnp.float32),
        ),
        in_specs=[pl.BlockSpec((ROWS, 256), lambda i: (i, 0))] + [whole] * 3,
        out_specs=(
            pl.BlockSpec((2, ROWS, 256), lambda i: (0, i, 0)),
            pl.BlockSpec((2, ROWS), lambda i: (0, i)),
        ),
        scratch_shapes=[
            pltpu.VMEM((3, 256 + ONES, tokens), jnp.bfloat16),
            pltpu.VMEM((2, 1, ROWS), jnp.float32),
            pltpu.VMEM((2, 256 + ONES, ROWS), jnp.float32),
        ],
        compiler_params=pltpu.CompilerParams(vmem_limit_bytes=48 * 2**20),
    )(queries, *blocks)


MESH = pl.DeviceIdType.MESH
CHUNKS = 4
SUB = 16


def place():
    head = lax.axis_index("head")
    return lax.axis_index("ctx"), head // 4, (head // 2) % 2, head % 2


def mid_kernel(
    x_cols,
    normed_ref,
    w_own_hbm,
    w_sib_hbm,
    residual_ref,
    gain_ref,
    w_qkv_hbm,
    hidden_ref,
    qkv_ref,
    w_own,
    w_sib,
    w_qkv,
    n_sib,
    part,
    x1_in,
    y1_in,
    x2_out,
    x2_in,
    y2_out,
    y2_in,
    rows_all,
    acc,
    load_sem,
    n_sem,
    x1_sem,
    x2_sem,
    y1_sem,
    y2_sem,
    h1_sem,
    h2_sem,
    g1_sem,
    g2_sem,
    s_sem,
):
    ctx, x, y, core = place()
    width = w_own.shape[1]
    low, high = pl.ds(0, x_cols), pl.ds(x_cols, width - x_cols)

    def across(d):
        return (ctx, lax.rem(x + d, 4) * 4 + y * 2 + core)

    over_y = (ctx, x * 4 + (1 - y) * 2 + core)
    sibling = (ctx, x * 4 + y * 2 + 1 - core)

    loads = [
        pltpu.make_async_copy(source, target, load_sem.at[n])
        for n, (source, target) in enumerate(
            [(w_own_hbm, w_own), (w_sib_hbm, w_sib), (w_qkv_hbm, w_qkv)]
        )
    ]
    for load in loads:
        load.start()

    barrier = pltpu.get_barrier_semaphore()
    for peer in (across(1), across(2), across(3), over_y, sibling):
        pl.semaphore_signal(barrier, inc=1, device_id=peer, device_id_type=MESH)
    pl.semaphore_wait(barrier, 5)

    started = []

    def send(source, target, sems, device):
        copy = pltpu.make_async_remote_copy(
            src_ref=source,
            dst_ref=target,
            send_sem=sems.at[0],
            recv_sem=sems.at[1],
            device_id=device,
            device_id_type=MESH,
        )
        copy.start()
        started.append(copy)
        return copy

    n_copy = send(normed_ref.at[:, 1 - core], n_sib, n_sem, sibling)
    loads[0].wait()
    loads[1].wait()
    n_copy.wait_recv()

    state = [dict() for _ in range(CHUNKS)]
    tile = min(1024, width)

    def stage_a(r):
        own_rows = normed_ref[:, core, r].reshape(8 * SUB, 256)
        sib_rows = n_sib[:, r].reshape(8 * SUB, 256)

        def columns(j, carry):
            span = pl.ds(pl.multiple_of(j * tile, tile), tile)
            value = jnp.dot(own_rows, w_own[:, span], preferred_element_type=jnp.float32)
            value += jnp.dot(sib_rows, w_sib[:, span], preferred_element_type=jnp.float32)
            part[r, :, :, :, span] = value.astype(jnp.bfloat16).reshape(4, 2, SUB, tile)
            return carry

        lax.fori_loop(0, width // tile, columns, 0)
        state[r]["1"] = [
            send(part.at[r, :, 1 - y, :, high], y1_in.at[r], y1_sem.at[r], over_y)
        ] + [
            send(
                part.at[r, lax.rem(x + d, 4), :, :, low],
                x1_in.at[r, d - 1],
                x1_sem.at[r, d - 1],
                across(d),
            )
            for d in (2, 1, 3)
        ]

    def wide(value):
        return value.astype(jnp.float32)

    def stage_b(r):
        for copy in state[r]["1"]:
            copy.wait_recv()
        for d in (1, 2, 3):
            other = lax.rem(x + d, 4)
            y2_out[r, d - 1] = (
                wide(part[r, other, y, :, high]) + wide(y1_in[r, other])
            ).astype(jnp.bfloat16)
        total = wide(part[r, x, 1 - y, :, low])
        for d in (1, 2, 3):
            total += wide(x1_in[r, d - 1, 1 - y])
        x2_out[r] = total.astype(jnp.bfloat16)
        state[r]["2"] = [send(x2_out.at[r], x2_in.at[r], x2_sem.at[r], over_y)] + [
            send(y2_out.at[r, d - 1], y2_in.at[r, d - 1], y2_sem.at[r, d - 1], across(d))
            for d in (2, 1, 3)
        ]

    def stage_c(r):
        for copy in state[r]["2"]:
            copy.wait_recv()
        left = wide(part[r, x, y, :, low]) + wide(x2_in[r])
        right = wide(part[r, x, y, :, high]) + wide(y1_in[r, x])
        for d in (1, 2, 3):
            left += wide(x1_in[r, d - 1, y])
            right += wide(y2_in[r, d - 1])
        left = (wide(residual_ref[r, :, low]) + left).astype(jnp.bfloat16)
        right = (wide(residual_ref[r, :, high]) + right).astype(jnp.bfloat16)
        hidden_ref[r, :, low] = left
        hidden_ref[r, :, high] = right
        left, right = wide(left), wide(right)
        squares = jnp.sum(left * left, axis=-1, keepdims=True)
        squares += jnp.sum(right * right, axis=-1, keepdims=True)
        factor = lax.rsqrt(squares / width + EPSILON)
        mine = rows_all.at[r, x, y, core]
        mine[:, low] = (left * factor * gain_ref[:, low]).astype(jnp.bfloat16)
        mine[:, high] = (right * factor * gain_ref[:, high]).astype(jnp.bfloat16)
        state[r]["3"] = [send(mine.at[:, high], mine.at[:, high], g1_sem.at[r], over_y)] + [
            send(mine.at[:, low], mine.at[:, low], h1_sem.at[r, d - 1], across(d))
            for d in (2, 1, 3)
        ]

    def stage_d(r):
        for copy in state[r]["3"]:
            copy.wait_recv()
        row = rows_all.at[r, :, y, core, :, low]
        column = rows_all.at[r, x, :, core, :, high]
        state[r]["4"] = [send(row, row, h2_sem.at[r], over_y)] + [
            send(column, column, g2_sem.at[r, d - 1], across(d)) for d in (2, 1, 3)
        ]

    def stage_e(r):
        for copy in state[r]["4"]:
            copy.wait_recv()
        ours = rows_all.at[r, :, :, core]
        state[r]["5"] = send(ours, ours, s_sem.at[r], sibling)

    def stage_f(r):
        state[r]["5"].wait_recv()
        if r == 0:
            loads[2].wait()

        def depth(j, carry):
            span = pl.ds(pl.multiple_of(j * tile, tile), tile)
            rows = rows_all[r, :, :, :, :, span].reshape(16 * SUB, tile)
            acc[...] += jnp.dot(rows, w_qkv[span, :], preferred_element_type=jnp.float32)
            return carry

        acc[...] = jnp.zeros_like(acc)
        lax.fori_loop(0, width // tile, depth, 0)
        qkv_ref[:, r] = acc[...].astype(jnp.bfloat16).reshape(16, SUB, acc.shape[1])

    stages = [stage_a, stage_b, stage_c, stage_d, stage_e, stage_f]
    for step in range(CHUNKS - 1 + len(stages)):
        for r in reversed(range(CHUNKS)):
            if 0 <= step - r < len(stages):
                stages[step - r](r)
    for copy in started:
        copy.wait_send()


def project_and_spread(normed, w_own, w_sib, residual, gain, w_qkv):
    width = w_own.shape[1]
    x_cols = width * 13 // 32
    out_cols = w_qkv.shape[1]
    bf16 = jnp.bfloat16
    any_space = pl.BlockSpec(memory_space=pl.ANY)
    vmem = pl.BlockSpec(memory_space=pltpu.VMEM)
    sem = pltpu.SemaphoreType.DMA
    hidden, qkv = pl.pallas_call(
        functools.partial(mid_kernel, x_cols),
        name="project_and_spread",
        out_shape=(
            jax.ShapeDtypeStruct((CHUNKS, SUB, width), bf16),
            jax.ShapeDtypeStruct((16, CHUNKS, SUB, out_cols), bf16),
        ),
        in_specs=[vmem, any_space, any_space, vmem, vmem, any_space],
        out_specs=(vmem, vmem),
        scratch_shapes=[
            pltpu.VMEM((256, width), bf16),
            pltpu.VMEM((256, width), bf16),
            pltpu.VMEM((width, out_cols), bf16),
            pltpu.VMEM((8, CHUNKS, SUB, 256), bf16),
            pltpu.VMEM((CHUNKS, 4, 2, SUB, width), bf16),
            pltpu.VMEM((CHUNKS, 3, 2, SUB, x_cols), bf16),
            pltpu.VMEM((CHUNKS, 4, SUB, width - x_cols), bf16),
            pltpu.VMEM((CHUNKS, SUB, x_cols), bf16),
            pltpu.VMEM((CHUNKS, SUB, x_cols), bf16),
            pltpu.VMEM((CHUNKS, 3, SUB, width - x_cols), bf16),
            pltpu.VMEM((CHUNKS, 3, SUB, width - x_cols), bf16),
            pltpu.VMEM((CHUNKS, 4, 2, 2, SUB, width), bf16),
            pltpu.VMEM((16 * SUB, out_cols), jnp.float32),
            sem((3,)),
            sem((2,)),
            sem((CHUNKS, 3, 2)),
            sem((CHUNKS, 2)),
            sem((CHUNKS, 2)),
            sem((CHUNKS, 3, 2)),
            sem((CHUNKS, 3, 2)),
            sem((CHUNKS, 2)),
            sem((CHUNKS, 2)),
            sem((CHUNKS, 3, 2)),
            sem((CHUNKS, 2)),
        ],
        compiler_params=pltpu.CompilerParams(
            collective_id=0, has_side_effects=True, vmem_limit_bytes=63 * 2**20
        ),
    )(
        normed.reshape(8, 2, CHUNKS, SUB, 256),
        w_own,
        w_sib,
        residual.reshape(CHUNKS, SUB, width),
        gain.reshape(1, width),
        w_qkv,
    )
    return hidden.reshape(CHUNKS * SUB, width), qkv.reshape(16 * CHUNKS * SUB, out_cols)


def on_device(residual, q_win, kv_win, lam_win, gn_gain, w_out_a, norm_gain, w_qkv):
    tokens_here = q_win.shape[0]
    lambda_full = (
        jnp.exp(jnp.sum(lam_win[0] * lam_win[1]))
        - jnp.exp(jnp.sum(lam_win[2] * lam_win[3]))
        + LAMBDA_INIT
    )
    w_sib = lax.ppermute(w_out_a, "head", [(i, i ^ 1) for i in range(lax.axis_size("head"))])
    kv_here = kv_win.reshape(tokens_here, 512)
    blocks = [kv_here] + [passed_along(kv_here, "ctx", behind) for behind in (1, 2, 3, 4)]
    normed = window_attention(q_win.reshape(tokens_here, 256), blocks, lambda_full, gn_gain)
    h_rows, qkv = project_and_spread(
        normed, w_out_a, w_sib, residual, norm_gain, w_qkv.reshape(w_qkv.shape[0], -1)
    )
    kv_next = qkv[:, 256:]
    next_blocks = [kv_next] + [passed_along(kv_next, "ctx", behind) for behind in (1, 2)]
    part_out, log_out = cycle_attention(qkv[:, :256], next_blocks)
    return (
        h_rows,
        part_out.reshape(2, tokens_here, 1, 256),
        log_out.reshape(2, 1, tokens_here),
    )


def solution(mesh):
    in_specs = (
        P(("ctx", "head"), None),
        P("ctx", "head", None),
        P("ctx", "head", None, None),
        P(),
        P(),
        P("head", None),
        P(),
        P(None, "head", None, None),
    )
    out_specs = (P(("ctx", "head"), None), P(None, "ctx", "head", None), P(None, "head", "ctx"))
    return jax.shard_map(
        on_device, mesh=mesh, in_specs=in_specs, out_specs=out_specs, check_vma=False
    )
```

```python
import functools
import math

import jax
import jax.numpy as jnp
from jax import lax
from jax.experimental import pallas as pl
from jax.experimental.pallas import tpu as pltpu
from jax.sharding import PartitionSpec as P

HDIM = 128
WINDOW = 4096
EPSILON = 1e-05
LAMBDA_INIT = 0.8 - 0.6 * math.exp(-3.3)
SCALE = math.log2(math.e) / math.sqrt(HDIM)
LN2 = math.log(2.0)
NEG = -1e30
ONES = 16
ROWS = 256
MESH = pl.DeviceIdType.MESH


def with_ones(values):
    flipped = values.astype(jnp.float32).T.astype(jnp.bfloat16)
    return jnp.concatenate([flipped, jnp.ones((ONES, values.shape[0]), jnp.bfloat16)], axis=0)


def scaled_queries(picked):
    return (picked.astype(jnp.float32) * SCALE).astype(jnp.bfloat16)


def online_step(queries, keys, values_up, m_ref, acc_ref, mask):
    for j in range(2):
        scores = lax.dot_general(
            keys[:, j * HDIM : (j + 1) * HDIM],
            queries[:, j * HDIM : (j + 1) * HDIM],
            (((1,), (1,)), ((), ())),
            preferred_element_type=jnp.float32,
        )
        if mask is not None:
            scores = jnp.where(mask, scores, NEG)
        before = m_ref[j]
        after = jnp.maximum(before, jnp.max(scores, axis=0, keepdims=True))
        weights = jnp.exp2(scores - after).astype(jnp.bfloat16)
        acc_ref[j] = acc_ref[j] * jnp.exp2(before - after) + jnp.dot(
            values_up, weights, preferred_element_type=jnp.float32
        )
        m_ref[j] = after


PIECES = 4


def window_kernel(
    lam_ref, q_ref, gain_ref, kv_ref, out_ref, kv_in, q_scaled, vt_ref, m_ref, acc_ref, up_sem, ring_sem
):
    ctx, head = lax.axis_index("ctx"), lax.axis_index("head")
    ring, z = ctx // 4, lax.rem(ctx, 4)
    tokens = kv_ref.shape[0]
    piece = tokens // PIECES
    over = ((1 - ring) * 4 + z, head)

    def along(e):
        return (ring * 4 + lax.rem(z + e, 4), head)

    def copy_up(n):
        rows = pl.ds(n * piece, piece)
        return pltpu.make_async_remote_copy(
            src_ref=kv_ref.at[rows],
            dst_ref=kv_in.at[3, rows],
            send_sem=up_sem.at[n, 0],
            recv_sem=up_sem.at[n, 1],
            device_id=over,
            device_id_type=MESH,
        )

    def copy_along(e, n, source):
        rows = pl.ds(n * piece, piece)
        return pltpu.make_async_remote_copy(
            src_ref=source.at[rows],
            dst_ref=kv_in.at[e - 1, rows],
            send_sem=ring_sem.at[e - 1, n, 0],
            recv_sem=ring_sem.at[e - 1, n, 1],
            device_id=along(e),
            device_id_type=MESH,
        )

    barrier = pltpu.get_barrier_semaphore()
    for peer in (along(1), along(2), along(3), over):
        pl.semaphore_signal(barrier, inc=1, device_id=peer, device_id_type=MESH)
    pl.semaphore_wait(barrier, 4)

    @pl.when(ring == 0)
    def _():
        for n in range(PIECES):
            copy_up(n).start()

    for e in (1, 3, 2):

        @pl.when(z + e <= 3)
        def _():
            for n in range(PIECES):
                copy_along(e, n, kv_ref).start()

    q_scaled[...] = scaled_queries(q_ref[...])
    m_ref[...] = jnp.full_like(m_ref, NEG)
    acc_ref[...] = jnp.zeros_like(acc_ref)

    def all_queries(keys, edge):
        vt_ref[...] = with_ones(keys[:, 256:])

        def some(i, carry):
            rows = pl.ds(pl.multiple_of(i * ROWS, ROWS), ROWS)
            mask = None
            if edge is not None:
                key_pos = lax.broadcasted_iota(jnp.int32, (tokens, ROWS), 0)
                row_pos = lax.broadcasted_iota(jnp.int32, (tokens, ROWS), 1) + i * ROWS
                mask = key_pos <= row_pos if edge == "own" else key_pos > row_pos
            online_step(q_scaled[rows, :], keys, vt_ref[...], m_ref.at[i], acc_ref.at[i], mask)
            return carry

        lax.fori_loop(0, tokens // ROWS, some, 0)

    all_queries(kv_ref, "own")

    @pl.when(ring == 1)
    def _():
        for n in range(PIECES):
            copy_up(n).wait_recv()
            for e in (1, 3, 2):

                @pl.when(z + e >= 4)
                def _():
                    copy_along(e, n, kv_in.at[3]).start()

        all_queries(kv_in.at[3], "far")

    for e in (1, 3, 2):

        @pl.when(ctx >= e)
        def _():
            for n in range(PIECES):
                copy_along(e, n, kv_ref).wait_recv()
            all_queries(kv_in.at[e - 1], None)

    def finish(i, carry):
        one = acc_ref[i, 0, :256] / acc_ref[i, 0, 256:257]
        two = acc_ref[i, 1, :256] / acc_ref[i, 1, 256:257]
        attended = one - lam_ref[0] * two
        factor = lax.rsqrt(jnp.mean(attended * attended, axis=0, keepdims=True) + EPSILON)
        normed = (attended * factor).T * (gain_ref[...] * (1.0 - LAMBDA_INIT))
        out_ref[pl.ds(pl.multiple_of(i * ROWS, ROWS), ROWS), :] = normed.astype(jnp.bfloat16)
        return carry

    lax.fori_loop(0, tokens // ROWS, finish, 0)

    @pl.when(ring == 0)
    def _():
        for n in range(PIECES):
            copy_up(n).wait_send()

    for e in (1, 2, 3):

        @pl.when((ring == 1) | (z + e <= 3))
        def _():
            for n in range(PIECES):
                copy_along(e, n, kv_ref).wait_send()


def window_attention(queries, keys_values, lam, gain):
    tokens = queries.shape[0]
    vmem = pl.BlockSpec(memory_space=pltpu.VMEM)
    return pl.pallas_call(
        window_kernel,
        name="window",
        out_shape=jax.ShapeDtypeStruct((tokens, 256), jnp.bfloat16),
        in_specs=[pl.BlockSpec(memory_space=pltpu.SMEM), vmem, vmem, vmem],
        out_specs=vmem,
        scratch_shapes=[
            pltpu.VMEM((4, tokens, 512), jnp.bfloat16),
            pltpu.VMEM((tokens, 256), jnp.bfloat16),
            pltpu.VMEM((256 + ONES, tokens), jnp.bfloat16),
            pltpu.VMEM((tokens // ROWS, 2, 1, ROWS), jnp.float32),
            pltpu.VMEM((tokens // ROWS, 2, 256 + ONES, ROWS), jnp.float32),
            pltpu.SemaphoreType.DMA((PIECES, 2)),
            pltpu.SemaphoreType.DMA((3, PIECES, 2)),
        ],
        compiler_params=pltpu.CompilerParams(
            collective_id=1, has_side_effects=True, vmem_limit_bytes=40 * 2**20
        ),
    )(lam.reshape(1), queries, gain.reshape(1, 256), keys_values)


def cycle_kernel(qkv_ref, kv1_ref, kv2_ref, out_ref, log_ref, vt_ref, m_ref, acc_ref):
    number = pl.program_id(0)
    ctx = lax.axis_index("ctx")
    kv_refs = (qkv_ref.at[:, 256:], kv1_ref, kv2_ref)

    @pl.when(number == 0)
    def _():
        for n in range(3):
            vt_ref[n] = with_ones(kv_refs[n][:, 256:])

    queries = scaled_queries(qkv_ref[pl.ds(pl.multiple_of(number * ROWS, ROWS), ROWS), :256])
    m_ref[...] = jnp.full_like(m_ref, NEG)
    acc_ref[...] = jnp.zeros_like(acc_ref)
    tokens = kv1_ref.shape[0]
    key_pos = lax.broadcasted_iota(jnp.int32, (tokens, ROWS), 0)
    row_pos = lax.broadcasted_iota(jnp.int32, (tokens, ROWS), 1) + number * ROWS
    online_step(queries, kv_refs[0], vt_ref[0], m_ref, acc_ref, key_pos <= row_pos)
    for n in (1, 2):

        @pl.when(ctx >= n)
        def _():
            online_step(queries, kv_refs[n], vt_ref[n], m_ref, acc_ref, None)

    for j in range(2):
        total = acc_ref[j, 256:257]
        value = (acc_ref[j, :256] / total).T
        for half in range(2):
            out_ref[j, pl.ds(half, ROWS, stride=2), :] = value[:, half * 128 : half * 128 + 128]
        log_ref[j : j + 1, :] = (m_ref[j] + jnp.log2(total)) * LN2


def cycle_attention(qkv, blocks):
    tokens = qkv.shape[0]
    whole = pl.BlockSpec((tokens, 512), lambda i: (0, 0))
    return pl.pallas_call(
        cycle_kernel,
        name="cycle",
        grid=(tokens // ROWS,),
        out_shape=(
            jax.ShapeDtypeStruct((2, 2 * tokens, 128), jnp.float32),
            jax.ShapeDtypeStruct((2, tokens), jnp.float32),
        ),
        in_specs=[pl.BlockSpec((tokens, 768), lambda i: (0, 0))] + [whole] * 2,
        out_specs=(
            pl.BlockSpec((2, 2 * ROWS, 128), lambda i: (0, i, 0)),
            pl.BlockSpec((2, ROWS), lambda i: (0, i)),
        ),
        scratch_shapes=[
            pltpu.VMEM((3, 256 + ONES, tokens), jnp.bfloat16),
            pltpu.VMEM((2, 1, ROWS), jnp.float32),
            pltpu.VMEM((2, 256 + ONES, ROWS), jnp.float32),
        ],
        compiler_params=pltpu.CompilerParams(vmem_limit_bytes=40 * 2**20),
    )(qkv, *blocks)


CHUNKS = 4
SUB = 16


def place():
    head = lax.axis_index("head")
    return lax.axis_index("ctx"), head // 4, (head // 2) % 2, head % 2


def mid_kernel(
    x_cols,
    normed_ref,
    w_own_hbm,
    w_sib_hbm,
    residual_ref,
    gain_ref,
    w_qkv_hbm,
    hidden_ref,
    qkv_ref,
    kv1_ref,
    kv2_ref,
    w_own,
    w_sib,
    w_qkv,
    n_sib,
    part,
    x1_in,
    y1_in,
    x2_out,
    x2_in,
    y2_out,
    y2_in,
    rows_all,
    acc,
    load_sem,
    n_sem,
    x1_sem,
    x2_sem,
    y1_sem,
    y2_sem,
    h1_sem,
    h2_sem,
    g1_sem,
    g2_sem,
    s_sem,
    next_sem,
):
    ctx, x, y, core = place()
    width = w_own.shape[1]
    low, high = pl.ds(0, x_cols), pl.ds(x_cols, width - x_cols)

    def across(d):
        return (ctx, lax.rem(x + d, 4) * 4 + y * 2 + core)

    over_y = (ctx, x * 4 + (1 - y) * 2 + core)
    sibling = (ctx, x * 4 + y * 2 + 1 - core)

    loads = [
        pltpu.make_async_copy(source, target, load_sem.at[n])
        for n, (source, target) in enumerate(
            [(w_own_hbm, w_own), (w_sib_hbm, w_sib), (w_qkv_hbm, w_qkv)]
        )
    ]
    for load in loads:
        load.start()

    barrier = pltpu.get_barrier_semaphore()
    later = [(lax.rem(ctx + d, 8), lax.axis_index("head")) for d in (1, 2, 6, 7)]
    for peer in [across(1), across(2), across(3), over_y, sibling] + later:
        pl.semaphore_signal(barrier, inc=1, device_id=peer, device_id_type=MESH)
    pl.semaphore_wait(barrier, 9)

    started = []

    def send(source, target, sems, device):
        copy = pltpu.make_async_remote_copy(
            src_ref=source,
            dst_ref=target,
            send_sem=sems.at[0],
            recv_sem=sems.at[1],
            device_id=device,
            device_id_type=MESH,
        )
        copy.start()
        started.append(copy)
        return copy

    n_copy = send(normed_ref.at[:, 1 - core], n_sib, n_sem, sibling)
    loads[0].wait()
    loads[1].wait()
    n_copy.wait_recv()

    state = [dict() for _ in range(CHUNKS)]
    tile = min(1024, width)

    def stage_a(r):
        own_rows = normed_ref[:, core, r].reshape(8 * SUB, 256)
        sib_rows = n_sib[:, r].reshape(8 * SUB, 256)

        def columns(j, carry):
            span = pl.ds(pl.multiple_of(j * tile, tile), tile)
            value = jnp.dot(own_rows, w_own[:, span], preferred_element_type=jnp.float32)
            value += jnp.dot(sib_rows, w_sib[:, span], preferred_element_type=jnp.float32)
            part[r, :, :, :, span] = value.astype(jnp.bfloat16).reshape(4, 2, SUB, tile)
            return carry

        lax.fori_loop(0, width // tile, columns, 0)
        state[r]["1"] = [
            send(part.at[r, :, 1 - y, :, high], y1_in.at[r], y1_sem.at[r], over_y)
        ] + [
            send(
                part.at[r, lax.rem(x + d, 4), :, :, low],
                x1_in.at[r, d - 1],
                x1_sem.at[r, d - 1],
                across(d),
            )
            for d in (2, 1, 3)
        ]

    def wide(value):
        return value.astype(jnp.float32)

    def stage_b(r):
        for copy in state[r]["1"]:
            copy.wait_recv()
        for d in (1, 2, 3):
            other = lax.rem(x + d, 4)
            y2_out[r, d - 1] = (
                wide(part[r, other, y, :, high]) + wide(y1_in[r, other])
            ).astype(jnp.bfloat16)
        total = wide(part[r, x, 1 - y, :, low])
        for d in (1, 2, 3):
            total += wide(x1_in[r, d - 1, 1 - y])
        x2_out[r] = total.astype(jnp.bfloat16)
        state[r]["2"] = [send(x2_out.at[r], x2_in.at[r], x2_sem.at[r], over_y)] + [
            send(y2_out.at[r, d - 1], y2_in.at[r, d - 1], y2_sem.at[r, d - 1], across(d))
            for d in (2, 1, 3)
        ]

    def stage_c(r):
        for copy in state[r]["2"]:
            copy.wait_recv()
        left = wide(part[r, x, y, :, low]) + wide(x2_in[r])
        right = wide(part[r, x, y, :, high]) + wide(y1_in[r, x])
        for d in (1, 2, 3):
            left += wide(x1_in[r, d - 1, y])
            right += wide(y2_in[r, d - 1])
        left = (wide(residual_ref[r, :, low]) + left).astype(jnp.bfloat16)
        right = (wide(residual_ref[r, :, high]) + right).astype(jnp.bfloat16)
        hidden_ref[r, :, low] = left
        hidden_ref[r, :, high] = right
        left, right = wide(left), wide(right)
        squares = jnp.sum(left * left, axis=-1, keepdims=True)
        squares += jnp.sum(right * right, axis=-1, keepdims=True)
        factor = lax.rsqrt(squares / width + EPSILON)
        mine = rows_all.at[r, x, y, core]
        mine[:, low] = (left * factor * gain_ref[:, low]).astype(jnp.bfloat16)
        mine[:, high] = (right * factor * gain_ref[:, high]).astype(jnp.bfloat16)
        state[r]["3"] = [send(mine.at[:, high], mine.at[:, high], g1_sem.at[r], over_y)] + [
            send(mine.at[:, low], mine.at[:, low], h1_sem.at[r, d - 1], across(d))
            for d in (2, 1, 3)
        ]

    def stage_d(r):
        for copy in state[r]["3"]:
            copy.wait_recv()
        row = rows_all.at[r, :, y, core, :, low]
        column = rows_all.at[r, x, :, core, :, high]
        state[r]["4"] = [send(row, row, h2_sem.at[r], over_y)] + [
            send(column, column, g2_sem.at[r, d - 1], across(d)) for d in (2, 1, 3)
        ]

    def stage_e(r):
        for copy in state[r]["4"]:
            copy.wait_recv()
        ours = rows_all.at[r, :, :, core]
        state[r]["5"] = send(ours, ours, s_sem.at[r], sibling)

    def stage_f(r):
        state[r]["5"].wait_recv()
        if r == 0:
            loads[2].wait()

        def depth(j, carry):
            span = pl.ds(pl.multiple_of(j * tile, tile), tile)
            rows = rows_all[r, :, :, :, :, span].reshape(16 * SUB, tile)
            for n in range(3):
                acc[n] += jnp.dot(rows, w_qkv[n, span], preferred_element_type=jnp.float32)
            return carry

        acc[...] = jnp.zeros_like(acc)
        lax.fori_loop(0, width // tile, depth, 0)
        for n in range(3):
            qkv_ref[:, r, :, n * 256 : n * 256 + 256] = (
                acc[n].astype(jnp.bfloat16).reshape(16, SUB, 256)
            )
        for d in (1, 2):

            @pl.when(ctx + d <= 7)
            def _():
                next_copy(d, r).start()

    def next_copy(d, r):
        return pltpu.make_async_remote_copy(
            src_ref=qkv_ref.at[:, r, :, 256:],
            dst_ref=(kv1_ref, kv2_ref)[d - 1].at[:, r],
            send_sem=next_sem.at[d - 1, r, 0],
            recv_sem=next_sem.at[d - 1, r, 1],
            device_id=later[d - 1],
            device_id_type=MESH,
        )

    stages = [stage_a, stage_b, stage_c, stage_d, stage_e, stage_f]
    for step in range(CHUNKS - 1 + len(stages)):
        for r in reversed(range(CHUNKS)):
            if 0 <= step - r < len(stages):
                stages[step - r](r)
    for copy in started:
        copy.wait_send()
    for d in (1, 2):

        @pl.when(ctx + d <= 7)
        def _():
            for r in range(CHUNKS):
                next_copy(d, r).wait_send()

        @pl.when(ctx >= d)
        def _():
            for r in range(CHUNKS):
                next_copy(d, r).wait_recv()


def project_and_spread(normed, w_own, w_sib, residual, gain, w_qkv):
    width = w_own.shape[1]
    x_cols = width * 13 // 32
    out_cols = 768
    bf16 = jnp.bfloat16
    any_space = pl.BlockSpec(memory_space=pl.ANY)
    vmem = pl.BlockSpec(memory_space=pltpu.VMEM)
    sem = pltpu.SemaphoreType.DMA
    hidden, qkv, kv1, kv2 = pl.pallas_call(
        functools.partial(mid_kernel, x_cols),
        name="project_and_spread",
        out_shape=(
            jax.ShapeDtypeStruct((CHUNKS, SUB, width), bf16),
            jax.ShapeDtypeStruct((16, CHUNKS, SUB, out_cols), bf16),
            jax.ShapeDtypeStruct((16, CHUNKS, SUB, 512), bf16),
            jax.ShapeDtypeStruct((16, CHUNKS, SUB, 512), bf16),
        ),
        in_specs=[vmem, any_space, any_space, vmem, vmem, any_space],
        out_specs=(vmem, vmem, any_space, any_space),
        scratch_shapes=[
            pltpu.VMEM((256, width), bf16),
            pltpu.VMEM((256, width), bf16),
            pltpu.VMEM((3, width, 256), bf16),
            pltpu.VMEM((8, CHUNKS, SUB, 256), bf16),
            pltpu.VMEM((CHUNKS, 4, 2, SUB, width), bf16),
            pltpu.VMEM((CHUNKS, 3, 2, SUB, x_cols), bf16),
            pltpu.VMEM((CHUNKS, 4, SUB, width - x_cols), bf16),
            pltpu.VMEM((CHUNKS, SUB, x_cols), bf16),
            pltpu.VMEM((CHUNKS, SUB, x_cols), bf16),
            pltpu.VMEM((CHUNKS, 3, SUB, width - x_cols), bf16),
            pltpu.VMEM((CHUNKS, 3, SUB, width - x_cols), bf16),
            pltpu.VMEM((CHUNKS, 4, 2, 2, SUB, width), bf16),
            pltpu.VMEM((3, 16 * SUB, 256), jnp.float32),
            sem((3,)),
            sem((2,)),
            sem((CHUNKS, 3, 2)),
            sem((CHUNKS, 2)),
            sem((CHUNKS, 2)),
            sem((CHUNKS, 3, 2)),
            sem((CHUNKS, 3, 2)),
            sem((CHUNKS, 2)),
            sem((CHUNKS, 2)),
            sem((CHUNKS, 3, 2)),
            sem((CHUNKS, 2)),
            sem((2, CHUNKS, 2)),
        ],
        compiler_params=pltpu.CompilerParams(
            collective_id=0, has_side_effects=True, vmem_limit_bytes=63 * 2**20
        ),
    )(
        normed.reshape(8, 2, CHUNKS, SUB, 256),
        w_own,
        w_sib,
        residual.reshape(CHUNKS, SUB, width),
        gain.reshape(1, width),
        w_qkv,
    )
    tokens = 16 * CHUNKS * SUB
    return (
        hidden.reshape(CHUNKS * SUB, width),
        qkv.reshape(tokens, out_cols),
        (kv1.reshape(tokens, 512), kv2.reshape(tokens, 512)),
    )


def on_device(residual, q_win, kv_win, lam_win, gn_gain, w_out_a, norm_gain, w_qkv):
    tokens_here = q_win.shape[0]
    lambda_full = (
        jnp.exp(jnp.sum(lam_win[0] * lam_win[1]))
        - jnp.exp(jnp.sum(lam_win[2] * lam_win[3]))
        + LAMBDA_INIT
    )
    w_sib = lax.ppermute(w_out_a, "head", [(i, i ^ 1) for i in range(lax.axis_size("head"))])
    normed = window_attention(
        q_win.reshape(tokens_here, 256), kv_win.reshape(tokens_here, 512), lambda_full, gn_gain
    )
    h_rows, qkv, blocks = project_and_spread(
        normed, w_out_a, w_sib, residual, norm_gain, w_qkv[:, 0].transpose(1, 0, 2)
    )
    part_out, log_out = cycle_attention(qkv, blocks)
    return (
        h_rows,
        part_out.reshape(2, tokens_here, 1, 256),
        log_out.reshape(2, 1, tokens_here),
    )


def solution(mesh):
    in_specs = (
        P(("ctx", "head"), None),
        P("ctx", "head", None),
        P("ctx", "head", None, None),
        P(),
        P(),
        P("head", None),
        P(),
        P(None, "head", None, None),
    )
    out_specs = (P(("ctx", "head"), None), P(None, "ctx", "head", None), P(None, "head", "ctx"))
    return jax.shard_map(
        on_device, mesh=mesh, in_specs=in_specs, out_specs=out_specs, check_vma=False
    )
```

```python
import functools
import math

import jax
import jax.numpy as jnp
from jax import lax
from jax.experimental import pallas as pl
from jax.experimental.pallas import tpu as pltpu
from jax.sharding import PartitionSpec as P

HDIM = 128
WINDOW = 4096
EPSILON = 1e-05
LAMBDA_INIT = 0.8 - 0.6 * math.exp(-3.3)
SCALE = math.log2(math.e) / math.sqrt(HDIM)
LN2 = math.log(2.0)
NEG = -1e30
ONES = 16
ROWS = 256
MESH = pl.DeviceIdType.MESH


def with_ones(values):
    flipped = values.astype(jnp.float32).T.astype(jnp.bfloat16)
    return jnp.concatenate([flipped, jnp.ones((ONES, values.shape[0]), jnp.bfloat16)], axis=0)


def scaled_queries(picked):
    return (picked.astype(jnp.float32) * SCALE).astype(jnp.bfloat16)


def online_step(queries, keys, values_up, m_ref, acc_ref, mask):
    for j in range(2):
        scores = lax.dot_general(
            keys[:, j * HDIM : (j + 1) * HDIM],
            queries[:, j * HDIM : (j + 1) * HDIM],
            (((1,), (1,)), ((), ())),
            preferred_element_type=jnp.float32,
        )
        if mask is not None:
            scores = jnp.where(mask, scores, NEG)
        before = m_ref[j]
        after = jnp.maximum(before, jnp.max(scores, axis=0, keepdims=True))
        weights = jnp.exp2(scores - after).astype(jnp.bfloat16)
        acc_ref[j] = acc_ref[j] * jnp.exp2(before - after) + jnp.dot(
            values_up, weights, preferred_element_type=jnp.float32
        )
        m_ref[j] = after


PIECES = 4


def window_kernel(
    lam_ref, q_ref, gain_ref, kv_ref, out_ref, kv_in, q_scaled, vt_ref, m_ref, acc_ref, up_sem, ring_sem
):
    ctx, head = lax.axis_index("ctx"), lax.axis_index("head")
    ring, z = ctx // 4, lax.rem(ctx, 4)
    tokens = kv_ref.shape[0]
    piece = tokens // PIECES
    over = ((1 - ring) * 4 + z, head)

    def along(e):
        return (ring * 4 + lax.rem(z + e, 4), head)

    def copy_up(n):
        rows = pl.ds(n * piece, piece)
        return pltpu.make_async_remote_copy(
            src_ref=kv_ref.at[rows],
            dst_ref=kv_in.at[3, rows],
            send_sem=up_sem.at[n, 0],
            recv_sem=up_sem.at[n, 1],
            device_id=over,
            device_id_type=MESH,
        )

    def copy_along(e, n, source):
        rows = pl.ds(n * piece, piece)
        return pltpu.make_async_remote_copy(
            src_ref=source.at[rows],
            dst_ref=kv_in.at[e - 1, rows],
            send_sem=ring_sem.at[e - 1, n, 0],
            recv_sem=ring_sem.at[e - 1, n, 1],
            device_id=along(e),
            device_id_type=MESH,
        )

    barrier = pltpu.get_barrier_semaphore()
    for peer in (along(1), along(2), along(3), over):
        pl.semaphore_signal(barrier, inc=1, device_id=peer, device_id_type=MESH)
    pl.semaphore_wait(barrier, 4)

    @pl.when(ring == 0)
    def _():
        for n in range(PIECES):
            copy_up(n).start()

    def send_own(e):
        @pl.when(z + e <= 3)
        def _():
            for n in range(PIECES):
                copy_along(e, n, kv_ref).start()

    def send_on(e, n):
        @pl.when(z + e >= 4)
        def _():
            copy_along(e, n, kv_in.at[3]).start()

    send_own(1)
    send_own(3)

    q_scaled[...] = scaled_queries(q_ref[...])
    m_ref[...] = jnp.full_like(m_ref, NEG)
    acc_ref[...] = jnp.zeros_like(acc_ref)

    def all_queries(keys, edge):
        vt_ref[...] = with_ones(keys[:, 256:])

        def some(i, carry):
            rows = pl.ds(pl.multiple_of(i * ROWS, ROWS), ROWS)
            mask = None
            if edge is not None:
                key_pos = lax.broadcasted_iota(jnp.int32, (tokens, ROWS), 0)
                row_pos = lax.broadcasted_iota(jnp.int32, (tokens, ROWS), 1) + i * ROWS
                mask = key_pos <= row_pos if edge == "own" else key_pos > row_pos
            online_step(q_scaled[rows, :], keys, vt_ref[...], m_ref.at[i], acc_ref.at[i], mask)
            return carry

        lax.fori_loop(0, tokens // ROWS, some, 0)

    all_queries(kv_ref, "own")

    @pl.when(ring == 1)
    def _():
        for n in range(PIECES):
            copy_up(n).wait_recv()
            send_on(3, n)
            send_on(1, n)
        for n in range(PIECES):
            send_on(2, n)

    send_own(2)

    @pl.when(ring == 1)
    def _():
        all_queries(kv_in.at[3], "far")

    for e in (1, 3, 2):

        @pl.when(ctx >= e)
        def _():
            for n in range(PIECES):
                copy_along(e, n, kv_ref).wait_recv()
            all_queries(kv_in.at[e - 1], None)

    pairs = lam_ref[...]
    lam = (
        jnp.exp(jnp.sum(pairs[0:1] * pairs[1:2], axis=1, keepdims=True))
        - jnp.exp(jnp.sum(pairs[2:3] * pairs[3:4], axis=1, keepdims=True))
        + LAMBDA_INIT
    )

    def finish(i, carry):
        one = acc_ref[i, 0, :256] / acc_ref[i, 0, 256:257]
        two = acc_ref[i, 1, :256] / acc_ref[i, 1, 256:257]
        attended = one - lam * two
        factor = lax.rsqrt(jnp.mean(attended * attended, axis=0, keepdims=True) + EPSILON)
        normed = (attended * factor).T * (gain_ref[...] * (1.0 - LAMBDA_INIT))
        out_ref[pl.ds(pl.multiple_of(i * ROWS, ROWS), ROWS), :] = normed.astype(jnp.bfloat16)
        return carry

    lax.fori_loop(0, tokens // ROWS, finish, 0)

    @pl.when(ring == 0)
    def _():
        for n in range(PIECES):
            copy_up(n).wait_send()

    for e in (1, 2, 3):

        @pl.when((ring == 1) | (z + e <= 3))
        def _():
            for n in range(PIECES):
                copy_along(e, n, kv_ref).wait_send()


def window_attention(queries, keys_values, lam_win, gain):
    tokens = queries.shape[0]
    vmem = pl.BlockSpec(memory_space=pltpu.VMEM)
    return pl.pallas_call(
        window_kernel,
        name="window",
        out_shape=jax.ShapeDtypeStruct((tokens, 256), jnp.bfloat16),
        in_specs=[vmem] * 4,
        out_specs=vmem,
        scratch_shapes=[
            pltpu.VMEM((4, tokens, 512), jnp.bfloat16),
            pltpu.VMEM((tokens, 256), jnp.bfloat16),
            pltpu.VMEM((256 + ONES, tokens), jnp.bfloat16),
            pltpu.VMEM((tokens // ROWS, 2, 1, ROWS), jnp.float32),
            pltpu.VMEM((tokens // ROWS, 2, 256 + ONES, ROWS), jnp.float32),
            pltpu.SemaphoreType.DMA((PIECES, 2)),
            pltpu.SemaphoreType.DMA((3, PIECES, 2)),
        ],
        compiler_params=pltpu.CompilerParams(
            collective_id=1, has_side_effects=True, vmem_limit_bytes=40 * 2**20
        ),
    )(lam_win, queries, gain.reshape(1, 256), keys_values)


def cycle_kernel(qkv_ref, kv1_ref, kv2_ref, out_ref, log_ref, vt_ref, m_ref, acc_ref):
    number = pl.program_id(0)
    ctx = lax.axis_index("ctx")
    kv_refs = (qkv_ref.at[:, 256:], kv1_ref, kv2_ref)

    @pl.when(number == 0)
    def _():
        for n in range(3):
            vt_ref[n] = with_ones(kv_refs[n][:, 256:])

    queries = scaled_queries(qkv_ref[pl.ds(pl.multiple_of(number * ROWS, ROWS), ROWS), :256])
    m_ref[...] = jnp.full_like(m_ref, NEG)
    acc_ref[...] = jnp.zeros_like(acc_ref)
    tokens = kv1_ref.shape[0]
    key_pos = lax.broadcasted_iota(jnp.int32, (tokens, ROWS), 0)
    row_pos = lax.broadcasted_iota(jnp.int32, (tokens, ROWS), 1) + number * ROWS
    online_step(queries, kv_refs[0], vt_ref[0], m_ref, acc_ref, key_pos <= row_pos)
    for n in (1, 2):

        @pl.when(ctx >= n)
        def _():
            online_step(queries, kv_refs[n], vt_ref[n], m_ref, acc_ref, None)

    for j in range(2):
        total = acc_ref[j, 256:257]
        value = (acc_ref[j, :256] / total).T
        for half in range(2):
            out_ref[j, pl.ds(half, ROWS, stride=2), :] = value[:, half * 128 : half * 128 + 128]
        log_ref[j : j + 1, :] = (m_ref[j] + jnp.log2(total)) * LN2


def cycle_attention(qkv, blocks):
    tokens = qkv.shape[0]
    whole = pl.BlockSpec((tokens, 512), lambda i: (0, 0))
    return pl.pallas_call(
        cycle_kernel,
        name="cycle",
        grid=(tokens // ROWS,),
        out_shape=(
            jax.ShapeDtypeStruct((2, 2 * tokens, 128), jnp.float32),
            jax.ShapeDtypeStruct((2, tokens), jnp.float32),
        ),
        in_specs=[pl.BlockSpec((tokens, 768), lambda i: (0, 0))] + [whole] * 2,
        out_specs=(
            pl.BlockSpec((2, 2 * ROWS, 128), lambda i: (0, i, 0)),
            pl.BlockSpec((2, ROWS), lambda i: (0, i)),
        ),
        scratch_shapes=[
            pltpu.VMEM((3, 256 + ONES, tokens), jnp.bfloat16),
            pltpu.VMEM((2, 1, ROWS), jnp.float32),
            pltpu.VMEM((2, 256 + ONES, ROWS), jnp.float32),
        ],
        compiler_params=pltpu.CompilerParams(vmem_limit_bytes=40 * 2**20),
    )(qkv, *blocks)


CHUNKS = 4
SUB = 16


def place():
    head = lax.axis_index("head")
    return lax.axis_index("ctx"), head // 4, (head // 2) % 2, head % 2


KINDS = (
    "normed",
    "y1",
    "x1_far",
    "x1_near",
    "x1_sum",
    "x2",
    "y2_far",
    "y2_near",
    "y2_sum",
    "h1",
    "h1_on",
    "g1",
    "h2",
    "g2",
    "g2_on",
    "core",
    "next",
)


def mid_kernel(
    x_cols,
    normed_ref,
    w_own_hbm,
    w_sib_hbm,
    residual_ref,
    gain_ref,
    w_qkv_hbm,
    hidden_ref,
    qkv_ref,
    kv1_ref,
    kv2_ref,
    w_own,
    w_sib,
    w_qkv,
    n_sib,
    part,
    x1_far,
    x1_in,
    y1_in,
    x2_out,
    x2_in,
    y2_far,
    y2_in,
    rows_all,
    acc,
    load_sem,
    sems,
):
    ctx, x, y, core = place()
    width = w_own.shape[1]
    y_cols = width - x_cols
    low, high = pl.ds(0, x_cols), pl.ds(x_cols, y_cols)
    low_half = (pl.ds(0, x_cols // 2), pl.ds(x_cols // 2, x_cols // 2))
    high_half = (pl.ds(x_cols, y_cols // 2), pl.ds(x_cols + y_cols // 2, y_cols // 2))
    y_half = (pl.ds(0, y_cols // 2), pl.ds(y_cols // 2, y_cols // 2))
    head = lax.axis_index("head")
    beside = (lax.rem(x + 1, 4), lax.rem(x + 3, 4))
    opposite = lax.rem(x + 2, 4)
    along = [(ctx, place_x * 4 + y * 2 + core) for place_x in beside]
    over_y = (ctx, x * 4 + (1 - y) * 2 + core)
    sibling = (ctx, x * 4 + y * 2 + 1 - core)
    blocks = lax.axis_size("ctx")
    later = [(lax.rem(ctx + d, blocks), head) for d in (1, 2, blocks - 2, blocks - 1)]

    loads = [
        pltpu.make_async_copy(source, target, load_sem.at[n])
        for n, (source, target) in enumerate(
            [(w_own_hbm, w_own), (w_sib_hbm, w_sib), (w_qkv_hbm, w_qkv)]
        )
    ]
    for load in loads:
        load.start()

    barrier = pltpu.get_barrier_semaphore()
    for peer in along + [over_y, sibling] + later:
        pl.semaphore_signal(barrier, inc=1, device_id=peer, device_id_type=MESH)
    pl.semaphore_wait(barrier, 8)

    started = []
    pending = {}

    def describe(kind, r, side, source, target, device):
        kind = KINDS.index(kind)
        return pltpu.make_async_remote_copy(
            src_ref=source,
            dst_ref=target,
            send_sem=sems.at[kind, r, side, 0],
            recv_sem=sems.at[kind, r, side, 1],
            device_id=device,
            device_id_type=MESH,
        )

    def send(kind, r, side, source, target, device):
        copy = describe(kind, r, side, source, target, device)
        copy.start()
        started.append(copy)
        pending[kind, r, side] = copy

    def arrived(kind, r, sides=(0,)):
        for side in sides:
            pending[kind, r, side].wait_recv()

    def wide(value):
        return value.astype(jnp.float32)

    both = (0, 1)
    send("normed", 0, 0, normed_ref.at[:, 1 - core], n_sib, sibling)
    loads[0].wait()
    loads[1].wait()
    arrived("normed", 0)
    tile = min(1024, width)

    def project(r):
        own_rows = normed_ref[:, core, r].reshape(8 * SUB, 256)
        sib_rows = n_sib[:, r].reshape(8 * SUB, 256)

        def columns(j, carry):
            span = pl.ds(pl.multiple_of(j * tile, tile), tile)
            value = jnp.dot(own_rows, w_own[:, span], preferred_element_type=jnp.float32)
            value += jnp.dot(sib_rows, w_sib[:, span], preferred_element_type=jnp.float32)
            part[r, :, :, :, span] = value.astype(jnp.bfloat16).reshape(4, 2, SUB, tile)
            return carry

        lax.fori_loop(0, width // tile, columns, 0)
        for s in both:
            source = part.at[r, opposite, :, :, low_half[s]]
            send("x1_far", r, s, source, x1_far.at[r, s], along[s])
        send("y1", r, 0, part.at[r, :, 1 - y, :, high], y1_in.at[r], over_y)
        for s in both:
            source = part.at[r, beside[s], :, :, low_half[1 - s]]
            send("x1_near", r, s, source, x1_in.at[r, s, :, :, low_half[1 - s]], along[s])

    def relay_x1(r):
        arrived("x1_far", r, both)
        for s in both:
            ours = part.at[r, beside[s], :, :, low_half[s]]
            ours[...] = (wide(ours[...]) + wide(x1_far[r, s])).astype(jnp.bfloat16)
            send("x1_sum", r, s, ours, x1_in.at[r, s, :, :, low_half[s]], along[s])

    def second(r):
        arrived("y1", r)
        for place_x in (opposite,) + beside:
            ours = part.at[r, place_x, y, :, high]
            ours[...] = (wide(ours[...]) + wide(y1_in[r, place_x])).astype(jnp.bfloat16)
        for s in both:
            source = part.at[r, opposite, y, :, high_half[s]]
            send("y2_far", r, s, source, y2_far.at[r, s], along[s])
        for s in both:
            source = part.at[r, beside[s], y, :, high_half[1 - s]]
            send("y2_near", r, s, source, y2_in.at[r, s, :, y_half[1 - s]], along[s])
        arrived("x1_near", r, both)
        arrived("x1_sum", r, both)
        total = wide(part[r, x, 1 - y, :, low])
        for s in both:
            total += wide(x1_in[r, s, 1 - y])
        x2_out[r] = total.astype(jnp.bfloat16)
        send("x2", r, 0, x2_out.at[r], x2_in.at[r], over_y)

    def relay_y2(r):
        arrived("y2_far", r, both)
        for s in both:
            ours = part.at[r, beside[s], y, :, high_half[s]]
            ours[...] = (wide(ours[...]) + wide(y2_far[r, s])).astype(jnp.bfloat16)
            send("y2_sum", r, s, ours, y2_in.at[r, s, :, y_half[s]], along[s])

    def finish(r):
        arrived("x2", r)
        arrived("y2_near", r, both)
        arrived("y2_sum", r, both)
        left = wide(part[r, x, y, :, low]) + wide(x2_in[r])
        right = wide(part[r, x, y, :, high]) + wide(y1_in[r, x])
        for s in both:
            left += wide(x1_in[r, s, y])
            right += wide(y2_in[r, s])
        left = (wide(residual_ref[r, :, low]) + left).astype(jnp.bfloat16)
        right = (wide(residual_ref[r, :, high]) + right).astype(jnp.bfloat16)
        hidden_ref[r, :, low] = left
        hidden_ref[r, :, high] = right
        left, right = wide(left), wide(right)
        squares = jnp.sum(left * left, axis=-1, keepdims=True)
        squares += jnp.sum(right * right, axis=-1, keepdims=True)
        factor = lax.rsqrt(squares / width + EPSILON)
        mine = rows_all.at[r, x, y, core]
        mine[:, low] = (left * factor * gain_ref[:, low]).astype(jnp.bfloat16)
        mine[:, high] = (right * factor * gain_ref[:, high]).astype(jnp.bfloat16)
        for s in both:
            send("h1", r, s, mine.at[:, low], mine.at[:, low], along[s])
        send("g1", r, 0, mine.at[:, high], mine.at[:, high], over_y)

    def pass_h1(r):
        arrived("h1", r, both)
        for s in both:
            came = rows_all.at[r, beside[1 - s], y, core, :, low_half[s]]
            send("h1_on", r, s, came, came, along[s])

    def spread(r):
        arrived("g1", r)
        column = rows_all.at[r, x, :, core, :, high]
        for s in both:
            send("g2", r, s, column, column, along[s])
        arrived("h1_on", r, both)
        row = rows_all.at[r, :, y, core, :, low]
        send("h2", r, 0, row, row, over_y)

    def pass_g2(r):
        arrived("g2", r, both)
        for s in both:
            came = rows_all.at[r, beside[1 - s], :, core, :, high_half[s]]
            send("g2_on", r, s, came, came, along[s])

    def share(r):
        arrived("h2", r)
        ours = rows_all.at[r, :, :, core, :, low]
        send("core", r, 0, ours, ours, sibling)
        arrived("g2_on", r, both)
        ours = rows_all.at[r, :, :, core, :, high]
        send("core", r, 1, ours, ours, sibling)

    def next_copy(d, r, source):
        target = (kv1_ref, kv2_ref)[d - 1].at[:, r]
        return describe("next", r, d - 1, source, target, later[d - 1])

    def project_next(r):
        arrived("core", r, both)
        if r == 0:
            loads[2].wait()

        def depth(j, carry):
            span = pl.ds(pl.multiple_of(j * tile, tile), tile)
            rows = rows_all[r, :, :, :, :, span].reshape(16 * SUB, tile)
            for n in range(3):
                acc[n] += jnp.dot(rows, w_qkv[n, span], preferred_element_type=jnp.float32)
            return carry

        acc[...] = jnp.zeros_like(acc)
        lax.fori_loop(0, width // tile, depth, 0)
        for n in range(3):
            qkv_ref[:, r, :, n * 256 : n * 256 + 256] = (
                acc[n].astype(jnp.bfloat16).reshape(16, SUB, 256)
            )
        source = qkv_ref.at[:, r, :, 256:]

        @pl.when(ctx <= 6)
        def _():
            next_copy(1, r, source).start()

        @pl.when((ctx <= 5) & (ctx != 3))
        def _():
            next_copy(2, r, source).start()

    def hand_on(r):
        source = qkv_ref.at[:, r, :, 256:]

        @pl.when(ctx >= 1)
        def _():
            next_copy(1, r, source).wait_recv()

        @pl.when(ctx == 4)
        def _():
            copy = describe("next", r, 2, kv1_ref.at[:, r], kv2_ref.at[:, r], later[0])
            copy.start()
            copy.wait_send()

        @pl.when(ctx == 5)
        def _():
            describe("next", r, 2, kv1_ref.at[:, r], kv2_ref.at[:, r], later[0]).wait_recv()

    stages = [
        project,
        relay_x1,
        second,
        relay_y2,
        finish,
        pass_h1,
        spread,
        pass_g2,
        share,
        project_next,
        hand_on,
    ]
    for step in range(CHUNKS - 1 + len(stages)):
        for r in reversed(range(CHUNKS)):
            if 0 <= step - r < len(stages):
                stages[step - r](r)
    for copy in started:
        copy.wait_send()
    for r in range(CHUNKS):
        source = qkv_ref.at[:, r, :, 256:]

        @pl.when(ctx <= 6)
        def _():
            next_copy(1, r, source).wait_send()

        @pl.when((ctx <= 5) & (ctx != 3))
        def _():
            next_copy(2, r, source).wait_send()

        @pl.when((ctx >= 2) & (ctx != 5))
        def _():
            next_copy(2, r, source).wait_recv()


def project_and_spread(normed, w_own, w_sib, residual, gain, w_qkv):
    width = w_own.shape[1]
    x_cols = width * 5 // 8
    out_cols = 768
    bf16 = jnp.bfloat16
    any_space = pl.BlockSpec(memory_space=pl.ANY)
    vmem = pl.BlockSpec(memory_space=pltpu.VMEM)
    sem = pltpu.SemaphoreType.DMA
    hidden, qkv, kv1, kv2 = pl.pallas_call(
        functools.partial(mid_kernel, x_cols),
        name="project_and_spread",
        out_shape=(
            jax.ShapeDtypeStruct((CHUNKS, SUB, width), bf16),
            jax.ShapeDtypeStruct((16, CHUNKS, SUB, out_cols), bf16),
            jax.ShapeDtypeStruct((16, CHUNKS, SUB, 512), bf16),
            jax.ShapeDtypeStruct((16, CHUNKS, SUB, 512), bf16),
        ),
        in_specs=[vmem, any_space, any_space, vmem, vmem, any_space],
        out_specs=(vmem, vmem, any_space, any_space),
        scratch_shapes=[
            pltpu.VMEM((256, width), bf16),
            pltpu.VMEM((256, width), bf16),
            pltpu.VMEM((3, width, 256), bf16),
            pltpu.VMEM((8, CHUNKS, SUB, 256), bf16),
            pltpu.VMEM((CHUNKS, 4, 2, SUB, width), bf16),
            pltpu.VMEM((CHUNKS, 2, 2, SUB, x_cols // 2), bf16),
            pltpu.VMEM((CHUNKS, 2, 2, SUB, x_cols), bf16),
            pltpu.VMEM((CHUNKS, 4, SUB, width - x_cols), bf16),
            pltpu.VMEM((CHUNKS, SUB, x_cols), bf16),
            pltpu.VMEM((CHUNKS, SUB, x_cols), bf16),
            pltpu.VMEM((CHUNKS, 2, SUB, (width - x_cols) // 2), bf16),
            pltpu.VMEM((CHUNKS, 2, SUB, width - x_cols), bf16),
            pltpu.VMEM((CHUNKS, 4, 2, 2, SUB, width), bf16),
            pltpu.VMEM((3, 16 * SUB, 256), jnp.float32),
            sem((3,)),
            sem((len(KINDS), CHUNKS, 3, 2)),
        ],
        compiler_params=pltpu.CompilerParams(
            collective_id=0, has_side_effects=True, vmem_limit_bytes=63 * 2**20
        ),
    )(
        normed.reshape(8, 2, CHUNKS, SUB, 256),
        w_own,
        w_sib,
        residual.reshape(CHUNKS, SUB, width),
        gain.reshape(1, width),
        w_qkv,
    )
    tokens = 16 * CHUNKS * SUB
    return (
        hidden.reshape(CHUNKS * SUB, width),
        qkv.reshape(tokens, out_cols),
        (kv1.reshape(tokens, 512), kv2.reshape(tokens, 512)),
    )


def on_device(residual, q_win, kv_win, lam_win, gn_gain, w_out_a, norm_gain, w_qkv):
    tokens_here = q_win.shape[0]
    w_sib = lax.ppermute(w_out_a, "head", [(i, i ^ 1) for i in range(lax.axis_size("head"))])
    normed = window_attention(
        q_win.reshape(tokens_here, 256), kv_win.reshape(tokens_here, 512), lam_win, gn_gain
    )
    h_rows, qkv, blocks = project_and_spread(
        normed, w_out_a, w_sib, residual, norm_gain, w_qkv[:, 0].transpose(1, 0, 2)
    )
    part_out, log_out = cycle_attention(qkv, blocks)
    return (
        h_rows,
        part_out.reshape(2, tokens_here, 1, 256),
        log_out.reshape(2, 1, tokens_here),
    )


def solution(mesh):
    in_specs = (
        P(("ctx", "head"), None),
        P("ctx", "head", None),
        P("ctx", "head", None, None),
        P(),
        P(),
        P("head", None),
        P(),
        P(None, "head", None, None),
    )
    out_specs = (P(("ctx", "head"), None), P(None, "ctx", "head", None), P(None, "head", "ctx"))
    return jax.shard_map(
        on_device, mesh=mesh, in_specs=in_specs, out_specs=out_specs, check_vma=False
    )
```

```python
import functools
import math

import jax
import jax.numpy as jnp
from jax import lax
from jax.experimental import pallas as pl
from jax.experimental.pallas import tpu as pltpu
from jax.sharding import PartitionSpec as P

HDIM = 128
WINDOW = 4096
EPSILON = 1e-05
LAMBDA_INIT = 0.8 - 0.6 * math.exp(-3.3)
SCALE = math.log2(math.e) / math.sqrt(HDIM)
LN2 = math.log(2.0)
NEG = -1e30
ONES = 16
ROWS = 256
MESH = pl.DeviceIdType.MESH


def with_ones(values):
    flipped = values.astype(jnp.float32).T.astype(jnp.bfloat16)
    return jnp.concatenate([flipped, jnp.ones((ONES, values.shape[0]), jnp.bfloat16)], axis=0)


def scaled_queries(picked):
    return (picked.astype(jnp.float32) * SCALE).astype(jnp.bfloat16)


def online_step(queries, keys, values_up, m_ref, acc_ref, mask):
    for j in range(2):
        scores = lax.dot_general(
            keys[:, j * HDIM : (j + 1) * HDIM],
            queries[:, j * HDIM : (j + 1) * HDIM],
            (((1,), (1,)), ((), ())),
            preferred_element_type=jnp.float32,
        )
        if mask is not None:
            scores = jnp.where(mask, scores, NEG)
        before = m_ref[j]
        after = jnp.maximum(before, jnp.max(scores, axis=0, keepdims=True))
        weights = jnp.exp2(scores - after).astype(jnp.bfloat16)
        acc_ref[j] = acc_ref[j] * jnp.exp2(before - after) + jnp.dot(
            values_up, weights, preferred_element_type=jnp.float32
        )
        m_ref[j] = after


PIECES = 8


def window_kernel(
    lam_ref, q_ref, gain_ref, kv_ref, out_ref, kv_in, q_scaled, vt_ref, m_ref, acc_ref, up_sem, ring_sem, on_sem
):
    ctx, head = lax.axis_index("ctx"), lax.axis_index("head")
    ring, z = ctx // 4, lax.rem(ctx, 4)
    tokens = kv_ref.shape[0]
    piece = tokens // PIECES
    over = ((1 - ring) * 4 + z, head)

    def along(e):
        return (ring * 4 + lax.rem(z + e, 4), head)

    def copy_up(n):
        rows = pl.ds(n * piece, piece)
        return pltpu.make_async_remote_copy(
            src_ref=kv_ref.at[rows],
            dst_ref=kv_in.at[3, rows],
            send_sem=up_sem.at[n, 0],
            recv_sem=up_sem.at[n, 1],
            device_id=over,
            device_id_type=MESH,
        )

    def copy_along(e, n, source):
        rows = pl.ds(n * piece, piece)
        return pltpu.make_async_remote_copy(
            src_ref=source.at[rows],
            dst_ref=kv_in.at[e - 1, rows],
            send_sem=ring_sem.at[e - 1, n, 0],
            recv_sem=ring_sem.at[e - 1, n, 1],
            device_id=along(e),
            device_id_type=MESH,
        )

    barrier = pltpu.get_barrier_semaphore()
    for peer in (along(1), along(2), along(3), over):
        pl.semaphore_signal(barrier, inc=1, device_id=peer, device_id_type=MESH)
    pl.semaphore_wait(barrier, 4)

    @pl.when(ring == 0)
    def _():
        for n in range(PIECES):
            copy_up(n).start()

    def copy_on(side, n):
        rows = pl.ds(n * piece, piece)
        return pltpu.make_async_remote_copy(
            src_ref=kv_in.at[2 * side, rows],
            dst_ref=kv_in.at[1, rows],
            send_sem=on_sem.at[side, n],
            recv_sem=ring_sem.at[1, n, 1],
            device_id=along(1 + 2 * side),
            device_id_type=MESH,
        )

    def passes_on(side, n):
        if side == 0:
            return (z <= 2) & (ctx >= 1) if n % 2 == 0 else (z == 2)
        return (ctx >= 3) & (z >= 1) if n % 2 == 1 else (ring == 1) & (z == 1)

    for e in (1, 3):

        @pl.when(z + e <= 3)
        def _():
            for n in range(PIECES):
                copy_along(e, n, kv_ref).start()

    q_scaled[...] = scaled_queries(q_ref[...])
    m_ref[...] = jnp.full_like(m_ref, NEG)
    acc_ref[...] = jnp.zeros_like(acc_ref)

    def all_queries(keys, edge):
        vt_ref[...] = with_ones(keys[:, 256:])

        def some(i, carry):
            rows = pl.ds(pl.multiple_of(i * ROWS, ROWS), ROWS)
            mask = None
            if edge is not None:
                key_pos = lax.broadcasted_iota(jnp.int32, (tokens, ROWS), 0)
                row_pos = lax.broadcasted_iota(jnp.int32, (tokens, ROWS), 1) + i * ROWS
                mask = key_pos <= row_pos if edge == "own" else key_pos > row_pos
            online_step(q_scaled[rows, :], keys, vt_ref[...], m_ref.at[i], acc_ref.at[i], mask)
            return carry

        lax.fori_loop(0, tokens // ROWS, some, 0)

    all_queries(kv_ref, "own")

    @pl.when(ring == 1)
    def _():
        for n in range(PIECES):
            copy_up(n).wait_recv()
            for e in (3, 1):

                @pl.when(z + e >= 4)
                def _():
                    copy_along(e, n, kv_in.at[3]).start()

    for side in (0, 1):

        @pl.when(ctx >= 1 + 2 * side)
        def _():
            for n in range(PIECES):
                copy_along(1 + 2 * side, n, kv_ref).wait_recv()

        for n in range(PIECES):

            @pl.when(passes_on(side, n))
            def _():
                copy_on(side, n).start()

    @pl.when(ring == 1)
    def _():
        all_queries(kv_in.at[3], "far")

    for e in (1, 3, 2):

        @pl.when(ctx >= e)
        def _():
            if e == 2:
                for n in range(PIECES):
                    copy_along(2, n, kv_ref).wait_recv()
            all_queries(kv_in.at[e - 1], None)

    pairs = lam_ref[...]
    lam = (
        jnp.exp(jnp.sum(pairs[0:1] * pairs[1:2], axis=1, keepdims=True))
        - jnp.exp(jnp.sum(pairs[2:3] * pairs[3:4], axis=1, keepdims=True))
        + LAMBDA_INIT
    )

    def finish(i, carry):
        one = acc_ref[i, 0, :256] / acc_ref[i, 0, 256:257]
        two = acc_ref[i, 1, :256] / acc_ref[i, 1, 256:257]
        attended = one - lam * two
        factor = lax.rsqrt(jnp.mean(attended * attended, axis=0, keepdims=True) + EPSILON)
        normed = (attended * factor).T * (gain_ref[...] * (1.0 - LAMBDA_INIT))
        out_ref[pl.ds(pl.multiple_of(i * ROWS, ROWS), ROWS), :] = normed.astype(jnp.bfloat16)
        return carry

    lax.fori_loop(0, tokens // ROWS, finish, 0)

    @pl.when(ring == 0)
    def _():
        for n in range(PIECES):
            copy_up(n).wait_send()

    for e in (1, 3):

        @pl.when((ring == 1) | (z + e <= 3))
        def _():
            for n in range(PIECES):
                copy_along(e, n, kv_ref).wait_send()

    for side in (0, 1):
        for n in range(PIECES):

            @pl.when(passes_on(side, n))
            def _():
                copy_on(side, n).wait_send()


def window_attention(queries, keys_values, lam_win, gain):
    tokens = queries.shape[0]
    vmem = pl.BlockSpec(memory_space=pltpu.VMEM)
    return pl.pallas_call(
        window_kernel,
        name="window",
        out_shape=jax.ShapeDtypeStruct((tokens, 256), jnp.bfloat16),
        in_specs=[vmem] * 4,
        out_specs=vmem,
        scratch_shapes=[
            pltpu.VMEM((4, tokens, 512), jnp.bfloat16),
            pltpu.VMEM((tokens, 256), jnp.bfloat16),
            pltpu.VMEM((256 + ONES, tokens), jnp.bfloat16),
            pltpu.VMEM((tokens // ROWS, 2, 1, ROWS), jnp.float32),
            pltpu.VMEM((tokens // ROWS, 2, 256 + ONES, ROWS), jnp.float32),
            pltpu.SemaphoreType.DMA((PIECES, 2)),
            pltpu.SemaphoreType.DMA((3, PIECES, 2)),
            pltpu.SemaphoreType.DMA((2, PIECES)),
        ],
        compiler_params=pltpu.CompilerParams(
            collective_id=1, has_side_effects=True, vmem_limit_bytes=40 * 2**20
        ),
    )(lam_win, queries, gain.reshape(1, 256), keys_values)


def cycle_kernel(qkv_ref, kv1_ref, kv2_ref, out_ref, log_ref, vt_ref, m_ref, acc_ref):
    number = pl.program_id(0)
    ctx = lax.axis_index("ctx")
    kv_refs = (qkv_ref.at[:, 256:], kv1_ref, kv2_ref)

    @pl.when(number == 0)
    def _():
        for n in range(3):
            vt_ref[n] = with_ones(kv_refs[n][:, 256:])

    queries = scaled_queries(qkv_ref[pl.ds(pl.multiple_of(number * ROWS, ROWS), ROWS), :256])
    m_ref[...] = jnp.full_like(m_ref, NEG)
    acc_ref[...] = jnp.zeros_like(acc_ref)
    tokens = kv1_ref.shape[0]
    key_pos = lax.broadcasted_iota(jnp.int32, (tokens, ROWS), 0)
    row_pos = lax.broadcasted_iota(jnp.int32, (tokens, ROWS), 1) + number * ROWS
    online_step(queries, kv_refs[0], vt_ref[0], m_ref, acc_ref, key_pos <= row_pos)
    for n in (1, 2):

        @pl.when(ctx >= n)
        def _():
            online_step(queries, kv_refs[n], vt_ref[n], m_ref, acc_ref, None)

    for j in range(2):
        total = acc_ref[j, 256:257]
        value = (acc_ref[j, :256] / total).T
        for half in range(2):
            out_ref[j, pl.ds(half, ROWS, stride=2), :] = value[:, half * 128 : half * 128 + 128]
        log_ref[j : j + 1, :] = (m_ref[j] + jnp.log2(total)) * LN2


def cycle_attention(qkv, blocks):
    tokens = qkv.shape[0]
    whole = pl.BlockSpec((tokens, 512), lambda i: (0, 0))
    return pl.pallas_call(
        cycle_kernel,
        name="cycle",
        grid=(tokens // ROWS,),
        out_shape=(
            jax.ShapeDtypeStruct((2, 2 * tokens, 128), jnp.float32),
            jax.ShapeDtypeStruct((2, tokens), jnp.float32),
        ),
        in_specs=[pl.BlockSpec((tokens, 768), lambda i: (0, 0))] + [whole] * 2,
        out_specs=(
            pl.BlockSpec((2, 2 * ROWS, 128), lambda i: (0, i, 0)),
            pl.BlockSpec((2, ROWS), lambda i: (0, i)),
        ),
        scratch_shapes=[
            pltpu.VMEM((3, 256 + ONES, tokens), jnp.bfloat16),
            pltpu.VMEM((2, 1, ROWS), jnp.float32),
            pltpu.VMEM((2, 256 + ONES, ROWS), jnp.float32),
        ],
        compiler_params=pltpu.CompilerParams(vmem_limit_bytes=40 * 2**20),
    )(qkv, *blocks)


CHUNKS = 4
SUB = 16


def place():
    head = lax.axis_index("head")
    return lax.axis_index("ctx"), head // 4, (head // 2) % 2, head % 2


KINDS = (
    "normed",
    "y1",
    "x1_far",
    "x1_near",
    "x1_sum",
    "x2",
    "y2_far",
    "y2_near",
    "y2_sum",
    "h1",
    "h1_on",
    "g1",
    "h2",
    "g2",
    "g2_on",
    "core",
    "next",
)


def mid_kernel(
    x_cols,
    g_cols,
    normed_ref,
    w_own_hbm,
    w_sib_hbm,
    residual_ref,
    gain_ref,
    w_qkv_hbm,
    hidden_ref,
    qkv_ref,
    kv1_ref,
    kv2_ref,
    w_own,
    w_sib,
    w_qkv,
    n_sib,
    part,
    x1_far,
    x1_in,
    y1_in,
    x2_out,
    x2_in,
    y2_far,
    y2_in,
    rows_all,
    acc,
    load_sem,
    sems,
):
    ctx, x, y, core = place()
    width = w_own.shape[1]
    y_cols = width - x_cols
    low, high = pl.ds(0, x_cols), pl.ds(x_cols, y_cols)
    low_half = (pl.ds(0, x_cols // 2), pl.ds(x_cols // 2, x_cols // 2))
    high_half = (pl.ds(x_cols, y_cols // 2), pl.ds(x_cols + y_cols // 2, y_cols // 2))
    g_low, g_high = pl.ds(0, g_cols), pl.ds(g_cols, width - g_cols)
    g_low_half = (pl.ds(0, g_cols // 2), pl.ds(g_cols // 2, g_cols // 2))
    g_high_half = tuple(
        pl.ds(g_cols + s * ((width - g_cols) // 2), (width - g_cols) // 2) for s in (0, 1)
    )
    y_half = (pl.ds(0, y_cols // 2), pl.ds(y_cols // 2, y_cols // 2))
    head = lax.axis_index("head")
    beside = (lax.rem(x + 1, 4), lax.rem(x + 3, 4))
    opposite = lax.rem(x + 2, 4)
    along = [(ctx, place_x * 4 + y * 2 + core) for place_x in beside]
    over_y = (ctx, x * 4 + (1 - y) * 2 + core)
    sibling = (ctx, x * 4 + y * 2 + 1 - core)
    blocks = lax.axis_size("ctx")
    later = [(lax.rem(ctx + d, blocks), head) for d in (1, 2, blocks - 2, blocks - 1)]

    loads = [
        pltpu.make_async_copy(source, target, load_sem.at[n])
        for n, (source, target) in enumerate(
            [(w_own_hbm, w_own), (w_sib_hbm, w_sib), (w_qkv_hbm, w_qkv)]
        )
    ]
    for load in loads:
        load.start()

    barrier = pltpu.get_barrier_semaphore()
    for peer in along + [over_y, sibling] + later:
        pl.semaphore_signal(barrier, inc=1, device_id=peer, device_id_type=MESH)
    pl.semaphore_wait(barrier, 8)

    started = []
    pending = {}

    def describe(kind, r, side, source, target, device):
        kind = KINDS.index(kind)
        return pltpu.make_async_remote_copy(
            src_ref=source,
            dst_ref=target,
            send_sem=sems.at[kind, r, side, 0],
            recv_sem=sems.at[kind, r, side, 1],
            device_id=device,
            device_id_type=MESH,
        )

    def send(kind, r, side, source, target, device):
        copy = describe(kind, r, side, source, target, device)
        copy.start()
        started.append(copy)
        pending[kind, r, side] = copy

    def arrived(kind, r, sides=(0,)):
        for side in sides:
            pending[kind, r, side].wait_recv()

    def wide(value):
        return value.astype(jnp.float32)

    both = (0, 1)
    send("normed", 0, 0, normed_ref.at[:, 1 - core], n_sib, sibling)
    loads[0].wait()
    loads[1].wait()
    arrived("normed", 0)
    tile = min(1024, width)

    def project(r):
        own_rows = normed_ref[:, core, r].reshape(8 * SUB, 256)
        sib_rows = n_sib[:, r].reshape(8 * SUB, 256)

        def columns(j, carry):
            span = pl.ds(pl.multiple_of(j * tile, tile), tile)
            value = jnp.dot(own_rows, w_own[:, span], preferred_element_type=jnp.float32)
            value += jnp.dot(sib_rows, w_sib[:, span], preferred_element_type=jnp.float32)
            part[r, :, :, :, span] = value.astype(jnp.bfloat16).reshape(4, 2, SUB, tile)
            return carry

        lax.fori_loop(0, width // tile, columns, 0)
        for s in both:
            source = part.at[r, opposite, :, :, low_half[s]]
            send("x1_far", r, s, source, x1_far.at[r, s], along[s])
        send("y1", r, 0, part.at[r, :, 1 - y, :, high], y1_in.at[r], over_y)
        for s in both:
            source = part.at[r, beside[s], :, :, low_half[1 - s]]
            send("x1_near", r, s, source, x1_in.at[r, s, :, :, low_half[1 - s]], along[s])

    def relay_x1(r):
        arrived("x1_far", r, both)
        for s in both:
            ours = part.at[r, beside[s], :, :, low_half[s]]
            ours[...] = (wide(ours[...]) + wide(x1_far[r, s])).astype(jnp.bfloat16)
            send("x1_sum", r, s, ours, x1_in.at[r, s, :, :, low_half[s]], along[s])

    def second(r):
        arrived("y1", r)
        for place_x in (opposite,) + beside:
            ours = part.at[r, place_x, y, :, high]
            ours[...] = (wide(ours[...]) + wide(y1_in[r, place_x])).astype(jnp.bfloat16)
        for s in both:
            source = part.at[r, opposite, y, :, high_half[s]]
            send("y2_far", r, s, source, y2_far.at[r, s], along[s])
        for s in both:
            source = part.at[r, beside[s], y, :, high_half[1 - s]]
            send("y2_near", r, s, source, y2_in.at[r, s, :, y_half[1 - s]], along[s])
        arrived("x1_near", r, both)
        arrived("x1_sum", r, both)
        total = wide(part[r, x, 1 - y, :, low])
        for s in both:
            total += wide(x1_in[r, s, 1 - y])
        x2_out[r] = total.astype(jnp.bfloat16)
        send("x2", r, 0, x2_out.at[r], x2_in.at[r], over_y)

    def relay_y2(r):
        arrived("y2_far", r, both)
        for s in both:
            ours = part.at[r, beside[s], y, :, high_half[s]]
            ours[...] = (wide(ours[...]) + wide(y2_far[r, s])).astype(jnp.bfloat16)
            send("y2_sum", r, s, ours, y2_in.at[r, s, :, y_half[s]], along[s])

    def finish(r):
        arrived("x2", r)
        arrived("y2_near", r, both)
        arrived("y2_sum", r, both)
        left = wide(part[r, x, y, :, low]) + wide(x2_in[r])
        right = wide(part[r, x, y, :, high]) + wide(y1_in[r, x])
        for s in both:
            left += wide(x1_in[r, s, y])
            right += wide(y2_in[r, s])
        left = (wide(residual_ref[r, :, low]) + left).astype(jnp.bfloat16)
        right = (wide(residual_ref[r, :, high]) + right).astype(jnp.bfloat16)
        hidden_ref[r, :, low] = left
        hidden_ref[r, :, high] = right
        left, right = wide(left), wide(right)
        squares = jnp.sum(left * left, axis=-1, keepdims=True)
        squares += jnp.sum(right * right, axis=-1, keepdims=True)
        factor = lax.rsqrt(squares / width + EPSILON)
        mine = rows_all.at[r, x, y, core]
        mine[:, low] = (left * factor * gain_ref[:, low]).astype(jnp.bfloat16)
        mine[:, high] = (right * factor * gain_ref[:, high]).astype(jnp.bfloat16)
        for s in both:
            send("h1", r, s, mine.at[:, g_low], mine.at[:, g_low], along[s])
        send("g1", r, 0, mine.at[:, g_high], mine.at[:, g_high], over_y)

    def pass_h1(r):
        arrived("h1", r, both)
        for s in both:
            came = rows_all.at[r, beside[1 - s], y, core, :, g_low_half[s]]
            send("h1_on", r, s, came, came, along[s])

    def spread(r):
        arrived("g1", r)
        column = rows_all.at[r, x, :, core, :, g_high]
        for s in both:
            send("g2", r, s, column, column, along[s])
        arrived("h1_on", r, both)
        row = rows_all.at[r, :, y, core, :, g_low]
        send("h2", r, 0, row, row, over_y)

    def pass_g2(r):
        arrived("g2", r, both)
        for s in both:
            came = rows_all.at[r, beside[1 - s], :, core, :, g_high_half[s]]
            send("g2_on", r, s, came, came, along[s])

    def share(r):
        arrived("h2", r)
        ours = rows_all.at[r, :, :, core, :, g_low]
        send("core", r, 0, ours, ours, sibling)
        arrived("g2_on", r, both)
        ours = rows_all.at[r, :, :, core, :, g_high]
        send("core", r, 1, ours, ours, sibling)

    def next_copy(d, r, source):
        target = (kv1_ref, kv2_ref)[d - 1].at[:, r]
        return describe("next", r, d - 1, source, target, later[d - 1])

    def project_next(r):
        arrived("core", r, both)
        if r == 0:
            loads[2].wait()

        def depth(j, carry):
            span = pl.ds(pl.multiple_of(j * tile, tile), tile)
            rows = rows_all[r, :, :, :, :, span].reshape(16 * SUB, tile)
            for n in range(3):
                acc[n] += jnp.dot(rows, w_qkv[n, span], preferred_element_type=jnp.float32)
            return carry

        acc[...] = jnp.zeros_like(acc)
        lax.fori_loop(0, width // tile, depth, 0)
        for n in range(3):
            qkv_ref[:, r, :, n * 256 : n * 256 + 256] = (
                acc[n].astype(jnp.bfloat16).reshape(16, SUB, 256)
            )
        source = qkv_ref.at[:, r, :, 256:]

        @pl.when(ctx <= 6)
        def _():
            next_copy(1, r, source).start()

        @pl.when(ctx <= 5)
        def _():
            next_copy(2, r, source).start()

    stages = [
        project,
        relay_x1,
        second,
        relay_y2,
        finish,
        pass_h1,
        spread,
        pass_g2,
        share,
        project_next,
    ]
    for step in range(CHUNKS - 1 + len(stages)):
        for r in reversed(range(CHUNKS)):
            if 0 <= step - r < len(stages):
                stages[step - r](r)
    for copy in started:
        copy.wait_send()
    for r in range(CHUNKS):
        source = qkv_ref.at[:, r, :, 256:]

        @pl.when(ctx <= 6)
        def _():
            next_copy(1, r, source).wait_send()

        @pl.when(ctx <= 5)
        def _():
            next_copy(2, r, source).wait_send()

        @pl.when(ctx >= 1)
        def _():
            next_copy(1, r, source).wait_recv()

        @pl.when(ctx >= 2)
        def _():
            next_copy(2, r, source).wait_recv()


def project_and_spread(normed, w_own, w_sib, residual, gain, w_qkv):
    width = w_own.shape[1]
    x_cols = width * 5 // 8
    g_cols = width * 3 // 8
    out_cols = 768
    bf16 = jnp.bfloat16
    any_space = pl.BlockSpec(memory_space=pl.ANY)
    vmem = pl.BlockSpec(memory_space=pltpu.VMEM)
    sem = pltpu.SemaphoreType.DMA
    hidden, qkv, kv1, kv2 = pl.pallas_call(
        functools.partial(mid_kernel, x_cols, g_cols),
        name="project_and_spread",
        out_shape=(
            jax.ShapeDtypeStruct((CHUNKS, SUB, width), bf16),
            jax.ShapeDtypeStruct((16, CHUNKS, SUB, out_cols), bf16),
            jax.ShapeDtypeStruct((16, CHUNKS, SUB, 512), bf16),
            jax.ShapeDtypeStruct((16, CHUNKS, SUB, 512), bf16),
        ),
        in_specs=[vmem, any_space, any_space, vmem, vmem, any_space],
        out_specs=(vmem, vmem, any_space, any_space),
        scratch_shapes=[
            pltpu.VMEM((256, width), bf16),
            pltpu.VMEM((256, width), bf16),
            pltpu.VMEM((3, width, 256), bf16),
            pltpu.VMEM((8, CHUNKS, SUB, 256), bf16),
            pltpu.VMEM((CHUNKS, 4, 2, SUB, width), bf16),
            pltpu.VMEM((CHUNKS, 2, 2, SUB, x_cols // 2), bf16),
            pltpu.VMEM((CHUNKS, 2, 2, SUB, x_cols), bf16),
            pltpu.VMEM((CHUNKS, 4, SUB, width - x_cols), bf16),
            pltpu.VMEM((CHUNKS, SUB, x_cols), bf16),
            pltpu.VMEM((CHUNKS, SUB, x_cols), bf16),
            pltpu.VMEM((CHUNKS, 2, SUB, (width - x_cols) // 2), bf16),
            pltpu.VMEM((CHUNKS, 2, SUB, width - x_cols), bf16),
            pltpu.VMEM((CHUNKS, 4, 2, 2, SUB, width), bf16),
            pltpu.VMEM((3, 16 * SUB, 256), jnp.float32),
            sem((3,)),
            sem((len(KINDS), CHUNKS, 2, 2)),
        ],
        compiler_params=pltpu.CompilerParams(
            collective_id=0, has_side_effects=True, vmem_limit_bytes=63 * 2**20
        ),
    )(
        normed.reshape(8, 2, CHUNKS, SUB, 256),
        w_own,
        w_sib,
        residual.reshape(CHUNKS, SUB, width),
        gain.reshape(1, width),
        w_qkv,
    )
    tokens = 16 * CHUNKS * SUB
    return (
        hidden.reshape(CHUNKS * SUB, width),
        qkv.reshape(tokens, out_cols),
        (kv1.reshape(tokens, 512), kv2.reshape(tokens, 512)),
    )


def on_device(residual, q_win, kv_win, lam_win, gn_gain, w_out_a, norm_gain, w_qkv):
    tokens_here = q_win.shape[0]
    w_sib = lax.ppermute(w_out_a, "head", [(i, i ^ 1) for i in range(lax.axis_size("head"))])
    normed = window_attention(
        q_win.reshape(tokens_here, 256), kv_win.reshape(tokens_here, 512), lam_win, gn_gain
    )
    h_rows, qkv, blocks = project_and_spread(
        normed, w_out_a, w_sib, residual, norm_gain, w_qkv[:, 0].transpose(1, 0, 2)
    )
    part_out, log_out = cycle_attention(qkv, blocks)
    return (
        h_rows,
        part_out.reshape(2, tokens_here, 1, 256),
        log_out.reshape(2, 1, tokens_here),
    )


def solution(mesh):
    in_specs = (
        P(("ctx", "head"), None),
        P("ctx", "head", None),
        P("ctx", "head", None, None),
        P(),
        P(),
        P("head", None),
        P(),
        P(None, "head", None, None),
    )
    out_specs = (P(("ctx", "head"), None), P(None, "ctx", "head", None), P(None, "head", "ctx"))
    return jax.shard_map(
        on_device, mesh=mesh, in_specs=in_specs, out_specs=out_specs, check_vma=False
    )
```

```python
import functools
import math

import jax
import jax.numpy as jnp
from jax import lax
from jax.experimental import pallas as pl
from jax.experimental.pallas import tpu as pltpu
from jax.sharding import PartitionSpec as P

HDIM = 128
WINDOW = 4096
EPSILON = 1e-05
LAMBDA_INIT = 0.8 - 0.6 * math.exp(-3.3)
SCALE = math.log2(math.e) / math.sqrt(HDIM)
LN2 = math.log(2.0)
NEG = -1e30
ONES = 16
ROWS = 256
MESH = pl.DeviceIdType.MESH


def with_ones(values):
    flipped = values.astype(jnp.float32).T.astype(jnp.bfloat16)
    return jnp.concatenate([flipped, jnp.ones((ONES, values.shape[0]), jnp.bfloat16)], axis=0)


def scaled_queries(picked):
    return (picked.astype(jnp.float32) * SCALE).astype(jnp.bfloat16)


def online_step(queries, keys_of, values_up, m_ref, acc_ref, mask):
    for j in range(2):
        scores = lax.dot_general(
            keys_of(j),
            queries[:, j * HDIM : (j + 1) * HDIM],
            (((1,), (1,)), ((), ())),
            preferred_element_type=jnp.float32,
        )
        if mask is not None:
            scores = jnp.where(mask, scores, NEG)
        before = m_ref[j]
        after = jnp.maximum(before, jnp.max(scores, axis=0, keepdims=True))
        weights = jnp.exp2(scores - after).astype(jnp.bfloat16)
        acc_ref[j] = acc_ref[j] * jnp.exp2(before - after) + jnp.dot(
            values_up, weights, preferred_element_type=jnp.float32
        )
        m_ref[j] = after


PIECES = 8


def window_kernel(
    lam_ref, q_ref, gain_ref, kv_ref, out_ref, kv_in, q_scaled, vt_ref, m_ref, acc_ref, up_sem, ring_sem, on_sem
):
    ctx, head = lax.axis_index("ctx"), lax.axis_index("head")
    ring, z = ctx // 4, lax.rem(ctx, 4)
    tokens = kv_ref.shape[0]
    piece = tokens // PIECES
    over = ((1 - ring) * 4 + z, head)

    def along(e):
        return (ring * 4 + lax.rem(z + e, 4), head)

    def copy_up(n):
        rows = pl.ds(n * piece, piece)
        return pltpu.make_async_remote_copy(
            src_ref=kv_ref.at[rows],
            dst_ref=kv_in.at[3, rows],
            send_sem=up_sem.at[n, 0],
            recv_sem=up_sem.at[n, 1],
            device_id=over,
            device_id_type=MESH,
        )

    def copy_along(e, n, source):
        rows = pl.ds(n * piece, piece)
        return pltpu.make_async_remote_copy(
            src_ref=source.at[rows],
            dst_ref=kv_in.at[e - 1, rows],
            send_sem=ring_sem.at[e - 1, n, 0],
            recv_sem=ring_sem.at[e - 1, n, 1],
            device_id=along(e),
            device_id_type=MESH,
        )

    barrier = pltpu.get_barrier_semaphore()
    for peer in (along(1), along(2), along(3), over):
        pl.semaphore_signal(barrier, inc=1, device_id=peer, device_id_type=MESH)
    pl.semaphore_wait(barrier, 4)

    @pl.when(ring == 0)
    def _():
        for n in range(PIECES):
            copy_up(n).start()

    def copy_on(side, n):
        rows = pl.ds(n * piece, piece)
        return pltpu.make_async_remote_copy(
            src_ref=kv_in.at[2 * side, rows],
            dst_ref=kv_in.at[1, rows],
            send_sem=on_sem.at[side, n],
            recv_sem=ring_sem.at[1, n, 1],
            device_id=along(1 + 2 * side),
            device_id_type=MESH,
        )

    def passes_on(side, n):
        if side == 0:
            return (z <= 2) & (ctx >= 1) if n % 2 == 0 else (z == 2)
        return (ctx >= 3) & (z >= 1) if n % 2 == 1 else (ring == 1) & (z == 1)

    for e in (1, 3):

        @pl.when(z + e <= 3)
        def _():
            for n in range(PIECES):
                copy_along(e, n, kv_ref).start()

    q_scaled[...] = scaled_queries(q_ref[...])
    m_ref[...] = jnp.full_like(m_ref, NEG)
    acc_ref[...] = jnp.zeros_like(acc_ref)

    def all_queries(keys, edge):
        vt_ref[...] = with_ones(keys[:, 256:])

        def some(i, carry):
            rows = pl.ds(pl.multiple_of(i * ROWS, ROWS), ROWS)
            mask = None
            if edge is not None:
                key_pos = lax.broadcasted_iota(jnp.int32, (tokens, ROWS), 0)
                row_pos = lax.broadcasted_iota(jnp.int32, (tokens, ROWS), 1) + i * ROWS
                mask = key_pos <= row_pos if edge == "own" else key_pos > row_pos
            online_step(
                q_scaled[rows, :],
                lambda j: keys[:, j * HDIM : (j + 1) * HDIM],
                vt_ref[...],
                m_ref.at[i],
                acc_ref.at[i],
                mask,
            )
            return carry

        lax.fori_loop(0, tokens // ROWS, some, 0)

    all_queries(kv_ref, "own")

    @pl.when(ring == 1)
    def _():
        for n in range(PIECES):
            copy_up(n).wait_recv()
            for e in (3, 1):

                @pl.when(z + e >= 4)
                def _():
                    copy_along(e, n, kv_in.at[3]).start()

    for side in (0, 1):

        @pl.when(ctx >= 1 + 2 * side)
        def _():
            for n in range(PIECES):
                copy_along(1 + 2 * side, n, kv_ref).wait_recv()

        for n in range(PIECES):

            @pl.when(passes_on(side, n))
            def _():
                copy_on(side, n).start()

    @pl.when(ring == 1)
    def _():
        all_queries(kv_in.at[3], "far")

    for e in (1, 3, 2):

        @pl.when(ctx >= e)
        def _():
            if e == 2:
                for n in range(PIECES):
                    copy_along(2, n, kv_ref).wait_recv()
            all_queries(kv_in.at[e - 1], None)

    pairs = lam_ref[...]
    lam = (
        jnp.exp(jnp.sum(pairs[0:1] * pairs[1:2], axis=1, keepdims=True))
        - jnp.exp(jnp.sum(pairs[2:3] * pairs[3:4], axis=1, keepdims=True))
        + LAMBDA_INIT
    )

    def finish(i, carry):
        one = acc_ref[i, 0, :256] / acc_ref[i, 0, 256:257]
        two = acc_ref[i, 1, :256] / acc_ref[i, 1, 256:257]
        attended = one - lam * two
        factor = lax.rsqrt(jnp.mean(attended * attended, axis=0, keepdims=True) + EPSILON)
        normed = (attended * factor).T * (gain_ref[...] * (1.0 - LAMBDA_INIT))
        out_ref[pl.ds(pl.multiple_of(i * ROWS, ROWS), ROWS), :] = normed.astype(jnp.bfloat16)
        return carry

    lax.fori_loop(0, tokens // ROWS, finish, 0)

    @pl.when(ring == 0)
    def _():
        for n in range(PIECES):
            copy_up(n).wait_send()

    for e in (1, 3):

        @pl.when((ring == 1) | (z + e <= 3))
        def _():
            for n in range(PIECES):
                copy_along(e, n, kv_ref).wait_send()

    for side in (0, 1):
        for n in range(PIECES):

            @pl.when(passes_on(side, n))
            def _():
                copy_on(side, n).wait_send()


def window_attention(queries, keys_values, lam_win, gain):
    tokens = queries.shape[0]
    vmem = pl.BlockSpec(memory_space=pltpu.VMEM)
    return pl.pallas_call(
        window_kernel,
        name="window",
        out_shape=jax.ShapeDtypeStruct((tokens, 256), jnp.bfloat16),
        in_specs=[vmem] * 4,
        out_specs=vmem,
        scratch_shapes=[
            pltpu.VMEM((4, tokens, 512), jnp.bfloat16),
            pltpu.VMEM((tokens, 256), jnp.bfloat16),
            pltpu.VMEM((256 + ONES, tokens), jnp.bfloat16),
            pltpu.VMEM((tokens // ROWS, 2, 1, ROWS), jnp.float32),
            pltpu.VMEM((tokens // ROWS, 2, 256 + ONES, ROWS), jnp.float32),
            pltpu.SemaphoreType.DMA((PIECES, 2)),
            pltpu.SemaphoreType.DMA((3, PIECES, 2)),
            pltpu.SemaphoreType.DMA((2, PIECES)),
        ],
        compiler_params=pltpu.CompilerParams(
            collective_id=1, has_side_effects=True, vmem_limit_bytes=40 * 2**20
        ),
    )(lam_win, queries, gain.reshape(1, 256), keys_values)


CHUNKS = 4
SUB = 16


def place():
    head = lax.axis_index("head")
    return lax.axis_index("ctx"), head // 4, (head // 2) % 2, head % 2


KINDS = (
    "normed",
    "y1",
    "x1_far",
    "x1_near",
    "x1_sum",
    "x2",
    "y2_far",
    "y2_near",
    "y2_sum",
    "h1",
    "h1_on",
    "g1",
    "h2",
    "g2",
    "g2_on",
    "core",
    "next",
)


def mid_kernel(
    x_cols,
    g_cols,
    normed_ref,
    w_own_hbm,
    w_sib_hbm,
    residual_ref,
    gain_ref,
    w_qkv_hbm,
    hidden_ref,
    out_ref,
    log_ref,
    qkv_ref,
    kv1_ref,
    kv2_ref,
    w_qkv,
    n_sib,
    part,
    x1_far,
    x1_in,
    y1_in,
    x2_out,
    x2_in,
    y2_far,
    y2_in,
    rows_all,
    load_sem,
    sems,
):
    ctx, x, y, core = place()
    width = w_own_hbm.shape[1]
    y_cols = width - x_cols
    low, high = pl.ds(0, x_cols), pl.ds(x_cols, y_cols)
    low_half = (pl.ds(0, x_cols // 2), pl.ds(x_cols // 2, x_cols // 2))
    high_half = (pl.ds(x_cols, y_cols // 2), pl.ds(x_cols + y_cols // 2, y_cols // 2))
    g_low, g_high = pl.ds(0, g_cols), pl.ds(g_cols, width - g_cols)
    g_low_half = (pl.ds(0, g_cols // 2), pl.ds(g_cols // 2, g_cols // 2))
    g_high_half = tuple(
        pl.ds(g_cols + s * ((width - g_cols) // 2), (width - g_cols) // 2) for s in (0, 1)
    )
    y_half = (pl.ds(0, y_cols // 2), pl.ds(y_cols // 2, y_cols // 2))
    head = lax.axis_index("head")
    beside = (lax.rem(x + 1, 4), lax.rem(x + 3, 4))
    opposite = lax.rem(x + 2, 4)
    along = [(ctx, place_x * 4 + y * 2 + core) for place_x in beside]
    over_y = (ctx, x * 4 + (1 - y) * 2 + core)
    sibling = (ctx, x * 4 + y * 2 + 1 - core)
    blocks = lax.axis_size("ctx")
    others = [(lax.rem(ctx + d, blocks), head) for d in range(1, 8)]

    late_load = pltpu.make_async_copy(w_qkv_hbm, w_qkv, load_sem.at[2])
    late_load.start()

    started = []
    pending = {}

    def describe(kind, r, side, source, target, device):
        kind = KINDS.index(kind)
        return pltpu.make_async_remote_copy(
            src_ref=source,
            dst_ref=target,
            send_sem=sems.at[kind, r, side, 0],
            recv_sem=sems.at[kind, r, side, 1],
            device_id=device,
            device_id_type=MESH,
        )

    def send(kind, r, side, ends):
        def copy():
            return describe(kind, r, side, *ends())

        copy().start()
        started.append(copy)
        pending[kind, r, side] = copy

    every = slice(None)

    def spread_rows(r, kind, side, index, device):
        send(kind, r, side, lambda: (rows_all.at[index()], rows_all.at[index()], device))

    def arrived(kind, r, sides=(0,)):
        for side in sides:
            pending[kind, r, side]().wait_recv()

    def wide(value):
        return value.astype(jnp.float32)

    both = (0, 1)
    tile = min(1024, width)

    def project(r, w_own, w_sib):
        own_rows = normed_ref[:, core, r].reshape(8 * SUB, 256)
        sib_rows = n_sib[:, r].reshape(8 * SUB, 256)

        def columns(j, carry):
            span = pl.ds(pl.multiple_of(j * tile, tile), tile)
            value = jnp.dot(own_rows, w_own[:, span], preferred_element_type=jnp.float32)
            value += jnp.dot(sib_rows, w_sib[:, span], preferred_element_type=jnp.float32)
            part[r, :, :, :, span] = value.astype(jnp.bfloat16).reshape(4, 2, SUB, tile)
            return carry

        lax.fori_loop(0, width // tile, columns, 0)
        for s in both:

            def far(s=s):
                return part.at[r, opposite, :, :, low_half[s]], x1_far.at[r, s], along[s]

            send("x1_far", r, s, far)
        send("y1", r, 0, lambda: (part.at[r, :, 1 - y, :, high], y1_in.at[r], over_y))
        for s in both:

            def near(s=s):
                half = low_half[1 - s]
                return part.at[r, beside[s], :, :, half], x1_in.at[r, s, :, :, half], along[s]

            send("x1_near", r, s, near)

    def relay_x1(r):
        arrived("x1_far", r, both)
        for s in both:
            ours = part.at[r, beside[s], :, :, low_half[s]]
            ours[...] = (wide(ours[...]) + wide(x1_far[r, s])).astype(jnp.bfloat16)

            def summed(s=s):
                half = low_half[s]
                return part.at[r, beside[s], :, :, half], x1_in.at[r, s, :, :, half], along[s]

            send("x1_sum", r, s, summed)

    def second(r):
        arrived("y1", r)
        for place_x in (opposite,) + beside:
            ours = part.at[r, place_x, y, :, high]
            ours[...] = (wide(ours[...]) + wide(y1_in[r, place_x])).astype(jnp.bfloat16)
        for s in both:

            def far(s=s):
                return part.at[r, opposite, y, :, high_half[s]], y2_far.at[r, s], along[s]

            send("y2_far", r, s, far)
        for s in both:

            def near(s=s):
                source = part.at[r, beside[s], y, :, high_half[1 - s]]
                return source, y2_in.at[r, s, :, y_half[1 - s]], along[s]

            send("y2_near", r, s, near)
        arrived("x1_near", r, both)
        arrived("x1_sum", r, both)
        total = wide(part[r, x, 1 - y, :, low])
        for s in both:
            total += wide(x1_in[r, s, 1 - y])
        x2_out[r] = total.astype(jnp.bfloat16)
        send("x2", r, 0, lambda: (x2_out.at[r], x2_in.at[r], over_y))

    def relay_y2(r):
        arrived("y2_far", r, both)
        for s in both:
            ours = part.at[r, beside[s], y, :, high_half[s]]
            ours[...] = (wide(ours[...]) + wide(y2_far[r, s])).astype(jnp.bfloat16)

            def summed(s=s):
                source = part.at[r, beside[s], y, :, high_half[s]]
                return source, y2_in.at[r, s, :, y_half[s]], along[s]

            send("y2_sum", r, s, summed)

    def finish(r):
        arrived("x2", r)
        arrived("y2_near", r, both)
        arrived("y2_sum", r, both)
        left = wide(part[r, x, y, :, low]) + wide(x2_in[r])
        right = wide(part[r, x, y, :, high]) + wide(y1_in[r, x])
        for s in both:
            left += wide(x1_in[r, s, y])
            right += wide(y2_in[r, s])
        left = (wide(residual_ref[r, :, low]) + left).astype(jnp.bfloat16)
        right = (wide(residual_ref[r, :, high]) + right).astype(jnp.bfloat16)
        hidden_ref[r, :, low] = left
        hidden_ref[r, :, high] = right
        left, right = wide(left), wide(right)
        squares = jnp.sum(left * left, axis=-1, keepdims=True)
        squares += jnp.sum(right * right, axis=-1, keepdims=True)
        factor = lax.rsqrt(squares / width + EPSILON)
        mine = rows_all.at[r, x, y, core]
        mine[:, low] = (left * factor * gain_ref[:, low]).astype(jnp.bfloat16)
        mine[:, high] = (right * factor * gain_ref[:, high]).astype(jnp.bfloat16)

        for s in both:
            spread_rows(r, "h1", s, lambda: (r, x, y, core, every, g_low), along[s])
        spread_rows(r, "g1", 0, lambda: (r, x, y, core, every, g_high), over_y)

    def pass_h1(r):
        arrived("h1", r, both)
        for s in both:
            spread_rows(
                r,
                "h1_on",
                s,
                lambda s=s: (r, beside[1 - s], y, core, every, g_low_half[s]),
                along[s],
            )

    def spread(r):
        arrived("g1", r)
        for s in both:
            spread_rows(r, "g2", s, lambda: (r, x, every, core, every, g_high), along[s])
        arrived("h1_on", r, both)
        spread_rows(r, "h2", 0, lambda: (r, every, y, core, every, g_low), over_y)

    def pass_g2(r):
        arrived("g2", r, both)
        for s in both:
            spread_rows(
                r,
                "g2_on",
                s,
                lambda s=s: (r, beside[1 - s], every, core, every, g_high_half[s]),
                along[s],
            )

    def share(r):
        arrived("h2", r)
        spread_rows(r, "core", 0, lambda: (r, every, every, core, every, g_low), sibling)
        arrived("g2_on", r, both)
        spread_rows(r, "core", 1, lambda: (r, every, every, core, every, g_high), sibling)

    def next_copy(d, r, target, forward=False):
        landing = (kv1_ref, kv2_ref)[d - 1].at[:, r]
        kind = KINDS.index("next")
        return pltpu.make_async_remote_copy(
            src_ref=landing if forward else qkv_ref.at[:, r, :, 256:],
            dst_ref=landing,
            send_sem=sems.at[kind, r, 2 if forward else d - 1, 0],
            recv_sem=sems.at[kind, r, d - 1, 1],
            device_id=(target, head),
            device_id_type=MESH,
        )

    def project_next(r, acc):
        arrived("core", r, both)
        if r == 0:
            late_load.wait()

        def depth(j, carry):
            span = pl.ds(pl.multiple_of(j * tile, tile), tile)
            rows = rows_all[r, :, :, :, :, span].reshape(16 * SUB, tile)
            for n in range(3):
                acc[n] += jnp.dot(rows, w_qkv[n, span], preferred_element_type=jnp.float32)
            return carry

        acc[...] = jnp.zeros_like(acc)
        lax.fori_loop(0, width // tile, depth, 0)
        for n in range(3):
            qkv_ref[:, r, :, n * 256 : n * 256 + 256] = (
                acc[n].astype(jnp.bfloat16).reshape(16, SUB, 256)
            )
        for d, target, sends in routes:

            @pl.when(sends)
            def _():
                next_copy(d, r, target).start()

    routes = [
        (1, lax.rem(ctx + 1, blocks), (ctx <= 6) & (ctx != 3)),
        (2, lax.rem(ctx + 2, blocks), (ctx <= 5) & (ctx != 3)),
        (1, lax.rem(ctx + 5, blocks), ctx == 3),
        (2, lax.rem(ctx + 6, blocks), ctx == 3),
    ]
    stages = [
        project,
        relay_x1,
        second,
        relay_y2,
        finish,
        pass_h1,
        spread,
        pass_g2,
        share,
        project_next,
    ]

    def steps(first, last, *weights):
        for step in range(first, last):
            for r in reversed(range(CHUNKS)):
                if 0 <= step - r < len(stages):
                    stages[step - r](r, *(weights if step - r in (0, len(stages) - 1) else ()))

    def first_steps(w_own, w_sib):
        loads = [
            pltpu.make_async_copy(source, target, load_sem.at[n])
            for n, (source, target) in enumerate([(w_own_hbm, w_own), (w_sib_hbm, w_sib)])
        ]
        for load in loads:
            load.start()
        barrier = pltpu.get_barrier_semaphore()
        for peer in along + [over_y, sibling] + others:
            pl.semaphore_signal(barrier, inc=1, device_id=peer, device_id_type=MESH)
        pl.semaphore_wait(barrier, 11)
        send("normed", 0, 0, lambda: (normed_ref.at[:, 1 - core], n_sib, sibling))
        arrived("normed", 0)
        for load in loads:
            load.wait()
        steps(0, CHUNKS, w_own, w_sib)

    def last_steps(acc):
        steps(CHUNKS, CHUNKS - 1 + len(stages), acc)

    pl.run_scoped(
        first_steps, pltpu.VMEM((256, width), jnp.bfloat16), pltpu.VMEM((256, width), jnp.bfloat16)
    )
    pl.run_scoped(last_steps, pltpu.VMEM((3, 16 * SUB, 256), jnp.float32))

    for d in (1, 2):

        @pl.when(ctx == d - 1)
        def _():
            for r in range(CHUNKS):
                next_copy(d, r, 0).wait_recv()
                next_copy(d, r, lax.rem(ctx + 4, blocks), True).start()

    tokens = 16 * CHUNKS * SUB
    groups = tokens // ROWS
    heads = 16 // groups

    def attend(vt_ref, m_ref, acc_ref):
        m_ref[...] = jnp.full_like(m_ref, NEG)
        acc_ref[...] = jnp.zeros_like(acc_ref)

        def block(kv, own):
            def columns(start, size):
                return kv[:, :, :, start : start + size].reshape(tokens, size)

            vt_ref[...] = with_ones(columns(256, 256))

            def some(i, carry):
                queries = qkv_ref[pl.ds(i * heads, heads), :, :, :256].reshape(ROWS, 256)
                mask = None
                if own:
                    key_pos = lax.broadcasted_iota(jnp.int32, (tokens, ROWS), 0)
                    row_pos = lax.broadcasted_iota(jnp.int32, (tokens, ROWS), 1) + i * ROWS
                    mask = key_pos <= row_pos
                online_step(
                    scaled_queries(queries),
                    lambda j: columns(j * HDIM, HDIM),
                    vt_ref[...],
                    m_ref.at[i],
                    acc_ref.at[i],
                    mask,
                )
                return carry

            lax.fori_loop(0, groups, some, 0)

        block(qkv_ref.at[:, :, :, 256:], True)
        for d, landing in ((1, kv1_ref), (2, kv2_ref)):

            @pl.when(ctx >= d)
            def _():
                for r in range(CHUNKS):
                    next_copy(d, r, 0).wait_recv()
                block(landing, False)

        for i in range(groups):
            for j in range(2):
                total = acc_ref[i, j, 256:257]
                value = (acc_ref[i, j, :256] / total).T
                for half in range(2):
                    out_ref[j, pl.ds(i * 2 * ROWS + half, ROWS, stride=2), :] = value[
                        :, half * 128 : half * 128 + 128
                    ]
                log_ref[j : j + 1, i * ROWS : (i + 1) * ROWS] = (m_ref[i, j] + jnp.log2(total)) * LN2

    pl.run_scoped(
        attend,
        pltpu.VMEM((256 + ONES, tokens), jnp.bfloat16),
        pltpu.VMEM((groups, 2, 1, ROWS), jnp.float32),
        pltpu.VMEM((groups, 2, 256 + ONES, ROWS), jnp.float32),
    )
    for copy in started:
        copy().wait_send()
    for r in range(CHUNKS):
        for d, target, sends in routes:

            @pl.when(sends)
            def _():
                next_copy(d, r, target).wait_send()

        for d in (1, 2):

            @pl.when(ctx == d - 1)
            def _():
                next_copy(d, r, 0, True).wait_send()


def project_and_spread(normed, w_own, w_sib, residual, gain, w_qkv):
    width = w_own.shape[1]
    x_cols = width * 5 // 8
    g_cols = width * 3 // 8
    tokens = 16 * CHUNKS * SUB
    bf16 = jnp.bfloat16
    any_space = pl.BlockSpec(memory_space=pl.ANY)
    vmem = pl.BlockSpec(memory_space=pltpu.VMEM)
    sem = pltpu.SemaphoreType.DMA
    hidden, part_out, log_sums = pl.pallas_call(
        functools.partial(mid_kernel, x_cols, g_cols),
        name="project_and_spread",
        out_shape=(
            jax.ShapeDtypeStruct((CHUNKS, SUB, width), bf16),
            jax.ShapeDtypeStruct((2, 2 * tokens, 128), jnp.float32),
            jax.ShapeDtypeStruct((2, tokens), jnp.float32),
        ),
        in_specs=[vmem, any_space, any_space, vmem, vmem, any_space],
        out_specs=(vmem, vmem, vmem),
        scratch_shapes=[
            pltpu.VMEM((16, CHUNKS, SUB, 768), bf16),
            pltpu.VMEM((16, CHUNKS, SUB, 512), bf16),
            pltpu.VMEM((16, CHUNKS, SUB, 512), bf16),
            pltpu.VMEM((3, width, 256), bf16),
            pltpu.VMEM((8, CHUNKS, SUB, 256), bf16),
            pltpu.VMEM((CHUNKS, 4, 2, SUB, width), bf16),
            pltpu.VMEM((CHUNKS, 2, 2, SUB, x_cols // 2), bf16),
            pltpu.VMEM((CHUNKS, 2, 2, SUB, x_cols), bf16),
            pltpu.VMEM((CHUNKS, 4, SUB, width - x_cols), bf16),
            pltpu.VMEM((CHUNKS, SUB, x_cols), bf16),
            pltpu.VMEM((CHUNKS, SUB, x_cols), bf16),
            pltpu.VMEM((CHUNKS, 2, SUB, (width - x_cols) // 2), bf16),
            pltpu.VMEM((CHUNKS, 2, SUB, width - x_cols), bf16),
            pltpu.VMEM((CHUNKS, 4, 2, 2, SUB, width), bf16),
            sem((3,)),
            sem((len(KINDS), CHUNKS, 3, 2)),
        ],
        compiler_params=pltpu.CompilerParams(
            collective_id=0, has_side_effects=True, vmem_limit_bytes=63 * 2**20
        ),
    )(
        normed.reshape(8, 2, CHUNKS, SUB, 256),
        w_own,
        w_sib,
        residual.reshape(CHUNKS, SUB, width),
        gain.reshape(1, width),
        w_qkv,
    )
    return hidden.reshape(CHUNKS * SUB, width), part_out, log_sums


def on_device(residual, q_win, kv_win, lam_win, gn_gain, w_out_a, norm_gain, w_qkv):
    tokens_here = q_win.shape[0]
    w_sib = lax.ppermute(w_out_a, "head", [(i, i ^ 1) for i in range(lax.axis_size("head"))])
    normed = window_attention(
        q_win.reshape(tokens_here, 256), kv_win.reshape(tokens_here, 512), lam_win, gn_gain
    )
    h_rows, part_out, log_out = project_and_spread(
        normed, w_out_a, w_sib, residual, norm_gain, w_qkv[:, 0].transpose(1, 0, 2)
    )
    return (
        h_rows,
        part_out.reshape(2, tokens_here, 1, 256),
        log_out.reshape(2, 1, tokens_here),
    )


def solution(mesh):
    in_specs = (
        P(("ctx", "head"), None),
        P("ctx", "head", None),
        P("ctx", "head", None, None),
        P(),
        P(),
        P("head", None),
        P(),
        P(None, "head", None, None),
    )
    out_specs = (P(("ctx", "head"), None), P(None, "ctx", "head", None), P(None, "head", "ctx"))
    return jax.shard_map(
        on_device, mesh=mesh, in_specs=in_specs, out_specs=out_specs, check_vma=False
    )
```

```python
import functools
import math

import jax
import jax.numpy as jnp
from jax import lax
from jax.experimental import pallas as pl
from jax.experimental.pallas import tpu as pltpu
from jax.sharding import PartitionSpec as P

HDIM = 128
WINDOW = 4096
EPSILON = 1e-05
LAMBDA_INIT = 0.8 - 0.6 * math.exp(-3.3)
SCALE = math.log2(math.e) / math.sqrt(HDIM)
LN2 = math.log(2.0)
NEG = -1e30
ONES = 16
ROWS = 256
MESH = pl.DeviceIdType.MESH


def with_ones(values):
    flipped = values.astype(jnp.float32).T.astype(jnp.bfloat16)
    return jnp.concatenate([flipped, jnp.ones((ONES, values.shape[0]), jnp.bfloat16)], axis=0)


def scaled_queries(picked):
    return (picked.astype(jnp.float32) * SCALE).astype(jnp.bfloat16)


def online_step(queries, keys_of, values_up, m_ref, acc_ref, mask):
    for j in range(2):
        scores = lax.dot_general(
            keys_of(j),
            queries[:, j * HDIM : (j + 1) * HDIM],
            (((1,), (1,)), ((), ())),
            preferred_element_type=jnp.float32,
        )
        if mask is not None:
            scores = jnp.where(mask, scores, NEG)
        before = m_ref[j]
        after = jnp.maximum(before, jnp.max(scores, axis=0, keepdims=True))
        weights = jnp.exp2(scores - after).astype(jnp.bfloat16)
        acc_ref[j] = acc_ref[j] * jnp.exp2(before - after) + jnp.dot(
            values_up, weights, preferred_element_type=jnp.float32
        )
        m_ref[j] = after


PIECES = 8


def window_kernel(
    lam_ref, q_ref, gain_ref, kv_ref, out_ref, kv_in, q_scaled, vt_ref, m_ref, acc_ref, up_sem, ring_sem, on_sem
):
    ctx, head = lax.axis_index("ctx"), lax.axis_index("head")
    ring, z = ctx // 4, lax.rem(ctx, 4)
    tokens = kv_ref.shape[0]
    piece = tokens // PIECES
    over = ((1 - ring) * 4 + z, head)

    def along(e):
        return (ring * 4 + lax.rem(z + e, 4), head)

    def copy_up(n):
        rows = pl.ds(n * piece, piece)
        return pltpu.make_async_remote_copy(
            src_ref=kv_ref.at[rows],
            dst_ref=kv_in.at[3, rows],
            send_sem=up_sem.at[n, 0],
            recv_sem=up_sem.at[n, 1],
            device_id=over,
            device_id_type=MESH,
        )

    def copy_along(e, n, source):
        rows = pl.ds(n * piece, piece)
        return pltpu.make_async_remote_copy(
            src_ref=source.at[rows],
            dst_ref=kv_in.at[e - 1, rows],
            send_sem=ring_sem.at[e - 1, n, 0],
            recv_sem=ring_sem.at[e - 1, n, 1],
            device_id=along(e),
            device_id_type=MESH,
        )

    barrier = pltpu.get_barrier_semaphore()
    for peer in (along(1), along(2), along(3), over):
        pl.semaphore_signal(barrier, inc=1, device_id=peer, device_id_type=MESH)
    pl.semaphore_wait(barrier, 4)

    @pl.when(ring == 0)
    def _():
        for n in range(PIECES):
            copy_up(n).start()

    def copy_on(side, n):
        rows = pl.ds(n * piece, piece)
        return pltpu.make_async_remote_copy(
            src_ref=kv_in.at[2 * side, rows],
            dst_ref=kv_in.at[1, rows],
            send_sem=on_sem.at[side, n],
            recv_sem=ring_sem.at[1, n, 1],
            device_id=along(1 + 2 * side),
            device_id_type=MESH,
        )

    def passes_on(side, n):
        if side == 0:
            return (z <= 2) & (ctx >= 1) if n % 2 == 0 else (z == 2)
        return (ctx >= 3) & (z >= 1) if n % 2 == 1 else (ring == 1) & (z == 1)

    for e in (1, 3):

        @pl.when(z + e <= 3)
        def _():
            for n in range(PIECES):
                copy_along(e, n, kv_ref).start()

    q_scaled[...] = scaled_queries(q_ref[...])
    m_ref[...] = jnp.full_like(m_ref, NEG)
    acc_ref[...] = jnp.zeros_like(acc_ref)

    def all_queries(keys, edge):
        vt_ref[...] = with_ones(keys[:, 256:])

        def some(i, carry):
            rows = pl.ds(pl.multiple_of(i * ROWS, ROWS), ROWS)
            mask = None
            if edge is not None:
                key_pos = lax.broadcasted_iota(jnp.int32, (tokens, ROWS), 0)
                row_pos = lax.broadcasted_iota(jnp.int32, (tokens, ROWS), 1) + i * ROWS
                mask = key_pos <= row_pos if edge == "own" else key_pos > row_pos
            online_step(
                q_scaled[rows, :],
                lambda j: keys[:, j * HDIM : (j + 1) * HDIM],
                vt_ref[...],
                m_ref.at[i],
                acc_ref.at[i],
                mask,
            )
            return carry

        lax.fori_loop(0, tokens // ROWS, some, 0)

    all_queries(kv_ref, "own")

    @pl.when(ring == 1)
    def _():
        for n in range(PIECES):
            copy_up(n).wait_recv()
            for e in (3, 1):

                @pl.when(z + e >= 4)
                def _():
                    copy_along(e, n, kv_in.at[3]).start()

    for side in (0, 1):

        @pl.when(ctx >= 1 + 2 * side)
        def _():
            for n in range(PIECES):
                copy_along(1 + 2 * side, n, kv_ref).wait_recv()

        for n in range(PIECES):

            @pl.when(passes_on(side, n))
            def _():
                copy_on(side, n).start()

    @pl.when(ring == 1)
    def _():
        all_queries(kv_in.at[3], "far")

    for e in (1, 3, 2):

        @pl.when(ctx >= e)
        def _():
            if e == 2:
                for n in range(PIECES):
                    copy_along(2, n, kv_ref).wait_recv()
            all_queries(kv_in.at[e - 1], None)

    pairs = lam_ref[...]
    lam = (
        jnp.exp(jnp.sum(pairs[0:1] * pairs[1:2], axis=1, keepdims=True))
        - jnp.exp(jnp.sum(pairs[2:3] * pairs[3:4], axis=1, keepdims=True))
        + LAMBDA_INIT
    )

    def finish(i, carry):
        one = acc_ref[i, 0, :256] / acc_ref[i, 0, 256:257]
        two = acc_ref[i, 1, :256] / acc_ref[i, 1, 256:257]
        attended = one - lam * two
        factor = lax.rsqrt(jnp.mean(attended * attended, axis=0, keepdims=True) + EPSILON)
        normed = (attended * factor).T * (gain_ref[...] * (1.0 - LAMBDA_INIT))
        out_ref[pl.ds(pl.multiple_of(i * ROWS, ROWS), ROWS), :] = normed.astype(jnp.bfloat16)
        return carry

    lax.fori_loop(0, tokens // ROWS, finish, 0)

    @pl.when(ring == 0)
    def _():
        for n in range(PIECES):
            copy_up(n).wait_send()

    for e in (1, 3):

        @pl.when((ring == 1) | (z + e <= 3))
        def _():
            for n in range(PIECES):
                copy_along(e, n, kv_ref).wait_send()

    for side in (0, 1):
        for n in range(PIECES):

            @pl.when(passes_on(side, n))
            def _():
                copy_on(side, n).wait_send()


def window_attention(queries, keys_values, lam_win, gain):
    tokens = queries.shape[0]
    vmem = pl.BlockSpec(memory_space=pltpu.VMEM)
    return pl.pallas_call(
        window_kernel,
        name="window",
        out_shape=jax.ShapeDtypeStruct((tokens, 256), jnp.bfloat16),
        in_specs=[vmem] * 4,
        out_specs=vmem,
        scratch_shapes=[
            pltpu.VMEM((4, tokens, 512), jnp.bfloat16),
            pltpu.VMEM((tokens, 256), jnp.bfloat16),
            pltpu.VMEM((256 + ONES, tokens), jnp.bfloat16),
            pltpu.VMEM((tokens // ROWS, 2, 1, ROWS), jnp.float32),
            pltpu.VMEM((tokens // ROWS, 2, 256 + ONES, ROWS), jnp.float32),
            pltpu.SemaphoreType.DMA((PIECES, 2)),
            pltpu.SemaphoreType.DMA((3, PIECES, 2)),
            pltpu.SemaphoreType.DMA((2, PIECES)),
        ],
        compiler_params=pltpu.CompilerParams(
            collective_id=1, has_side_effects=True, vmem_limit_bytes=62 * 2**20
        ),
    )(lam_win, queries, gain.reshape(1, 256), keys_values)


CHUNKS = 4
SUB = 16


def place():
    head = lax.axis_index("head")
    return lax.axis_index("ctx"), head // 4, (head // 2) % 2, head % 2


KINDS = (
    "normed",
    "y1",
    "x1_far",
    "x1_near",
    "x1_sum",
    "x2",
    "y2_far",
    "y2_near",
    "y2_sum",
    "h1",
    "h1_on",
    "g1",
    "h2",
    "g2",
    "g2_on",
    "core",
    "next",
)


def mid_kernel(
    x_cols,
    g_cols,
    normed_ref,
    w_own_hbm,
    w_sib_hbm,
    residual_ref,
    gain_ref,
    w_qkv_hbm,
    hidden_ref,
    acc_ref,
    m_ref,
    qkv_ref,
    kv1_ref,
    kv2_ref,
    w_qkv,
    n_sib,
    part,
    x1_far,
    x1_in,
    y1_in,
    x2_out,
    x2_in,
    y2_far,
    y2_in,
    rows_all,
    load_sem,
    sems,
):
    ctx, x, y, core = place()
    width = w_own_hbm.shape[1]
    y_cols = width - x_cols
    low, high = pl.ds(0, x_cols), pl.ds(x_cols, y_cols)
    low_half = (pl.ds(0, x_cols // 2), pl.ds(x_cols // 2, x_cols // 2))
    high_half = (pl.ds(x_cols, y_cols // 2), pl.ds(x_cols + y_cols // 2, y_cols // 2))
    g_low, g_high = pl.ds(0, g_cols), pl.ds(g_cols, width - g_cols)
    g_low_half = (pl.ds(0, g_cols // 2), pl.ds(g_cols // 2, g_cols // 2))
    g_high_half = tuple(
        pl.ds(g_cols + s * ((width - g_cols) // 2), (width - g_cols) // 2) for s in (0, 1)
    )
    y_half = (pl.ds(0, y_cols // 2), pl.ds(y_cols // 2, y_cols // 2))
    head = lax.axis_index("head")
    beside = (lax.rem(x + 1, 4), lax.rem(x + 3, 4))
    opposite = lax.rem(x + 2, 4)
    along = [(ctx, place_x * 4 + y * 2 + core) for place_x in beside]
    over_y = (ctx, x * 4 + (1 - y) * 2 + core)
    sibling = (ctx, x * 4 + y * 2 + 1 - core)
    blocks = lax.axis_size("ctx")
    others = [(lax.rem(ctx + d, blocks), head) for d in range(1, 8)]

    late_load = pltpu.make_async_copy(w_qkv_hbm, w_qkv, load_sem.at[2])
    late_load.start()

    started = []
    pending = {}

    def describe(kind, r, side, source, target, device):
        kind = KINDS.index(kind)
        return pltpu.make_async_remote_copy(
            src_ref=source,
            dst_ref=target,
            send_sem=sems.at[kind, r, side, 0],
            recv_sem=sems.at[kind, r, side, 1],
            device_id=device,
            device_id_type=MESH,
        )

    def send(kind, r, side, ends):
        def copy():
            return describe(kind, r, side, *ends())

        copy().start()
        started.append(copy)
        pending[kind, r, side] = copy

    every = slice(None)

    def spread_rows(r, kind, side, index, device):
        send(kind, r, side, lambda: (rows_all.at[index()], rows_all.at[index()], device))

    def arrived(kind, r, sides=(0,)):
        for side in sides:
            pending[kind, r, side]().wait_recv()

    def wide(value):
        return value.astype(jnp.float32)

    both = (0, 1)
    tile = min(1024, width)

    def project(r, w_own, w_sib):
        own_rows = normed_ref[:, core, r].reshape(8 * SUB, 256)
        sib_rows = n_sib[:, r].reshape(8 * SUB, 256)

        def columns(j, carry):
            span = pl.ds(pl.multiple_of(j * tile, tile), tile)
            value = jnp.dot(own_rows, w_own[:, span], preferred_element_type=jnp.float32)
            value += jnp.dot(sib_rows, w_sib[:, span], preferred_element_type=jnp.float32)
            part[r, :, :, :, span] = value.astype(jnp.bfloat16).reshape(4, 2, SUB, tile)
            return carry

        lax.fori_loop(0, width // tile, columns, 0)
        for s in both:

            def far(s=s):
                return part.at[r, opposite, :, :, low_half[s]], x1_far.at[r, s], along[s]

            send("x1_far", r, s, far)
        send("y1", r, 0, lambda: (part.at[r, :, 1 - y, :, high], y1_in.at[r], over_y))
        for s in both:

            def near(s=s):
                half = low_half[1 - s]
                return part.at[r, beside[s], :, :, half], x1_in.at[r, s, :, :, half], along[s]

            send("x1_near", r, s, near)

    def relay_x1(r):
        arrived("x1_far", r, both)
        for s in both:
            ours = part.at[r, beside[s], :, :, low_half[s]]
            ours[...] = (wide(ours[...]) + wide(x1_far[r, s])).astype(jnp.bfloat16)

            def summed(s=s):
                half = low_half[s]
                return part.at[r, beside[s], :, :, half], x1_in.at[r, s, :, :, half], along[s]

            send("x1_sum", r, s, summed)

    def second(r):
        arrived("y1", r)
        for place_x in (opposite,) + beside:
            ours = part.at[r, place_x, y, :, high]
            ours[...] = (wide(ours[...]) + wide(y1_in[r, place_x])).astype(jnp.bfloat16)
        for s in both:

            def far(s=s):
                return part.at[r, opposite, y, :, high_half[s]], y2_far.at[r, s], along[s]

            send("y2_far", r, s, far)
        for s in both:

            def near(s=s):
                source = part.at[r, beside[s], y, :, high_half[1 - s]]
                return source, y2_in.at[r, s, :, y_half[1 - s]], along[s]

            send("y2_near", r, s, near)
        arrived("x1_near", r, both)
        arrived("x1_sum", r, both)
        total = wide(part[r, x, 1 - y, :, low])
        for s in both:
            total += wide(x1_in[r, s, 1 - y])
        x2_out[r] = total.astype(jnp.bfloat16)
        send("x2", r, 0, lambda: (x2_out.at[r], x2_in.at[r], over_y))

    def relay_y2(r):
        arrived("y2_far", r, both)
        for s in both:
            ours = part.at[r, beside[s], y, :, high_half[s]]
            ours[...] = (wide(ours[...]) + wide(y2_far[r, s])).astype(jnp.bfloat16)

            def summed(s=s):
                source = part.at[r, beside[s], y, :, high_half[s]]
                return source, y2_in.at[r, s, :, y_half[s]], along[s]

            send("y2_sum", r, s, summed)

    def finish(r):
        arrived("x2", r)
        arrived("y2_near", r, both)
        arrived("y2_sum", r, both)
        left = wide(part[r, x, y, :, low]) + wide(x2_in[r])
        right = wide(part[r, x, y, :, high]) + wide(y1_in[r, x])
        for s in both:
            left += wide(x1_in[r, s, y])
            right += wide(y2_in[r, s])
        left = (wide(residual_ref[r, :, low]) + left).astype(jnp.bfloat16)
        right = (wide(residual_ref[r, :, high]) + right).astype(jnp.bfloat16)
        hidden_ref[r, :, low] = left
        hidden_ref[r, :, high] = right
        left, right = wide(left), wide(right)
        squares = jnp.sum(left * left, axis=-1, keepdims=True)
        squares += jnp.sum(right * right, axis=-1, keepdims=True)
        factor = lax.rsqrt(squares / width + EPSILON)
        mine = rows_all.at[r, x, y, core]
        mine[:, low] = (left * factor * gain_ref[:, low]).astype(jnp.bfloat16)
        mine[:, high] = (right * factor * gain_ref[:, high]).astype(jnp.bfloat16)

        for s in both:
            spread_rows(r, "h1", s, lambda: (r, x, y, core, every, g_low), along[s])
        spread_rows(r, "g1", 0, lambda: (r, x, y, core, every, g_high), over_y)

    def pass_h1(r):
        arrived("h1", r, both)
        for s in both:
            spread_rows(
                r,
                "h1_on",
                s,
                lambda s=s: (r, beside[1 - s], y, core, every, g_low_half[s]),
                along[s],
            )

    def spread(r):
        arrived("g1", r)
        for s in both:
            spread_rows(r, "g2", s, lambda: (r, x, every, core, every, g_high), along[s])
        arrived("h1_on", r, both)
        spread_rows(r, "h2", 0, lambda: (r, every, y, core, every, g_low), over_y)

    def pass_g2(r):
        arrived("g2", r, both)
        for s in both:
            spread_rows(
                r,
                "g2_on",
                s,
                lambda s=s: (r, beside[1 - s], every, core, every, g_high_half[s]),
                along[s],
            )

    def share(r):
        arrived("h2", r)
        spread_rows(r, "core", 0, lambda: (r, every, every, core, every, g_low), sibling)
        arrived("g2_on", r, both)
        spread_rows(r, "core", 1, lambda: (r, every, every, core, every, g_high), sibling)

    def next_copy(d, r, target, forward=False):
        landing = (kv1_ref, kv2_ref)[d - 1].at[:, r]
        kind = KINDS.index("next")
        return pltpu.make_async_remote_copy(
            src_ref=landing if forward else qkv_ref.at[:, r, :, 256:],
            dst_ref=landing,
            send_sem=sems.at[kind, r, 2 if forward else d - 1, 0],
            recv_sem=sems.at[kind, r, d - 1, 1],
            device_id=(target, head),
            device_id_type=MESH,
        )

    def project_next(r, acc):
        arrived("core", r, both)
        if r == 0:
            late_load.wait()

        def depth(j, carry):
            span = pl.ds(pl.multiple_of(j * tile, tile), tile)
            rows = rows_all[r, :, :, :, :, span].reshape(16 * SUB, tile)
            for n in range(3):
                acc[n] += jnp.dot(rows, w_qkv[n, span], preferred_element_type=jnp.float32)
            return carry

        acc[...] = jnp.zeros_like(acc)
        lax.fori_loop(0, width // tile, depth, 0)
        for n in range(3):
            qkv_ref[:, r, :, n * 256 : n * 256 + 256] = (
                acc[n].astype(jnp.bfloat16).reshape(16, SUB, 256)
            )
        for d, target, sends in routes:

            @pl.when(sends)
            def _():
                next_copy(d, r, target).start()

    routes = [
        (1, lax.rem(ctx + 1, blocks), (ctx <= 6) & (ctx != 3)),
        (2, lax.rem(ctx + 2, blocks), (ctx <= 5) & (ctx != 3)),
        (1, lax.rem(ctx + 5, blocks), ctx == 3),
        (2, lax.rem(ctx + 6, blocks), ctx == 3),
    ]
    stages = [
        project,
        relay_x1,
        second,
        relay_y2,
        finish,
        pass_h1,
        spread,
        pass_g2,
        share,
        project_next,
    ]

    def steps(first, last, *weights):
        for step in range(first, last):
            for r in range(CHUNKS):
                if 0 <= step - r < len(stages):
                    stages[step - r](r, *(weights if step - r in (0, len(stages) - 1) else ()))

    def first_steps(w_own, w_sib):
        loads = [
            pltpu.make_async_copy(source, target, load_sem.at[n])
            for n, (source, target) in enumerate([(w_own_hbm, w_own), (w_sib_hbm, w_sib)])
        ]
        for load in loads:
            load.start()
        barrier = pltpu.get_barrier_semaphore()
        for peer in along + [over_y, sibling] + others:
            pl.semaphore_signal(barrier, inc=1, device_id=peer, device_id_type=MESH)
        pl.semaphore_wait(barrier, 11)
        send("normed", 0, 0, lambda: (normed_ref.at[:, 1 - core], n_sib, sibling))
        arrived("normed", 0)
        for load in loads:
            load.wait()
        steps(0, CHUNKS, w_own, w_sib)

    def last_steps(acc):
        steps(CHUNKS, CHUNKS - 1 + len(stages), acc)

    pl.run_scoped(
        first_steps, pltpu.VMEM((256, width), jnp.bfloat16), pltpu.VMEM((256, width), jnp.bfloat16)
    )
    pl.run_scoped(last_steps, pltpu.VMEM((3, 16 * SUB, 256), jnp.float32))

    for d in (1, 2):

        @pl.when(ctx == d - 1)
        def _():
            for r in range(CHUNKS):
                next_copy(d, r, 0).wait_recv()
                next_copy(d, r, lax.rem(ctx + 4, blocks), True).start()

    tokens = 16 * CHUNKS * SUB
    groups = tokens // ROWS
    heads = 16 // groups

    def attend(vt_ref):
        m_ref[...] = jnp.full_like(m_ref, NEG)
        acc_ref[...] = jnp.zeros_like(acc_ref)

        def block(kv, own):
            def columns(start, size):
                return kv[:, :, :, start : start + size].reshape(tokens, size)

            vt_ref[...] = with_ones(columns(256, 256))

            def some(i, carry):
                queries = qkv_ref[pl.ds(i * heads, heads), :, :, :256].reshape(ROWS, 256)
                mask = None
                if own:
                    key_pos = lax.broadcasted_iota(jnp.int32, (tokens, ROWS), 0)
                    row_pos = lax.broadcasted_iota(jnp.int32, (tokens, ROWS), 1) + i * ROWS
                    mask = key_pos <= row_pos
                online_step(
                    scaled_queries(queries),
                    lambda j: columns(j * HDIM, HDIM),
                    vt_ref[...],
                    m_ref.at[i],
                    acc_ref.at[i],
                    mask,
                )
                return carry

            lax.fori_loop(0, groups, some, 0)

        block(qkv_ref.at[:, :, :, 256:], True)
        for d, landing in ((1, kv1_ref), (2, kv2_ref)):

            @pl.when(ctx >= d)
            def _():
                for r in range(CHUNKS):
                    next_copy(d, r, 0).wait_recv()
                block(landing, False)

    pl.run_scoped(attend, pltpu.VMEM((256 + ONES, tokens), jnp.bfloat16))
    for copy in started:
        copy().wait_send()
    for r in range(CHUNKS):
        for d, target, sends in routes:

            @pl.when(sends)
            def _():
                next_copy(d, r, target).wait_send()

        for d in (1, 2):

            @pl.when(ctx == d - 1)
            def _():
                next_copy(d, r, 0, True).wait_send()


def project_and_spread(normed, w_own, w_sib, residual, gain, w_qkv):
    width = w_own.shape[1]
    x_cols = width * 9 // 16
    g_cols = width * 7 // 16
    tokens = 16 * CHUNKS * SUB
    bf16 = jnp.bfloat16
    any_space = pl.BlockSpec(memory_space=pl.ANY)
    vmem = pl.BlockSpec(memory_space=pltpu.VMEM)
    sem = pltpu.SemaphoreType.DMA
    hidden, sums, highest = pl.pallas_call(
        functools.partial(mid_kernel, x_cols, g_cols),
        name="project_and_spread",
        out_shape=(
            jax.ShapeDtypeStruct((CHUNKS, SUB, width), bf16),
            jax.ShapeDtypeStruct((tokens // ROWS, 2, 256 + ONES, ROWS), jnp.float32),
            jax.ShapeDtypeStruct((tokens // ROWS, 2, 1, ROWS), jnp.float32),
        ),
        in_specs=[vmem, any_space, any_space, vmem, vmem, any_space],
        out_specs=(vmem, vmem, vmem),
        scratch_shapes=[
            pltpu.VMEM((16, CHUNKS, SUB, 768), bf16),
            pltpu.VMEM((16, CHUNKS, SUB, 512), bf16),
            pltpu.VMEM((16, CHUNKS, SUB, 512), bf16),
            pltpu.VMEM((3, width, 256), bf16),
            pltpu.VMEM((8, CHUNKS, SUB, 256), bf16),
            pltpu.VMEM((CHUNKS, 4, 2, SUB, width), bf16),
            pltpu.VMEM((CHUNKS, 2, 2, SUB, x_cols // 2), bf16),
            pltpu.VMEM((CHUNKS, 2, 2, SUB, x_cols), bf16),
            pltpu.VMEM((CHUNKS, 4, SUB, width - x_cols), bf16),
            pltpu.VMEM((CHUNKS, SUB, x_cols), bf16),
            pltpu.VMEM((CHUNKS, SUB, x_cols), bf16),
            pltpu.VMEM((CHUNKS, 2, SUB, (width - x_cols) // 2), bf16),
            pltpu.VMEM((CHUNKS, 2, SUB, width - x_cols), bf16),
            pltpu.VMEM((CHUNKS, 4, 2, 2, SUB, width), bf16),
            sem((3,)),
            sem((len(KINDS), CHUNKS, 3, 2)),
        ],
        compiler_params=pltpu.CompilerParams(
            collective_id=0, has_side_effects=True, vmem_limit_bytes=63 * 2**20
        ),
    )(
        normed.reshape(8, 2, CHUNKS, SUB, 256),
        w_own,
        w_sib,
        residual.reshape(CHUNKS, SUB, width),
        gain.reshape(1, width),
        w_qkv,
    )
    return hidden.reshape(CHUNKS * SUB, width), sums, highest


def settle_kernel(hidden_in, acc_ref, m_ref, hidden_ref, out_ref, log_ref):
    hidden_ref[...] = hidden_in[...]
    for j in range(2):
        total = acc_ref[0, j, 256:257]
        value = (acc_ref[0, j, :256] / total).T
        for half in range(2):
            out_ref[j, pl.ds(half, ROWS, stride=2), :] = value[:, half * 128 : half * 128 + 128]
        log_ref[j] = (m_ref[0, j] + jnp.log2(total)) * LN2


def settle(hidden, sums, highest):
    groups = sums.shape[0]
    rows, width = hidden.shape
    return pl.pallas_call(
        settle_kernel,
        name="settle",
        grid=(groups,),
        out_shape=(
            jax.ShapeDtypeStruct((rows, width), jnp.bfloat16),
            jax.ShapeDtypeStruct((2, 2 * groups * ROWS, 128), jnp.float32),
            jax.ShapeDtypeStruct((2, 1, groups * ROWS), jnp.float32),
        ),
        in_specs=[
            pl.BlockSpec((rows // groups, width), lambda i: (i, 0)),
            pl.BlockSpec((1, 2, 256 + ONES, ROWS), lambda i: (i, 0, 0, 0)),
            pl.BlockSpec((1, 2, 1, ROWS), lambda i: (i, 0, 0, 0)),
        ],
        out_specs=(
            pl.BlockSpec((rows // groups, width), lambda i: (i, 0)),
            pl.BlockSpec((2, 2 * ROWS, 128), lambda i: (0, i, 0)),
            pl.BlockSpec((2, 1, ROWS), lambda i: (0, 0, i)),
        ),
        compiler_params=pltpu.CompilerParams(vmem_limit_bytes=62 * 2**20),
    )(hidden, sums, highest)


def on_device(residual, q_win, kv_win, lam_win, gn_gain, w_out_a, norm_gain, w_qkv):
    tokens_here = q_win.shape[0]
    w_sib = lax.ppermute(w_out_a, "head", [(i, i ^ 1) for i in range(lax.axis_size("head"))])
    normed = window_attention(
        q_win.reshape(tokens_here, 256), kv_win.reshape(tokens_here, 512), lam_win, gn_gain
    )
    h_rows, part_out, log_out = settle(
        *project_and_spread(
            normed, w_out_a, w_sib, residual, norm_gain, w_qkv[:, 0].transpose(1, 0, 2)
        )
    )
    return (
        h_rows,
        part_out.reshape(2, tokens_here, 1, 256),
        log_out,
    )


def solution(mesh):
    in_specs = (
        P(("ctx", "head"), None),
        P("ctx", "head", None),
        P("ctx", "head", None, None),
        P(),
        P(),
        P("head", None),
        P(),
        P(None, "head", None, None),
    )
    out_specs = (P(("ctx", "head"), None), P(None, "ctx", "head", None), P(None, "head", "ctx"))
    return jax.shard_map(
        on_device, mesh=mesh, in_specs=in_specs, out_specs=out_specs, check_vma=False
    )
```

```python
import functools
import math

import jax
import jax.numpy as jnp
from jax import lax
from jax.experimental import pallas as pl
from jax.experimental.pallas import tpu as pltpu
from jax.sharding import PartitionSpec as P

HDIM = 128
WINDOW = 4096
EPSILON = 1e-05
LAMBDA_INIT = 0.8 - 0.6 * math.exp(-3.3)
SCALE = math.log2(math.e) / math.sqrt(HDIM)
LN2 = math.log(2.0)
NEG = -1e30
ONES = 16
ROWS = 256
MESH = pl.DeviceIdType.MESH


def with_ones(values):
    flipped = values.astype(jnp.float32).T.astype(jnp.bfloat16)
    return jnp.concatenate([flipped, jnp.ones((ONES, values.shape[0]), jnp.bfloat16)], axis=0)


def scaled_queries(picked):
    return (picked.astype(jnp.float32) * SCALE).astype(jnp.bfloat16)


def online_step(queries, keys_of, values_up, m_ref, acc_ref, mask):
    for j in range(2):
        scores = lax.dot_general(
            keys_of(j),
            queries[:, j * HDIM : (j + 1) * HDIM],
            (((1,), (1,)), ((), ())),
            preferred_element_type=jnp.float32,
        )
        if mask is not None:
            scores = jnp.where(mask, scores, NEG)
        before = m_ref[j]
        after = jnp.maximum(before, jnp.max(scores, axis=0, keepdims=True))
        weights = jnp.exp2(scores - after).astype(jnp.bfloat16)
        acc_ref[j] = acc_ref[j] * jnp.exp2(before - after) + jnp.dot(
            values_up, weights, preferred_element_type=jnp.float32
        )
        m_ref[j] = after


PIECES = 8


def window_kernel(
    lam_ref, q_ref, gain_ref, kv_ref, out_ref, kv_in, q_scaled, vt_ref, m_ref, acc_ref, up_sem, ring_sem, on_sem
):
    ctx, head = lax.axis_index("ctx"), lax.axis_index("head")
    ring, z = ctx // 4, lax.rem(ctx, 4)
    tokens = kv_ref.shape[0]
    piece = tokens // PIECES
    over = ((1 - ring) * 4 + z, head)

    def along(e):
        return (ring * 4 + lax.rem(z + e, 4), head)

    def copy_up(n):
        rows = pl.ds(n * piece, piece)
        return pltpu.make_async_remote_copy(
            src_ref=kv_ref.at[rows],
            dst_ref=kv_in.at[3, rows],
            send_sem=up_sem.at[n, 0],
            recv_sem=up_sem.at[n, 1],
            device_id=over,
            device_id_type=MESH,
        )

    def copy_along(e, n, source):
        rows = pl.ds(n * piece, piece)
        return pltpu.make_async_remote_copy(
            src_ref=source.at[rows],
            dst_ref=kv_in.at[e - 1, rows],
            send_sem=ring_sem.at[e - 1, n, 0],
            recv_sem=ring_sem.at[e - 1, n, 1],
            device_id=along(e),
            device_id_type=MESH,
        )

    barrier = pltpu.get_barrier_semaphore()
    for peer in (along(1), along(2), along(3), over):
        pl.semaphore_signal(barrier, inc=1, device_id=peer, device_id_type=MESH)
    pl.semaphore_wait(barrier, 4)

    @pl.when(ring == 0)
    def _():
        for n in range(PIECES):
            copy_up(n).start()

    def copy_on(side, n):
        rows = pl.ds(n * piece, piece)
        return pltpu.make_async_remote_copy(
            src_ref=kv_in.at[2 * side, rows],
            dst_ref=kv_in.at[1, rows],
            send_sem=on_sem.at[side, n],
            recv_sem=ring_sem.at[1, n, 1],
            device_id=along(1 + 2 * side),
            device_id_type=MESH,
        )

    def passes_on(side, n):
        if side == 0:
            return (z <= 2) & (ctx >= 1) if n % 2 == 0 else (z == 2)
        return (ctx >= 3) & (z >= 1) if n % 2 == 1 else (ring == 1) & (z == 1)

    for e in (1, 3):

        @pl.when(z + e <= 3)
        def _():
            for n in range(PIECES):
                copy_along(e, n, kv_ref).start()

    q_scaled[...] = scaled_queries(q_ref[...])
    m_ref[...] = jnp.full_like(m_ref, NEG)
    acc_ref[...] = jnp.zeros_like(acc_ref)

    def all_queries(keys, edge):
        count = keys.shape[0]
        vt_ref[:, :count] = with_ones(keys[:, 256:])

        def some(i, carry):
            rows = pl.ds(pl.multiple_of(i * ROWS, ROWS), ROWS)
            mask = None
            if edge is not None:
                key_pos = lax.broadcasted_iota(jnp.int32, (tokens, ROWS), 0)
                row_pos = lax.broadcasted_iota(jnp.int32, (tokens, ROWS), 1) + i * ROWS
                mask = key_pos <= row_pos if edge == "own" else key_pos > row_pos
            online_step(
                q_scaled[rows, :],
                lambda j: keys[:, j * HDIM : (j + 1) * HDIM],
                vt_ref[:, :count],
                m_ref.at[i],
                acc_ref.at[i],
                mask,
            )
            return carry

        lax.fori_loop(0, tokens // ROWS, some, 0)

    all_queries(kv_ref, "own")

    @pl.when(ring == 1)
    def _():
        for n in range(PIECES):
            copy_up(n).wait_recv()
            for e in (3, 1):

                @pl.when(z + e >= 4)
                def _():
                    copy_along(e, n, kv_in.at[3]).start()

    for side in (0, 1):

        @pl.when(ctx >= 1 + 2 * side)
        def _():
            for n in range(PIECES):
                copy_along(1 + 2 * side, n, kv_ref).wait_recv()

        for n in range(PIECES):

            @pl.when(passes_on(side, n))
            def _():
                copy_on(side, n).start()

    @pl.when(ring == 1)
    def _():
        all_queries(kv_in.at[3], "far")

    for e in (1, 3, 2):

        @pl.when(ctx >= e)
        def _():
            if e != 2:
                all_queries(kv_in.at[e - 1], None)
                return
            for half in range(2):
                for n in range(half * PIECES // 2, (half + 1) * PIECES // 2):
                    copy_along(2, n, kv_ref).wait_recv()
                all_queries(kv_in.at[1, pl.ds(half * tokens // 2, tokens // 2)], None)

    pairs = lam_ref[...]
    lam = (
        jnp.exp(jnp.sum(pairs[0:1] * pairs[1:2], axis=1, keepdims=True))
        - jnp.exp(jnp.sum(pairs[2:3] * pairs[3:4], axis=1, keepdims=True))
        + LAMBDA_INIT
    )

    def finish(i, carry):
        one = acc_ref[i, 0, :256] / acc_ref[i, 0, 256:257]
        two = acc_ref[i, 1, :256] / acc_ref[i, 1, 256:257]
        attended = one - lam * two
        factor = lax.rsqrt(jnp.mean(attended * attended, axis=0, keepdims=True) + EPSILON)
        normed = (attended * factor).T * (gain_ref[...] * (1.0 - LAMBDA_INIT))
        out_ref[pl.ds(pl.multiple_of(i * ROWS, ROWS), ROWS), :] = normed.astype(jnp.bfloat16)
        return carry

    lax.fori_loop(0, tokens // ROWS, finish, 0)

    @pl.when(ring == 0)
    def _():
        for n in range(PIECES):
            copy_up(n).wait_send()

    for e in (1, 3):

        @pl.when((ring == 1) | (z + e <= 3))
        def _():
            for n in range(PIECES):
                copy_along(e, n, kv_ref).wait_send()

    for side in (0, 1):
        for n in range(PIECES):

            @pl.when(passes_on(side, n))
            def _():
                copy_on(side, n).wait_send()


def window_attention(queries, keys_values, lam_win, gain):
    tokens = queries.shape[0]
    vmem = pl.BlockSpec(memory_space=pltpu.VMEM)
    return pl.pallas_call(
        window_kernel,
        name="window",
        out_shape=jax.ShapeDtypeStruct((tokens, 256), jnp.bfloat16),
        in_specs=[vmem] * 4,
        out_specs=vmem,
        scratch_shapes=[
            pltpu.VMEM((4, tokens, 512), jnp.bfloat16),
            pltpu.VMEM((tokens, 256), jnp.bfloat16),
            pltpu.VMEM((256 + ONES, tokens), jnp.bfloat16),
            pltpu.VMEM((tokens // ROWS, 2, 1, ROWS), jnp.float32),
            pltpu.VMEM((tokens // ROWS, 2, 256 + ONES, ROWS), jnp.float32),
            pltpu.SemaphoreType.DMA((PIECES, 2)),
            pltpu.SemaphoreType.DMA((3, PIECES, 2)),
            pltpu.SemaphoreType.DMA((2, PIECES)),
        ],
        compiler_params=pltpu.CompilerParams(
            collective_id=1, has_side_effects=True, vmem_limit_bytes=62 * 2**20
        ),
    )(lam_win, queries, gain.reshape(1, 256), keys_values)


CHUNKS = 4
SUB = 16


def place():
    head = lax.axis_index("head")
    return lax.axis_index("ctx"), head // 4, (head // 2) % 2, head % 2


KINDS = (
    "normed",
    "y1",
    "x1_far",
    "x1_near",
    "x1_sum",
    "x2",
    "y2_far",
    "y2_near",
    "y2_sum",
    "h1",
    "h1_on",
    "g1",
    "h2",
    "g2",
    "g2_on",
    "core",
    "next",
)


def mid_kernel(
    x_cols,
    g_cols,
    normed_ref,
    w_own_hbm,
    w_sib_hbm,
    residual_ref,
    gain_ref,
    w_qkv_hbm,
    hidden_ref,
    acc_ref,
    m_ref,
    qkv_ref,
    kv1_ref,
    kv2_ref,
    w_qkv,
    n_sib,
    part,
    x1_far,
    x1_in,
    y1_in,
    x2_out,
    x2_in,
    y2_far,
    y2_in,
    rows_all,
    load_sem,
    sems,
):
    ctx, x, y, core = place()
    width = w_own_hbm.shape[1]
    y_cols = width - x_cols
    low, high = pl.ds(0, x_cols), pl.ds(x_cols, y_cols)
    low_half = (pl.ds(0, x_cols // 2), pl.ds(x_cols // 2, x_cols // 2))
    high_half = (pl.ds(x_cols, y_cols // 2), pl.ds(x_cols + y_cols // 2, y_cols // 2))
    g_low, g_high = pl.ds(0, g_cols), pl.ds(g_cols, width - g_cols)
    g_low_half = (pl.ds(0, g_cols // 2), pl.ds(g_cols // 2, g_cols // 2))
    g_high_half = tuple(
        pl.ds(g_cols + s * ((width - g_cols) // 2), (width - g_cols) // 2) for s in (0, 1)
    )
    y_half = (pl.ds(0, y_cols // 2), pl.ds(y_cols // 2, y_cols // 2))
    head = lax.axis_index("head")
    beside = (lax.rem(x + 1, 4), lax.rem(x + 3, 4))
    opposite = lax.rem(x + 2, 4)
    along = [(ctx, place_x * 4 + y * 2 + core) for place_x in beside]
    over_y = (ctx, x * 4 + (1 - y) * 2 + core)
    sibling = (ctx, x * 4 + y * 2 + 1 - core)
    blocks = lax.axis_size("ctx")
    others = [(lax.rem(ctx + d, blocks), head) for d in range(1, 8)]

    late_load = pltpu.make_async_copy(w_qkv_hbm, w_qkv, load_sem.at[2])
    late_load.start()

    started = []
    pending = {}

    def describe(kind, r, side, source, target, device):
        kind = KINDS.index(kind)
        return pltpu.make_async_remote_copy(
            src_ref=source,
            dst_ref=target,
            send_sem=sems.at[kind, r, side, 0],
            recv_sem=sems.at[kind, r, side, 1],
            device_id=device,
            device_id_type=MESH,
        )

    def send(kind, r, side, ends):
        def copy():
            return describe(kind, r, side, *ends())

        copy().start()
        started.append(copy)
        pending[kind, r, side] = copy

    every = slice(None)

    def spread_rows(r, kind, side, index, device):
        send(kind, r, side, lambda: (rows_all.at[index()], rows_all.at[index()], device))

    def arrived(kind, r, sides=(0,)):
        for side in sides:
            pending[kind, r, side]().wait_recv()

    def wide(value):
        return value.astype(jnp.float32)

    both = (0, 1)
    tile = min(1024, width)

    def project(r, w_own, w_sib):
        own_rows = normed_ref[:, core, r].reshape(8 * SUB, 256)
        sib_rows = n_sib[:, r].reshape(8 * SUB, 256)

        def columns(j, carry):
            span = pl.ds(pl.multiple_of(j * tile, tile), tile)
            value = jnp.dot(own_rows, w_own[:, span], preferred_element_type=jnp.float32)
            value += jnp.dot(sib_rows, w_sib[:, span], preferred_element_type=jnp.float32)
            part[r, :, :, :, span] = value.astype(jnp.bfloat16).reshape(4, 2, SUB, tile)
            return carry

        lax.fori_loop(0, width // tile, columns, 0)
        for s in both:

            def far(s=s):
                return part.at[r, opposite, :, :, low_half[s]], x1_far.at[r, s], along[s]

            send("x1_far", r, s, far)
        send("y1", r, 0, lambda: (part.at[r, :, 1 - y, :, high], y1_in.at[r], over_y))
        for s in both:

            def near(s=s):
                half = low_half[1 - s]
                return part.at[r, beside[s], :, :, half], x1_in.at[r, s, :, :, half], along[s]

            send("x1_near", r, s, near)

    def relay_x1(r):
        arrived("x1_far", r, both)
        for s in both:
            ours = part.at[r, beside[s], :, :, low_half[s]]
            ours[...] = (wide(ours[...]) + wide(x1_far[r, s])).astype(jnp.bfloat16)

            def summed(s=s):
                half = low_half[s]
                return part.at[r, beside[s], :, :, half], x1_in.at[r, s, :, :, half], along[s]

            send("x1_sum", r, s, summed)

    def second(r):
        arrived("y1", r)
        for place_x in (opposite,) + beside:
            ours = part.at[r, place_x, y, :, high]
            ours[...] = (wide(ours[...]) + wide(y1_in[r, place_x])).astype(jnp.bfloat16)
        for s in both:

            def far(s=s):
                return part.at[r, opposite, y, :, high_half[s]], y2_far.at[r, s], along[s]

            send("y2_far", r, s, far)
        for s in both:

            def near(s=s):
                source = part.at[r, beside[s], y, :, high_half[1 - s]]
                return source, y2_in.at[r, s, :, y_half[1 - s]], along[s]

            send("y2_near", r, s, near)
        arrived("x1_near", r, both)
        arrived("x1_sum", r, both)
        total = wide(part[r, x, 1 - y, :, low])
        for s in both:
            total += wide(x1_in[r, s, 1 - y])
        x2_out[r] = total.astype(jnp.bfloat16)
        send("x2", r, 0, lambda: (x2_out.at[r], x2_in.at[r], over_y))

    def relay_y2(r):
        arrived("y2_far", r, both)
        for s in both:
            ours = part.at[r, beside[s], y, :, high_half[s]]
            ours[...] = (wide(ours[...]) + wide(y2_far[r, s])).astype(jnp.bfloat16)

            def summed(s=s):
                source = part.at[r, beside[s], y, :, high_half[s]]
                return source, y2_in.at[r, s, :, y_half[s]], along[s]

            send("y2_sum", r, s, summed)

    def finish(r):
        arrived("x2", r)
        arrived("y2_near", r, both)
        arrived("y2_sum", r, both)
        left = wide(part[r, x, y, :, low]) + wide(x2_in[r])
        right = wide(part[r, x, y, :, high]) + wide(y1_in[r, x])
        for s in both:
            left += wide(x1_in[r, s, y])
            right += wide(y2_in[r, s])
        left = (wide(residual_ref[r, :, low]) + left).astype(jnp.bfloat16)
        right = (wide(residual_ref[r, :, high]) + right).astype(jnp.bfloat16)
        hidden_ref[r, :, low] = left
        hidden_ref[r, :, high] = right
        left, right = wide(left), wide(right)
        squares = jnp.sum(left * left, axis=-1, keepdims=True)
        squares += jnp.sum(right * right, axis=-1, keepdims=True)
        factor = lax.rsqrt(squares / width + EPSILON)
        mine = rows_all.at[r, x, y, core]
        mine[:, low] = (left * factor * gain_ref[:, low]).astype(jnp.bfloat16)
        mine[:, high] = (right * factor * gain_ref[:, high]).astype(jnp.bfloat16)

        for s in both:
            spread_rows(r, "h1", s, lambda: (r, x, y, core, every, g_low), along[s])
        spread_rows(r, "g1", 0, lambda: (r, x, y, core, every, g_high), over_y)

    def pass_h1(r):
        arrived("h1", r, both)
        for s in both:
            spread_rows(
                r,
                "h1_on",
                s,
                lambda s=s: (r, beside[1 - s], y, core, every, g_low_half[s]),
                along[s],
            )

    def spread(r):
        arrived("g1", r)
        for s in both:
            spread_rows(r, "g2", s, lambda: (r, x, every, core, every, g_high), along[s])
        arrived("h1_on", r, both)
        spread_rows(r, "h2", 0, lambda: (r, every, y, core, every, g_low), over_y)

    def pass_g2(r):
        arrived("g2", r, both)
        for s in both:
            spread_rows(
                r,
                "g2_on",
                s,
                lambda s=s: (r, beside[1 - s], every, core, every, g_high_half[s]),
                along[s],
            )

    def share(r):
        arrived("h2", r)
        spread_rows(r, "core", 0, lambda: (r, every, every, core, every, g_low), sibling)
        arrived("g2_on", r, both)
        spread_rows(r, "core", 1, lambda: (r, every, every, core, every, g_high), sibling)

    def next_copy(d, r, target, forward=False):
        landing = (kv1_ref, kv2_ref)[d - 1].at[:, r]
        kind = KINDS.index("next")
        return pltpu.make_async_remote_copy(
            src_ref=landing if forward else qkv_ref.at[:, r, :, 256:],
            dst_ref=landing,
            send_sem=sems.at[kind, r, 2 if forward else d - 1, 0],
            recv_sem=sems.at[kind, r, d - 1, 1],
            device_id=(target, head),
            device_id_type=MESH,
        )

    def project_next(r, acc):
        arrived("core", r, both)
        if r == 0:
            late_load.wait()

        def depth(j, carry):
            span = pl.ds(pl.multiple_of(j * tile, tile), tile)
            rows = rows_all[r, :, :, :, :, span].reshape(16 * SUB, tile)
            for n in range(3):
                acc[n] += jnp.dot(rows, w_qkv[n, span], preferred_element_type=jnp.float32)
            return carry

        acc[...] = jnp.zeros_like(acc)
        lax.fori_loop(0, width // tile, depth, 0)
        for n in range(3):
            qkv_ref[:, r, :, n * 256 : n * 256 + 256] = (
                acc[n].astype(jnp.bfloat16).reshape(16, SUB, 256)
            )
        for d, target, sends in routes:

            @pl.when(sends)
            def _():
                next_copy(d, r, target).start()

    routes = [
        (1, lax.rem(ctx + 1, blocks), (ctx <= 6) & (ctx != 3)),
        (2, lax.rem(ctx + 2, blocks), (ctx <= 5) & (ctx != 3)),
        (1, lax.rem(ctx + 5, blocks), ctx == 3),
        (2, lax.rem(ctx + 6, blocks), ctx == 3),
    ]
    stages = [
        project,
        relay_x1,
        second,
        relay_y2,
        finish,
        pass_h1,
        spread,
        pass_g2,
        share,
        project_next,
    ]

    def steps(first, last, *weights):
        for step in range(first, last):
            for r in range(CHUNKS):
                if 0 <= step - r < len(stages):
                    stages[step - r](r, *(weights if step - r in (0, len(stages) - 1) else ()))

    def first_steps(w_own, w_sib):
        loads = [
            pltpu.make_async_copy(source, target, load_sem.at[n])
            for n, (source, target) in enumerate([(w_own_hbm, w_own), (w_sib_hbm, w_sib)])
        ]
        for load in loads:
            load.start()
        barrier = pltpu.get_barrier_semaphore()
        for peer in along + [over_y, sibling] + others:
            pl.semaphore_signal(barrier, inc=1, device_id=peer, device_id_type=MESH)
        pl.semaphore_wait(barrier, 11)
        send("normed", 0, 0, lambda: (normed_ref.at[:, 1 - core], n_sib, sibling))
        arrived("normed", 0)
        for load in loads:
            load.wait()
        steps(0, CHUNKS, w_own, w_sib)

    def last_steps(acc):
        steps(CHUNKS, CHUNKS - 1 + len(stages), acc)

    pl.run_scoped(
        first_steps, pltpu.VMEM((256, width), jnp.bfloat16), pltpu.VMEM((256, width), jnp.bfloat16)
    )
    pl.run_scoped(last_steps, pltpu.VMEM((3, 16 * SUB, 256), jnp.float32))

    for d in (1, 2):

        @pl.when(ctx == d - 1)
        def _():
            for r in range(CHUNKS):
                next_copy(d, r, 0).wait_recv()
                next_copy(d, r, lax.rem(ctx + 4, blocks), True).start()

    tokens = 16 * CHUNKS * SUB
    groups = tokens // ROWS
    heads = 16 // groups

    def attend(vt_ref):
        m_ref[...] = jnp.full_like(m_ref, NEG)
        acc_ref[...] = jnp.zeros_like(acc_ref)

        def block(kv, own, first=0, last=CHUNKS):
            count = 16 * (last - first) * SUB

            def columns(start, size):
                return kv[:, first:last, :, start : start + size].reshape(count, size)

            vt_ref[:, :count] = with_ones(columns(256, 256))

            def some(i, carry):
                queries = qkv_ref[pl.ds(i * heads, heads), :, :, :256].reshape(ROWS, 256)
                mask = None
                if own:
                    key_pos = lax.broadcasted_iota(jnp.int32, (tokens, ROWS), 0)
                    row_pos = lax.broadcasted_iota(jnp.int32, (tokens, ROWS), 1) + i * ROWS
                    mask = key_pos <= row_pos
                online_step(
                    scaled_queries(queries),
                    lambda j: columns(j * HDIM, HDIM),
                    vt_ref[:, :count],
                    m_ref.at[i],
                    acc_ref.at[i],
                    mask,
                )
                return carry

            lax.fori_loop(0, groups, some, 0)

        block(qkv_ref.at[:, :, :, 256:], True)
        for first, last in ((0, CHUNKS - 1), (CHUNKS - 1, CHUNKS)):
            for d, landing in ((1, kv1_ref), (2, kv2_ref)):

                @pl.when(ctx >= d)
                def _():
                    for r in range(first, last):
                        next_copy(d, r, 0).wait_recv()
                    block(landing, False, first, last)

    pl.run_scoped(attend, pltpu.VMEM((256 + ONES, tokens), jnp.bfloat16))
    for copy in started:
        copy().wait_send()
    for r in range(CHUNKS):
        for d, target, sends in routes:

            @pl.when(sends)
            def _():
                next_copy(d, r, target).wait_send()

        for d in (1, 2):

            @pl.when(ctx == d - 1)
            def _():
                next_copy(d, r, 0, True).wait_send()


def project_and_spread(normed, w_own, w_sib, residual, gain, w_qkv):
    width = w_own.shape[1]
    x_cols = width * 9 // 16
    g_cols = width * 7 // 16
    tokens = 16 * CHUNKS * SUB
    bf16 = jnp.bfloat16
    any_space = pl.BlockSpec(memory_space=pl.ANY)
    vmem = pl.BlockSpec(memory_space=pltpu.VMEM)
    sem = pltpu.SemaphoreType.DMA
    hidden, sums, highest = pl.pallas_call(
        functools.partial(mid_kernel, x_cols, g_cols),
        name="project_and_spread",
        out_shape=(
            jax.ShapeDtypeStruct((CHUNKS, SUB, width), bf16),
            jax.ShapeDtypeStruct((tokens // ROWS, 2, 256 + ONES, ROWS), jnp.float32),
            jax.ShapeDtypeStruct((tokens // ROWS, 2, 1, ROWS), jnp.float32),
        ),
        in_specs=[vmem, any_space, any_space, vmem, vmem, any_space],
        out_specs=(vmem, vmem, vmem),
        scratch_shapes=[
            pltpu.VMEM((16, CHUNKS, SUB, 768), bf16),
            pltpu.VMEM((16, CHUNKS, SUB, 512), bf16),
            pltpu.VMEM((16, CHUNKS, SUB, 512), bf16),
            pltpu.VMEM((3, width, 256), bf16),
            pltpu.VMEM((8, CHUNKS, SUB, 256), bf16),
            pltpu.VMEM((CHUNKS, 4, 2, SUB, width), bf16),
            pltpu.VMEM((CHUNKS, 2, 2, SUB, x_cols // 2), bf16),
            pltpu.VMEM((CHUNKS, 2, 2, SUB, x_cols), bf16),
            pltpu.VMEM((CHUNKS, 4, SUB, width - x_cols), bf16),
            pltpu.VMEM((CHUNKS, SUB, x_cols), bf16),
            pltpu.VMEM((CHUNKS, SUB, x_cols), bf16),
            pltpu.VMEM((CHUNKS, 2, SUB, (width - x_cols) // 2), bf16),
            pltpu.VMEM((CHUNKS, 2, SUB, width - x_cols), bf16),
            pltpu.VMEM((CHUNKS, 4, 2, 2, SUB, width), bf16),
            sem((3,)),
            sem((len(KINDS), CHUNKS, 3, 2)),
        ],
        compiler_params=pltpu.CompilerParams(
            collective_id=0, has_side_effects=True, vmem_limit_bytes=63 * 2**20
        ),
    )(
        normed.reshape(8, 2, CHUNKS, SUB, 256),
        w_own,
        w_sib,
        residual.reshape(CHUNKS, SUB, width),
        gain.reshape(1, width),
        w_qkv,
    )
    return hidden.reshape(CHUNKS * SUB, width), sums, highest


def settle_kernel(hidden_in, acc_ref, m_ref, hidden_ref, out_ref, log_ref):
    hidden_ref[...] = hidden_in[...]
    for j in range(2):
        total = acc_ref[0, j, 256:257]
        value = (acc_ref[0, j, :256] / total).T
        for half in range(2):
            out_ref[j, pl.ds(half, ROWS, stride=2), :] = value[:, half * 128 : half * 128 + 128]
        log_ref[j] = (m_ref[0, j] + jnp.log2(total)) * LN2


def settle(hidden, sums, highest):
    groups = sums.shape[0]
    rows, width = hidden.shape
    return pl.pallas_call(
        settle_kernel,
        name="settle",
        grid=(groups,),
        out_shape=(
            jax.ShapeDtypeStruct((rows, width), jnp.bfloat16),
            jax.ShapeDtypeStruct((2, 2 * groups * ROWS, 128), jnp.float32),
            jax.ShapeDtypeStruct((2, 1, groups * ROWS), jnp.float32),
        ),
        in_specs=[
            pl.BlockSpec((rows // groups, width), lambda i: (i, 0)),
            pl.BlockSpec((1, 2, 256 + ONES, ROWS), lambda i: (i, 0, 0, 0)),
            pl.BlockSpec((1, 2, 1, ROWS), lambda i: (i, 0, 0, 0)),
        ],
        out_specs=(
            pl.BlockSpec((rows // groups, width), lambda i: (i, 0)),
            pl.BlockSpec((2, 2 * ROWS, 128), lambda i: (0, i, 0)),
            pl.BlockSpec((2, 1, ROWS), lambda i: (0, 0, i)),
        ),
        compiler_params=pltpu.CompilerParams(vmem_limit_bytes=62 * 2**20),
    )(hidden, sums, highest)


def on_device(residual, q_win, kv_win, lam_win, gn_gain, w_out_a, norm_gain, w_qkv):
    tokens_here = q_win.shape[0]
    w_sib = lax.ppermute(w_out_a, "head", [(i, i ^ 1) for i in range(lax.axis_size("head"))])
    normed = window_attention(
        q_win.reshape(tokens_here, 256), kv_win.reshape(tokens_here, 512), lam_win, gn_gain
    )
    h_rows, part_out, log_out = settle(
        *project_and_spread(
            normed, w_out_a, w_sib, residual, norm_gain, w_qkv[:, 0].transpose(1, 0, 2)
        )
    )
    return (
        h_rows,
        part_out.reshape(2, tokens_here, 1, 256),
        log_out,
    )


def solution(mesh):
    in_specs = (
        P(("ctx", "head"), None),
        P("ctx", "head", None),
        P("ctx", "head", None, None),
        P(),
        P(),
        P("head", None),
        P(),
        P(None, "head", None, None),
    )
    out_specs = (P(("ctx", "head"), None), P(None, "ctx", "head", None), P(None, "head", "ctx"))
    return jax.shard_map(
        on_device, mesh=mesh, in_specs=in_specs, out_specs=out_specs, check_vma=False
    )
```

```python
import functools
import math

import jax
import jax.numpy as jnp
from jax import lax
from jax.experimental import pallas as pl
from jax.experimental.pallas import tpu as pltpu
from jax.sharding import PartitionSpec as P

HDIM = 128
WINDOW = 4096
EPSILON = 1e-05
LAMBDA_INIT = 0.8 - 0.6 * math.exp(-3.3)
SCALE = math.log2(math.e) / math.sqrt(HDIM)
LN2 = math.log(2.0)
NEG = -1e30
ONES = 16
ROWS = 256
MESH = pl.DeviceIdType.MESH


def with_ones(values):
    flipped = values.astype(jnp.float32).T.astype(jnp.bfloat16)
    return jnp.concatenate([flipped, jnp.ones((ONES, values.shape[0]), jnp.bfloat16)], axis=0)


def scaled_queries(picked):
    return (picked.astype(jnp.float32) * SCALE).astype(jnp.bfloat16)


def online_step(queries, keys_of, values_up, m_ref, acc_ref, mask):
    for j in range(2):
        scores = lax.dot_general(
            keys_of(j),
            queries[:, j * HDIM : (j + 1) * HDIM],
            (((1,), (1,)), ((), ())),
            preferred_element_type=jnp.float32,
        )
        if mask is not None:
            scores = jnp.where(mask, scores, NEG)
        before = m_ref[j]
        after = jnp.maximum(before, jnp.max(scores, axis=0, keepdims=True))
        weights = jnp.exp2(scores - after).astype(jnp.bfloat16)
        acc_ref[j] = acc_ref[j] * jnp.exp2(before - after) + jnp.dot(
            values_up, weights, preferred_element_type=jnp.float32
        )
        m_ref[j] = after


PIECES = 8


def window_kernel(
    lam_ref, q_ref, gain_ref, kv_ref, out_ref, kv_in, q_scaled, vt_ref, m_ref, acc_ref, up_sem, ring_sem, on_sem
):
    ctx, head = lax.axis_index("ctx"), lax.axis_index("head")
    ring, z = ctx // 4, lax.rem(ctx, 4)
    tokens = kv_ref.shape[0]
    piece = tokens // PIECES
    over = ((1 - ring) * 4 + z, head)

    def along(e):
        return (ring * 4 + lax.rem(z + e, 4), head)

    def copy_up(n):
        rows = pl.ds(n * piece, piece)
        return pltpu.make_async_remote_copy(
            src_ref=kv_ref.at[rows],
            dst_ref=kv_in.at[3, rows],
            send_sem=up_sem.at[n, 0],
            recv_sem=up_sem.at[n, 1],
            device_id=over,
            device_id_type=MESH,
        )

    def copy_along(e, n, source):
        rows = pl.ds(n * piece, piece)
        return pltpu.make_async_remote_copy(
            src_ref=source.at[rows],
            dst_ref=kv_in.at[e - 1, rows],
            send_sem=ring_sem.at[e - 1, n, 0],
            recv_sem=ring_sem.at[e - 1, n, 1],
            device_id=along(e),
            device_id_type=MESH,
        )

    barrier = pltpu.get_barrier_semaphore()
    for peer in (along(1), along(2), along(3), over):
        pl.semaphore_signal(barrier, inc=1, device_id=peer, device_id_type=MESH)
    pl.semaphore_wait(barrier, 4)

    @pl.when(ring == 0)
    def _():
        for n in range(PIECES):
            copy_up(n).start()

    def copy_on(side, n):
        rows = pl.ds(n * piece, piece)
        return pltpu.make_async_remote_copy(
            src_ref=kv_in.at[2 * side, rows],
            dst_ref=kv_in.at[1, rows],
            send_sem=on_sem.at[side, n],
            recv_sem=ring_sem.at[1, n, 1],
            device_id=along(1 + 2 * side),
            device_id_type=MESH,
        )

    def passes_on(side, n):
        if side == 0:
            return (z <= 2) & (ctx >= 1) if n % 2 == 0 else (z == 2)
        return (ctx >= 3) & (z >= 1) if n % 2 == 1 else (ring == 1) & (z == 1)

    for e in (1, 3):

        @pl.when(z + e <= 3)
        def _():
            for n in range(PIECES):
                copy_along(e, n, kv_ref).start()

    q_scaled[...] = scaled_queries(q_ref[...])
    m_ref[...] = jnp.full_like(m_ref, NEG)
    acc_ref[...] = jnp.zeros_like(acc_ref)

    def all_queries(keys, edge):
        count = keys.shape[0]
        vt_ref[:, :count] = with_ones(keys[:, 256:])

        def some(i, carry):
            if edge == "far":
                rows = pl.ds(i * ROWS, ROWS)
                seen = (tokens - i * ROWS, ROWS)
                online_step(
                    q_scaled[rows, :],
                    lambda j: keys[i * ROWS : tokens, j * HDIM : (j + 1) * HDIM],
                    vt_ref[:, i * ROWS : tokens],
                    m_ref.at[i],
                    acc_ref.at[i],
                    lax.broadcasted_iota(jnp.int32, seen, 0) > lax.broadcasted_iota(jnp.int32, seen, 1),
                )
                return carry
            rows = pl.ds(pl.multiple_of(i * ROWS, ROWS), ROWS)
            mask = None
            if edge is not None:
                key_pos = lax.broadcasted_iota(jnp.int32, (tokens, ROWS), 0)
                row_pos = lax.broadcasted_iota(jnp.int32, (tokens, ROWS), 1) + i * ROWS
                mask = key_pos <= row_pos
            online_step(
                q_scaled[rows, :],
                lambda j: keys[:, j * HDIM : (j + 1) * HDIM],
                vt_ref[:, :count],
                m_ref.at[i],
                acc_ref.at[i],
                mask,
            )
            return carry

        if edge == "far":
            for i in range(tokens // ROWS):
                some(i, 0)
        else:
            lax.fori_loop(0, tokens // ROWS, some, 0)

    all_queries(kv_ref, "own")

    @pl.when(ring == 1)
    def _():
        for n in range(PIECES):
            copy_up(n).wait_recv()
            for e in (3, 1):

                @pl.when(z + e >= 4)
                def _():
                    copy_along(e, n, kv_in.at[3]).start()

    for side in (0, 1):

        @pl.when(ctx >= 1 + 2 * side)
        def _():
            for n in range(PIECES):
                copy_along(1 + 2 * side, n, kv_ref).wait_recv()

        for n in range(PIECES):

            @pl.when(passes_on(side, n))
            def _():
                copy_on(side, n).start()

    @pl.when(ring == 1)
    def _():
        all_queries(kv_in.at[3], "far")

    for e in (1, 3, 2):

        @pl.when(ctx >= e)
        def _():
            if e != 2:
                all_queries(kv_in.at[e - 1], None)
                return
            for half in range(2):
                for n in range(half * PIECES // 2, (half + 1) * PIECES // 2):
                    copy_along(2, n, kv_ref).wait_recv()
                all_queries(kv_in.at[1, pl.ds(half * tokens // 2, tokens // 2)], None)

    pairs = lam_ref[...]
    lam = (
        jnp.exp(jnp.sum(pairs[0:1] * pairs[1:2], axis=1, keepdims=True))
        - jnp.exp(jnp.sum(pairs[2:3] * pairs[3:4], axis=1, keepdims=True))
        + LAMBDA_INIT
    )

    def finish(i, carry):
        one = acc_ref[i, 0, :256] / acc_ref[i, 0, 256:257]
        two = acc_ref[i, 1, :256] / acc_ref[i, 1, 256:257]
        attended = one - lam * two
        factor = lax.rsqrt(jnp.mean(attended * attended, axis=0, keepdims=True) + EPSILON)
        normed = (attended * factor).T * (gain_ref[...] * (1.0 - LAMBDA_INIT))
        out_ref[pl.ds(pl.multiple_of(i * ROWS, ROWS), ROWS), :] = normed.astype(jnp.bfloat16)
        return carry

    lax.fori_loop(0, tokens // ROWS, finish, 0)

    @pl.when(ring == 0)
    def _():
        for n in range(PIECES):
            copy_up(n).wait_send()

    for e in (1, 3):

        @pl.when((ring == 1) | (z + e <= 3))
        def _():
            for n in range(PIECES):
                copy_along(e, n, kv_ref).wait_send()

    for side in (0, 1):
        for n in range(PIECES):

            @pl.when(passes_on(side, n))
            def _():
                copy_on(side, n).wait_send()


def window_attention(queries, keys_values, lam_win, gain):
    tokens = queries.shape[0]
    vmem = pl.BlockSpec(memory_space=pltpu.VMEM)
    return pl.pallas_call(
        window_kernel,
        name="window",
        out_shape=jax.ShapeDtypeStruct((tokens, 256), jnp.bfloat16),
        in_specs=[vmem] * 4,
        out_specs=vmem,
        scratch_shapes=[
            pltpu.VMEM((4, tokens, 512), jnp.bfloat16),
            pltpu.VMEM((tokens, 256), jnp.bfloat16),
            pltpu.VMEM((256 + ONES, tokens), jnp.bfloat16),
            pltpu.VMEM((tokens // ROWS, 2, 1, ROWS), jnp.float32),
            pltpu.VMEM((tokens // ROWS, 2, 256 + ONES, ROWS), jnp.float32),
            pltpu.SemaphoreType.DMA((PIECES, 2)),
            pltpu.SemaphoreType.DMA((3, PIECES, 2)),
            pltpu.SemaphoreType.DMA((2, PIECES)),
        ],
        compiler_params=pltpu.CompilerParams(
            collective_id=1, has_side_effects=True, vmem_limit_bytes=62 * 2**20
        ),
    )(lam_win, queries, gain.reshape(1, 256), keys_values)


CHUNKS = 4
SUB = 16


def place():
    head = lax.axis_index("head")
    return lax.axis_index("ctx"), head // 4, (head // 2) % 2, head % 2


KINDS = (
    "normed",
    "y1",
    "x1_far",
    "x1_near",
    "x1_sum",
    "x2",
    "y2_far",
    "y2_near",
    "y2_sum",
    "h1",
    "h1_on",
    "g1",
    "h2",
    "g2",
    "g2_on",
    "core",
    "next",
)


def mid_kernel(
    x_cols,
    g_cols,
    normed_ref,
    w_own_hbm,
    w_sib_hbm,
    residual_ref,
    gain_ref,
    w_qkv_hbm,
    hidden_ref,
    acc_ref,
    m_ref,
    qkv_ref,
    kv1_ref,
    kv2_ref,
    w_qkv,
    n_sib,
    part,
    x1_far,
    x1_in,
    y1_in,
    x2_out,
    x2_in,
    y2_far,
    y2_in,
    rows_all,
    load_sem,
    sems,
):
    ctx, x, y, core = place()
    width = w_own_hbm.shape[1]
    y_cols = width - x_cols
    low, high = pl.ds(0, x_cols), pl.ds(x_cols, y_cols)
    low_half = (pl.ds(0, x_cols // 2), pl.ds(x_cols // 2, x_cols // 2))
    high_half = (pl.ds(x_cols, y_cols // 2), pl.ds(x_cols + y_cols // 2, y_cols // 2))
    g_low, g_high = pl.ds(0, g_cols), pl.ds(g_cols, width - g_cols)
    g_low_half = (pl.ds(0, g_cols // 2), pl.ds(g_cols // 2, g_cols // 2))
    g_high_half = tuple(
        pl.ds(g_cols + s * ((width - g_cols) // 2), (width - g_cols) // 2) for s in (0, 1)
    )
    y_half = (pl.ds(0, y_cols // 2), pl.ds(y_cols // 2, y_cols // 2))
    head = lax.axis_index("head")
    beside = (lax.rem(x + 1, 4), lax.rem(x + 3, 4))
    opposite = lax.rem(x + 2, 4)
    along = [(ctx, place_x * 4 + y * 2 + core) for place_x in beside]
    over_y = (ctx, x * 4 + (1 - y) * 2 + core)
    sibling = (ctx, x * 4 + y * 2 + 1 - core)
    blocks = lax.axis_size("ctx")
    others = [(lax.rem(ctx + d, blocks), head) for d in range(1, 8)]

    late_load = pltpu.make_async_copy(w_qkv_hbm, w_qkv, load_sem.at[2])
    late_load.start()

    started = []
    pending = {}

    def describe(kind, r, side, source, target, device):
        kind = KINDS.index(kind)
        return pltpu.make_async_remote_copy(
            src_ref=source,
            dst_ref=target,
            send_sem=sems.at[kind, r, side, 0],
            recv_sem=sems.at[kind, r, side, 1],
            device_id=device,
            device_id_type=MESH,
        )

    def send(kind, r, side, ends):
        def copy():
            return describe(kind, r, side, *ends())

        copy().start()
        started.append(copy)
        pending[kind, r, side] = copy

    every = slice(None)

    def spread_rows(r, kind, side, index, device):
        send(kind, r, side, lambda: (rows_all.at[index()], rows_all.at[index()], device))

    def arrived(kind, r, sides=(0,)):
        for side in sides:
            pending[kind, r, side]().wait_recv()

    def wide(value):
        return value.astype(jnp.float32)

    both = (0, 1)
    tile = min(1024, width)

    def project(r, w_own, w_sib):
        own_rows = normed_ref[:, core, r].reshape(8 * SUB, 256)
        sib_rows = n_sib[:, r].reshape(8 * SUB, 256)

        def columns(j, carry):
            span = pl.ds(pl.multiple_of(j * tile, tile), tile)
            value = jnp.dot(own_rows, w_own[:, span], preferred_element_type=jnp.float32)
            value += jnp.dot(sib_rows, w_sib[:, span], preferred_element_type=jnp.float32)
            part[r, :, :, :, span] = value.astype(jnp.bfloat16).reshape(4, 2, SUB, tile)
            return carry

        lax.fori_loop(0, width // tile, columns, 0)
        for s in both:

            def far(s=s):
                return part.at[r, opposite, :, :, low_half[s]], x1_far.at[r, s], along[s]

            send("x1_far", r, s, far)
        send("y1", r, 0, lambda: (part.at[r, :, 1 - y, :, high], y1_in.at[r], over_y))
        for s in both:

            def near(s=s):
                half = low_half[1 - s]
                return part.at[r, beside[s], :, :, half], x1_in.at[r, s, :, :, half], along[s]

            send("x1_near", r, s, near)

    def relay_x1(r):
        arrived("x1_far", r, both)
        for s in both:
            ours = part.at[r, beside[s], :, :, low_half[s]]
            ours[...] = (wide(ours[...]) + wide(x1_far[r, s])).astype(jnp.bfloat16)

            def summed(s=s):
                half = low_half[s]
                return part.at[r, beside[s], :, :, half], x1_in.at[r, s, :, :, half], along[s]

            send("x1_sum", r, s, summed)

    def second(r):
        arrived("y1", r)
        for place_x in (opposite,) + beside:
            ours = part.at[r, place_x, y, :, high]
            ours[...] = (wide(ours[...]) + wide(y1_in[r, place_x])).astype(jnp.bfloat16)
        for s in both:

            def far(s=s):
                return part.at[r, opposite, y, :, high_half[s]], y2_far.at[r, s], along[s]

            send("y2_far", r, s, far)
        for s in both:

            def near(s=s):
                source = part.at[r, beside[s], y, :, high_half[1 - s]]
                return source, y2_in.at[r, s, :, y_half[1 - s]], along[s]

            send("y2_near", r, s, near)
        arrived("x1_near", r, both)
        arrived("x1_sum", r, both)
        total = wide(part[r, x, 1 - y, :, low])
        for s in both:
            total += wide(x1_in[r, s, 1 - y])
        x2_out[r] = total.astype(jnp.bfloat16)
        send("x2", r, 0, lambda: (x2_out.at[r], x2_in.at[r], over_y))

    def relay_y2(r):
        arrived("y2_far", r, both)
        for s in both:
            ours = part.at[r, beside[s], y, :, high_half[s]]
            ours[...] = (wide(ours[...]) + wide(y2_far[r, s])).astype(jnp.bfloat16)

            def summed(s=s):
                source = part.at[r, beside[s], y, :, high_half[s]]
                return source, y2_in.at[r, s, :, y_half[s]], along[s]

            send("y2_sum", r, s, summed)

    def finish(r):
        arrived("x2", r)
        arrived("y2_near", r, both)
        arrived("y2_sum", r, both)
        left = wide(part[r, x, y, :, low]) + wide(x2_in[r])
        right = wide(part[r, x, y, :, high]) + wide(y1_in[r, x])
        for s in both:
            left += wide(x1_in[r, s, y])
            right += wide(y2_in[r, s])
        left = (wide(residual_ref[r, :, low]) + left).astype(jnp.bfloat16)
        right = (wide(residual_ref[r, :, high]) + right).astype(jnp.bfloat16)
        hidden_ref[r, :, low] = left
        hidden_ref[r, :, high] = right
        left, right = wide(left), wide(right)
        squares = jnp.sum(left * left, axis=-1, keepdims=True)
        squares += jnp.sum(right * right, axis=-1, keepdims=True)
        factor = lax.rsqrt(squares / width + EPSILON)
        mine = rows_all.at[r, x, y, core]
        mine[:, low] = (left * factor * gain_ref[:, low]).astype(jnp.bfloat16)
        mine[:, high] = (right * factor * gain_ref[:, high]).astype(jnp.bfloat16)

        for s in both:
            spread_rows(r, "h1", s, lambda: (r, x, y, core, every, g_low), along[s])
        spread_rows(r, "g1", 0, lambda: (r, x, y, core, every, g_high), over_y)

    def pass_h1(r):
        arrived("h1", r, both)
        for s in both:
            spread_rows(
                r,
                "h1_on",
                s,
                lambda s=s: (r, beside[1 - s], y, core, every, g_low_half[s]),
                along[s],
            )

    def spread(r):
        arrived("g1", r)
        for s in both:
            spread_rows(r, "g2", s, lambda: (r, x, every, core, every, g_high), along[s])
        arrived("h1_on", r, both)
        spread_rows(r, "h2", 0, lambda: (r, every, y, core, every, g_low), over_y)

    def pass_g2(r):
        arrived("g2", r, both)
        for s in both:
            spread_rows(
                r,
                "g2_on",
                s,
                lambda s=s: (r, beside[1 - s], every, core, every, g_high_half[s]),
                along[s],
            )

    def share(r):
        arrived("h2", r)
        spread_rows(r, "core", 0, lambda: (r, every, every, core, every, g_low), sibling)
        arrived("g2_on", r, both)
        spread_rows(r, "core", 1, lambda: (r, every, every, core, every, g_high), sibling)

    def next_copy(d, r, target, forward=False):
        landing = (kv1_ref, kv2_ref)[d - 1].at[:, r]
        kind = KINDS.index("next")
        return pltpu.make_async_remote_copy(
            src_ref=landing if forward else qkv_ref.at[:, r, :, 256:],
            dst_ref=landing,
            send_sem=sems.at[kind, r, 2 if forward else d - 1, 0],
            recv_sem=sems.at[kind, r, d - 1, 1],
            device_id=(target, head),
            device_id_type=MESH,
        )

    def project_next(r, acc):
        arrived("core", r, both)
        if r == 0:
            late_load.wait()

        def depth(j, carry):
            span = pl.ds(pl.multiple_of(j * tile, tile), tile)
            rows = rows_all[r, :, :, :, :, span].reshape(16 * SUB, tile)
            for n in range(3):
                acc[n] += jnp.dot(rows, w_qkv[n, span], preferred_element_type=jnp.float32)
            return carry

        acc[...] = jnp.zeros_like(acc)
        lax.fori_loop(0, width // tile, depth, 0)
        for n in range(3):
            qkv_ref[:, r, :, n * 256 : n * 256 + 256] = (
                acc[n].astype(jnp.bfloat16).reshape(16, SUB, 256)
            )
        for d, target, sends in routes:

            @pl.when(sends)
            def _():
                next_copy(d, r, target).start()

    routes = [
        (1, lax.rem(ctx + 1, blocks), (ctx <= 6) & (ctx != 3)),
        (2, lax.rem(ctx + 2, blocks), (ctx <= 5) & (ctx != 3)),
        (1, lax.rem(ctx + 5, blocks), ctx == 3),
        (2, lax.rem(ctx + 6, blocks), ctx == 3),
    ]
    stages = [
        project,
        relay_x1,
        second,
        relay_y2,
        finish,
        pass_h1,
        spread,
        pass_g2,
        share,
        project_next,
    ]

    def steps(first, last, *weights):
        for step in range(first, last):
            for r in range(CHUNKS):
                if 0 <= step - r < len(stages):
                    stages[step - r](r, *(weights if step - r in (0, len(stages) - 1) else ()))

    def first_steps(w_own, w_sib):
        loads = [
            pltpu.make_async_copy(source, target, load_sem.at[n])
            for n, (source, target) in enumerate([(w_own_hbm, w_own), (w_sib_hbm, w_sib)])
        ]
        for load in loads:
            load.start()
        barrier = pltpu.get_barrier_semaphore()
        for peer in along + [over_y, sibling] + others:
            pl.semaphore_signal(barrier, inc=1, device_id=peer, device_id_type=MESH)
        pl.semaphore_wait(barrier, 11)
        send("normed", 0, 0, lambda: (normed_ref.at[:, 1 - core], n_sib, sibling))
        arrived("normed", 0)
        for load in loads:
            load.wait()
        steps(0, CHUNKS, w_own, w_sib)

    def last_steps(acc):
        steps(CHUNKS, CHUNKS - 1 + len(stages), acc)

    pl.run_scoped(
        first_steps, pltpu.VMEM((256, width), jnp.bfloat16), pltpu.VMEM((256, width), jnp.bfloat16)
    )
    pl.run_scoped(last_steps, pltpu.VMEM((3, 16 * SUB, 256), jnp.float32))

    for d in (1, 2):

        @pl.when(ctx == d - 1)
        def _():
            for r in range(CHUNKS):
                next_copy(d, r, 0).wait_recv()
                next_copy(d, r, lax.rem(ctx + 4, blocks), True).start()

    tokens = 16 * CHUNKS * SUB
    groups = tokens // ROWS
    heads = 16 // groups

    def attend(vt_ref):
        m_ref[...] = jnp.full_like(m_ref, NEG)
        acc_ref[...] = jnp.zeros_like(acc_ref)

        def block(kv, own, first=0, last=CHUNKS):
            count = 16 * (last - first) * SUB

            def columns(start, size):
                return kv[:, first:last, :, start : start + size].reshape(count, size)

            vt_ref[:, :count] = with_ones(columns(256, 256))

            def some(i, carry):
                queries = qkv_ref[pl.ds(i * heads, heads), :, :, :256].reshape(ROWS, 256)
                mask = None
                seen = count
                if own:
                    seen = (i + 1) * ROWS
                    key_pos = lax.broadcasted_iota(jnp.int32, (seen, ROWS), 0)
                    row_pos = lax.broadcasted_iota(jnp.int32, (seen, ROWS), 1) + i * ROWS
                    mask = key_pos <= row_pos

                def keys_of(j):
                    if own:
                        part_of = kv[: (i + 1) * heads, :, :, j * HDIM : (j + 1) * HDIM]
                        return part_of.reshape(seen, HDIM)
                    return columns(j * HDIM, HDIM)

                online_step(
                    scaled_queries(queries),
                    keys_of,
                    vt_ref[:, :seen],
                    m_ref.at[i],
                    acc_ref.at[i],
                    mask,
                )
                return carry

            if own:
                for i in range(groups):
                    some(i, 0)
            else:
                lax.fori_loop(0, groups, some, 0)

        block(qkv_ref.at[:, :, :, 256:], True)
        for first, last in ((0, CHUNKS - 1), (CHUNKS - 1, CHUNKS)):
            for d, landing in ((1, kv1_ref), (2, kv2_ref)):

                @pl.when(ctx >= d)
                def _():
                    for r in range(first, last):
                        next_copy(d, r, 0).wait_recv()
                    block(landing, False, first, last)

    pl.run_scoped(attend, pltpu.VMEM((256 + ONES, tokens), jnp.bfloat16))
    for copy in started:
        copy().wait_send()
    for r in range(CHUNKS):
        for d, target, sends in routes:

            @pl.when(sends)
            def _():
                next_copy(d, r, target).wait_send()

        for d in (1, 2):

            @pl.when(ctx == d - 1)
            def _():
                next_copy(d, r, 0, True).wait_send()


def project_and_spread(normed, w_own, w_sib, residual, gain, w_qkv):
    width = w_own.shape[1]
    x_cols = width * 9 // 16
    g_cols = width * 7 // 16
    tokens = 16 * CHUNKS * SUB
    bf16 = jnp.bfloat16
    any_space = pl.BlockSpec(memory_space=pl.ANY)
    vmem = pl.BlockSpec(memory_space=pltpu.VMEM)
    sem = pltpu.SemaphoreType.DMA
    hidden, sums, highest = pl.pallas_call(
        functools.partial(mid_kernel, x_cols, g_cols),
        name="project_and_spread",
        out_shape=(
            jax.ShapeDtypeStruct((CHUNKS, SUB, width), bf16),
            jax.ShapeDtypeStruct((tokens // ROWS, 2, 256 + ONES, ROWS), jnp.float32),
            jax.ShapeDtypeStruct((tokens // ROWS, 2, 1, ROWS), jnp.float32),
        ),
        in_specs=[vmem, any_space, any_space, vmem, vmem, any_space],
        out_specs=(vmem, vmem, vmem),
        scratch_shapes=[
            pltpu.VMEM((16, CHUNKS, SUB, 768), bf16),
            pltpu.VMEM((16, CHUNKS, SUB, 512), bf16),
            pltpu.VMEM((16, CHUNKS, SUB, 512), bf16),
            pltpu.VMEM((3, width, 256), bf16),
            pltpu.VMEM((8, CHUNKS, SUB, 256), bf16),
            pltpu.VMEM((CHUNKS, 4, 2, SUB, width), bf16),
            pltpu.VMEM((CHUNKS, 2, 2, SUB, x_cols // 2), bf16),
            pltpu.VMEM((CHUNKS, 2, 2, SUB, x_cols), bf16),
            pltpu.VMEM((CHUNKS, 4, SUB, width - x_cols), bf16),
            pltpu.VMEM((CHUNKS, SUB, x_cols), bf16),
            pltpu.VMEM((CHUNKS, SUB, x_cols), bf16),
            pltpu.VMEM((CHUNKS, 2, SUB, (width - x_cols) // 2), bf16),
            pltpu.VMEM((CHUNKS, 2, SUB, width - x_cols), bf16),
            pltpu.VMEM((CHUNKS, 4, 2, 2, SUB, width), bf16),
            sem((3,)),
            sem((len(KINDS), CHUNKS, 3, 2)),
        ],
        compiler_params=pltpu.CompilerParams(
            collective_id=0, has_side_effects=True, vmem_limit_bytes=63 * 2**20
        ),
    )(
        normed.reshape(8, 2, CHUNKS, SUB, 256),
        w_own,
        w_sib,
        residual.reshape(CHUNKS, SUB, width),
        gain.reshape(1, width),
        w_qkv,
    )
    return hidden.reshape(CHUNKS * SUB, width), sums, highest


def settle_kernel(hidden_in, acc_ref, m_ref, hidden_ref, out_ref, log_ref):
    hidden_ref[...] = hidden_in[...]
    for j in range(2):
        total = acc_ref[0, j, 256:257]
        value = (acc_ref[0, j, :256] / total).T
        for half in range(2):
            out_ref[j, pl.ds(half, ROWS, stride=2), :] = value[:, half * 128 : half * 128 + 128]
        log_ref[j] = (m_ref[0, j] + jnp.log2(total)) * LN2


def settle(hidden, sums, highest):
    groups = sums.shape[0]
    rows, width = hidden.shape
    return pl.pallas_call(
        settle_kernel,
        name="settle",
        grid=(groups,),
        out_shape=(
            jax.ShapeDtypeStruct((rows, width), jnp.bfloat16),
            jax.ShapeDtypeStruct((2, 2 * groups * ROWS, 128), jnp.float32),
            jax.ShapeDtypeStruct((2, 1, groups * ROWS), jnp.float32),
        ),
        in_specs=[
            pl.BlockSpec((rows // groups, width), lambda i: (i, 0)),
            pl.BlockSpec((1, 2, 256 + ONES, ROWS), lambda i: (i, 0, 0, 0)),
            pl.BlockSpec((1, 2, 1, ROWS), lambda i: (i, 0, 0, 0)),
        ],
        out_specs=(
            pl.BlockSpec((rows // groups, width), lambda i: (i, 0)),
            pl.BlockSpec((2, 2 * ROWS, 128), lambda i: (0, i, 0)),
            pl.BlockSpec((2, 1, ROWS), lambda i: (0, 0, i)),
        ),
        compiler_params=pltpu.CompilerParams(vmem_limit_bytes=62 * 2**20),
    )(hidden, sums, highest)


def on_device(residual, q_win, kv_win, lam_win, gn_gain, w_out_a, norm_gain, w_qkv):
    tokens_here = q_win.shape[0]
    w_sib = lax.ppermute(w_out_a, "head", [(i, i ^ 1) for i in range(lax.axis_size("head"))])
    normed = window_attention(
        q_win.reshape(tokens_here, 256), kv_win.reshape(tokens_here, 512), lam_win, gn_gain
    )
    h_rows, part_out, log_out = settle(
        *project_and_spread(
            normed, w_out_a, w_sib, residual, norm_gain, w_qkv[:, 0].transpose(1, 0, 2)
        )
    )
    return (
        h_rows,
        part_out.reshape(2, tokens_here, 1, 256),
        log_out,
    )


def solution(mesh):
    in_specs = (
        P(("ctx", "head"), None),
        P("ctx", "head", None),
        P("ctx", "head", None, None),
        P(),
        P(),
        P("head", None),
        P(),
        P(None, "head", None, None),
    )
    out_specs = (P(("ctx", "head"), None), P(None, "ctx", "head", None), P(None, "head", "ctx"))
    return jax.shard_map(
        on_device, mesh=mesh, in_specs=in_specs, out_specs=out_specs, check_vma=False
    )
```
